32 devices in a mesh: ctx: 4 (over y, x), head: 8 (over z, core).
Axes of the slice: x: 2, y: 2, z: 4, core: 2. Of those that a mesh axis runs over, the one named last changes fastest.
Arguments:
- tokens: bfloat16 [4096, 4096], P('ctx', 'head'), may hold values from -6 to 6
- doc_ids: int32 [4096], P('ctx'), may hold values from 0 to 7, never falling along the last dimension, each value on 1 to 2048 neighbouring positions
- w_feat: bfloat16 [4096, 1024], P(None, 'head'), may hold values from -0.09375 to 0.09375
- w_value: bfloat16 [4096, 4096], P(None, 'head'), may hold values from -0.09375 to 0.09375
- w_window: bfloat16 [4096, 8192], P(None, 'head'), may hold values from -4 to 4
- w_out: bfloat16 [4096, 4096], P('head'), may hold values from -0.09375 to 0.09375
Outputs:
- layer_out: bfloat16 [4096, 4096], P('ctx', 'head')
The draws below stay inside these ranges and needn't reach their ends.
Inputs may be any that keep to these rules, and one draw needn't show every extreme that they name: `doc_ids`: document ids never fall along the sequence; each of the 8 documents has 1 to 2048 tokens, and one has exactly 2048.
All inputs are finite; a program needn't handle non-finite values.
Results may differ from the reference program's by a relative error of at most 0.019.
Values may be sent and summed in bfloat16 or wider, within the bound.
No kernel may reach another device: no remote copies, remote signals or barrier semaphores. Data moves between devices by JAX's collectives and lax.ppermute only.
A program may use at most 128 MiB of HBM per device.

```python
import math
import jax
import jax.numpy as jnp
import numpy as np
from jax import lax

D = 4096
HEADS = 32
HEAD_DIM = 128
FEAT = 16
PHI = 273
WIN = 64
DOCS = 8
TOK_DEV = 1024
TOKENS = 4096
N_CTX = 4


def draw_w_window(key, part):
    first_key = jax.random.fold_in(jax.random.fold_in(key, 17), 0)
    base = jax.random.normal(first_key, (D, HEADS, 2, HEAD_DIM), jnp.float32)
    scaled = (base * D ** (-0.5)).reshape(D, HEADS * 2 * HEAD_DIM)
    return jnp.clip(scaled, -4.0, 4.0).astype(jnp.bfloat16)


def block_levels(key, dims, cuts, smallest, largest):
    loudness = 1.0
    for position, shards_of in cuts:
        steps = jax.random.uniform(jax.random.fold_in(jax.random.fold_in(key, 6), position), (shards_of,), jnp.float32, smallest / len(cuts), largest / len(cuts))
        loudness = loudness * jnp.repeat(jnp.exp(steps), dims[position] // shards_of).reshape((-1,) + (1,) * (len(dims) - 1 - position))
    return loudness


def length_profile(amount, total, most, skew):
    weights = [(1 << 20) // math.isqrt(standing ** skew) + 1 for standing in range(2, amount + 1)]
    surplus, counts = total - most - (amount - 1), [1] * (amount - 1)
    while surplus > 0:
        movable = [i for i in range(amount - 1) if counts[i] < most]
        pool, left = sum([weights[i] for i in movable]), surplus
        for i in movable:
            addition = min(most - counts[i], max(1, left * weights[i] // pool), surplus)
            counts[i] = counts[i] + addition
            surplus = surplus - addition
    return np.array([most] + counts)


def ragged_sizes(stream_key, count, total, reach, lean):
    if count == 2:
        one = jax.random.randint(stream_key, (), max(1, total - reach), min(reach, total - 1) + 1)
        return jnp.stack([one, total - one])
    sizes = jnp.asarray(length_profile(count, total, reach, lean), jnp.int32)
    couples = (count - 1) // 2
    source_of, receiver = sizes[1:1 + 2 * couples:2], sizes[2:2 + 2 * couples:2]
    slack = jnp.minimum(source_of - 1, reach - receiver)
    passed = jax.random.randint(jax.random.fold_in(stream_key, 1), (couples,), 0, 1 << 20) % (slack + 1)
    sizes = sizes.at[1:1 + 2 * couples:2].set(source_of - passed).at[2:2 + 2 * couples:2].set(receiver + passed)
    return sizes[jax.random.permutation(jax.random.fold_in(stream_key, 2), count)]


def noise(key, dims, width, bound, cuts=(), held_as=jnp.bfloat16):
    values = width * jax.random.normal(key, dims, jnp.float32)
    if cuts:
        values = values * block_levels(key, dims, cuts, -0.22, 0.18)
    return jnp.clip(values, -bound, bound).astype(held_as)


def setup_inputs(seed: int = 0) -> dict:
    key_of = jax.random.split(jax.random.key(seed), 7)
    tokens = noise(key_of[0], (TOKENS, D), 1.0, 6.0, ((0, 4), (1, 8)))
    doc_ids = jnp.searchsorted(jnp.cumsum(ragged_sizes(key_of[1], DOCS, TOKENS, TOKENS // 2, 0)), jnp.arange(TOKENS), side="right").astype(jnp.int32)
    w_feat = noise(key_of[2], (D, HEADS * 2 * FEAT), D ** -0.5, 0.09375, ((1, 8),))
    w_value = noise(key_of[3], (D, HEADS * HEAD_DIM), D ** -0.5, 0.09375, ((1, 8),))
    w_window = draw_w_window(jax.random.fold_in(key_of[6], 71), 0)
    w_out = noise(key_of[5], (HEADS * HEAD_DIM, D), (HEADS * HEAD_DIM) ** -0.5, 0.09375, ((0, 8),))
    return {"tokens": tokens, "doc_ids": doc_ids, "w_feat": w_feat, "w_value": w_value, "w_window": w_window, "w_out": w_out}


def feature_map(projected):
    widened = projected.astype(jnp.float32)
    products = widened[..., :, None] * widened[..., None, :]
    products = products.reshape(widened.shape[:-1] + (FEAT * FEAT,))
    constant_term = jnp.ones(widened.shape[:-1] + (1,), jnp.float32)
    return jnp.concatenate([constant_term, widened * FEAT ** (-0.25), products * (2.0 * FEAT) ** (-0.5)], -1).astype(jnp.bfloat16)

def reference(tokens, doc_ids, w_feat, w_value, w_window, w_out):
    total_rows = tokens.shape[0]
    features = jnp.dot(tokens, w_feat, preferred_element_type=jnp.float32).astype(jnp.bfloat16)
    features = features.reshape(total_rows, HEADS, 2 * FEAT)
    phi_query = feature_map(features[..., :FEAT])
    phi_key = feature_map(features[..., FEAT:])
    values_all = jnp.dot(tokens, w_value, preferred_element_type=jnp.float32).astype(jnp.bfloat16)
    values_all = values_all.reshape(total_rows, HEADS, HEAD_DIM)
    window_proj = jnp.dot(tokens, w_window, preferred_element_type=jnp.float32).astype(jnp.bfloat16)
    window_proj = window_proj.reshape(total_rows, HEADS, 2, HEAD_DIM)
    win_query = window_proj[:, :, 0]
    win_key = window_proj[:, :, 1]

    def blocked(array):
        return array.reshape((N_CTX, TOK_DEV) + array.shape[1:])
    inputs = (blocked(phi_query), blocked(phi_key), blocked(values_all), blocked(win_query), blocked(win_key), blocked(doc_ids))
    positions = jnp.arange(TOK_DEV)
    key_pos = jnp.arange(WIN + TOK_DEV)
    highest = lax.Precision.HIGHEST

    def step_block(carry, block_inputs):
        state, last_doc, tail_key, tail_value, tail_doc = carry
        block_q, block_k, block_v, query_block, key_block, doc_block = block_inputs
        allowed = ((doc_block[:, None] == doc_block[None, :]) & (positions[:, None] >= positions[None, :])).astype(jnp.float32)
        wide_q = block_q.astype(jnp.float32)
        wide_k = block_k.astype(jnp.float32)
        wide_v = block_v.astype(jnp.float32)
        scores = (jnp.einsum('thp,shp->hts', wide_q, wide_k, precision=highest) * allowed[None]).astype(jnp.bfloat16)
        inner = jnp.einsum('hts,shd->thd', scores.astype(jnp.float32), wide_v, precision=highest)
        carried = jnp.einsum('thp,hpd->thd', wide_q, state, precision=highest)
        uses = doc_block == last_doc
        linear_out = inner + jnp.where(uses[:, None, None], carried, jnp.zeros_like(carried))
        keeps = (doc_block == doc_block[-1])[:, None, None]
        kept_keys = jnp.where(keeps, wide_k, jnp.zeros_like(wide_k))
        local_state = jnp.einsum('shp,shd->hpd', kept_keys, wide_v, precision=highest)
        new_state = local_state + jnp.where(last_doc == doc_block[-1], state, jnp.zeros_like(state))
        mean_square = lax.optimization_barrier(jnp.mean(linear_out * linear_out, -1, keepdims=True))
        normed = linear_out * lax.rsqrt(mean_square + 1e-05)
        keys_all = jnp.concatenate([tail_key, key_block], 0).astype(jnp.float32)
        values_cat = jnp.concatenate([tail_value, block_v], 0).astype(jnp.float32)
        docs_cat = jnp.concatenate([tail_doc, doc_block], 0)
        within = (key_pos[None, :] > positions[:, None]) & (key_pos[None, :] <= positions[:, None] + WIN) & (docs_cat[None, :] == doc_block[:, None])
        logits = jnp.einsum('thd,shd->hts', query_block.astype(jnp.float32), keys_all, precision=highest) * HEAD_DIM ** (-0.5)
        logits = jnp.where(within[None], logits, -1e+30)
        top_logit = lax.optimization_barrier(jnp.max(logits, -1, keepdims=True))
        weights = jnp.exp(logits - top_logit) * within[None].astype(jnp.float32)
        probs = (weights / lax.optimization_barrier(jnp.sum(weights, -1, keepdims=True))).astype(jnp.bfloat16)
        window_out = jnp.einsum('hts,shd->thd', probs.astype(jnp.float32), values_cat, precision=highest)
        mixed = (normed + window_out).astype(jnp.bfloat16).reshape(TOK_DEV, HEADS * HEAD_DIM)
        new_carry = (new_state, doc_block[-1], key_block[TOK_DEV - WIN:], block_v[TOK_DEV - WIN:], doc_block[TOK_DEV - WIN:])
        return (new_carry, mixed)
    start_carry = (jnp.zeros((HEADS, PHI, HEAD_DIM), jnp.float32), jnp.array(-1, jnp.int32), jnp.zeros((WIN, HEADS, HEAD_DIM), jnp.bfloat16), jnp.zeros((WIN, HEADS, HEAD_DIM), jnp.bfloat16), jnp.full((WIN,), -1, jnp.int32))
    final_carry, mixed_blocks = lax.scan(step_block, start_carry, inputs)
    mixed_all = mixed_blocks.reshape(total_rows, HEADS * HEAD_DIM)
    return jnp.dot(mixed_all, w_out, preferred_element_type=jnp.float32).astype(jnp.bfloat16)
```

```python
import functools

import jax
import jax.numpy as jnp
import numpy as np
from jax import lax
from jax.experimental import pallas as pl
from jax.experimental.pallas import tpu as pltpu
from jax.sharding import PartitionSpec as P

HEAD_DIM = 128
FEAT = 16
WIN = 64
PAIRS = [(i, j) for i in range(FEAT) for j in range(i, FEAT)]
WIDE = 256
STATE = -(-(len(PAIRS) + FEAT + 1) // 16) * 16
VMEM = 60 * 1024 * 1024
F32 = jnp.float32
BF16 = jnp.bfloat16


def params():
    return pltpu.CompilerParams(vmem_limit_bytes=VMEM, dimension_semantics=("arbitrary",))


def line(count, step, sources):
    return [(2 * z + c, 2 * (z + step) + c) for z in sources for c in (0, 1) if 0 <= z + step < count]


def swap(x, count):
    return lax.ppermute(x, "head", [(h, h ^ 1) for h in range(2 * count)])


def gather_pieces(x, count):
    mine = [x]
    up = down = x
    for s in range(1, count):
        up = lax.ppermute(up, "head", line(count, 1, range(s - 1, count)))
        down = lax.ppermute(down, "head", line(count, -1, range(0, count - s + 1)))
        mine += [up, down]
    return mine, [swap(p, count) for p in mine]


def project_kernel(count, extra, place, *refs):
    slots = 2 * count - 1
    pieces = refs[: 2 * slots]
    weights = refs[2 * slots : 2 * slots + 1 + extra]
    outs = refs[2 * slots + 1 + extra : 2 * slots + 2 * (1 + extra)]
    x, sems = refs[-2:]
    width = pieces[0].shape[1]

    @pl.when(pl.program_id(0) == 0)
    def _():
        z, c = place[0], place[1]

        def copy(slot, other, source):
            column = pl.multiple_of((2 * source + lax.rem(c + other, 2)) * width, width)
            return pltpu.make_async_copy(
                pieces[other * slots + slot], x.at[:, pl.ds(column, width)], sems.at[other, slot]
            )

        def visit(do):
            for other in (0, 1):
                do(copy(0, other, z))
            for s in range(1, count):

                @pl.when(z >= s)
                def _():
                    for other in (0, 1):
                        do(copy(2 * s - 1, other, z - s))

                @pl.when(z + s < count)
                def _():
                    for other in (0, 1):
                        do(copy(2 * s, other, z + s))

        visit(lambda one: one.start())
        visit(lambda one: one.wait())
        if extra:
            outs[1][...] = jnp.dot(x[...], weights[1][...], preferred_element_type=F32).astype(BF16)

    outs[0][...] = jnp.dot(x[...], weights[0][...], preferred_element_type=F32).astype(BF16)


def project(place, mine, theirs, weight, extra=None):
    count = (len(mine) + 1) // 2
    rows = mine[0].shape[0]
    depth, columns = weight.shape
    tile = min(256, columns)
    specs = [pl.BlockSpec(memory_space=pl.ANY)] * (2 * len(mine))
    specs += [pl.BlockSpec((depth, tile), lambda j, _: (0, j))]
    out_specs = [pl.BlockSpec((rows, tile), lambda j, _: (0, j))]
    shapes = [jax.ShapeDtypeStruct((rows, columns), BF16)]
    args = [weight]
    if extra is not None:
        args.append(extra)
        specs.append(pl.BlockSpec(extra.shape, lambda j, _: (0, 0)))
        out_specs.append(pl.BlockSpec((rows, extra.shape[1]), lambda j, _: (0, 0)))
        shapes.append(jax.ShapeDtypeStruct((rows, extra.shape[1]), BF16))
    return pl.pallas_call(
        functools.partial(project_kernel, count, len(args) - 1),
        grid_spec=pltpu.PrefetchScalarGridSpec(
            num_scalar_prefetch=1,
            grid=(columns // tile,),
            in_specs=specs,
            out_specs=out_specs,
            scratch_shapes=[
                pltpu.VMEM((rows, depth), BF16),
                pltpu.SemaphoreType.DMA((2, len(mine))),
            ],
        ),
        out_shape=shapes,
        compiler_params=params(),
    )(place, *mine, *theirs, *args)


def expansions(heads):
    lanes = heads * 2 * FEAT
    maps = np.zeros((2, heads, lanes, 2 * WIDE), np.float32)
    rows = np.zeros((3, WIDE), np.float32)
    for h in range(heads):
        for side in (0, 1):
            base = h * 2 * FEAT + side * FEAT
            for n, (i, j) in enumerate(PAIRS):
                maps[side, h, base + i, n] = 1.0
                maps[side, h, base + j, WIDE + n] = 1.0
            for i in range(FEAT):
                maps[side, h, base + i, len(PAIRS) + i] = 1.0
    for n, (i, j) in enumerate(PAIRS):
        rows[2, n] = (2.0 * FEAT) ** -0.5 * (1.0 if i == j else 2.0**0.5)
    rows[1, len(PAIRS) : len(PAIRS) + FEAT + 1] = 1.0
    rows[0, len(PAIRS) + FEAT] = 1.0
    rows[2, len(PAIRS) : len(PAIRS) + FEAT] = FEAT**-0.25
    rows[2, len(PAIRS) + FEAT] = 1.0
    return maps.astype(jnp.bfloat16), rows


def picks(heads):
    lanes = heads * 2 * FEAT
    maps = np.zeros((heads, lanes, 256), np.float32)
    for h in range(heads):
        for i in range(FEAT):
            maps[h, h * 2 * FEAT + i, i] = 1.0
            maps[h, h * 2 * FEAT + FEAT + i, 128 + i] = 1.0
    return maps.astype(jnp.bfloat16)


def phi(features, expand, rows):
    factors = jnp.dot(features, expand, preferred_element_type=F32)
    left = factors[:, :WIDE] + rows[0:1]
    right = factors[:, WIDE:] + rows[1:2]
    return (left * right * rows[2:3]).astype(BF16)


def state_kernel(final, features, values, keep, expand, rows, *refs):
    phi_key = phi(features[...], expand[0], rows[...])
    kept = jnp.where(keep[...] > 0, values[...].astype(F32), 0.0).astype(BF16)
    state = lax.dot_general(phi_key, kept, (((0,), (0,)), ((), ())), preferred_element_type=F32)
    state = state[:STATE]
    if final:
        state = state + refs[0][0]
    refs[-1][0] = state.astype(refs[-1].dtype)


def local_state(features, values, keep, expand, rows, before=None):
    heads = values.shape[1] // HEAD_DIM
    count = features.shape[0]
    specs = [
        pl.BlockSpec(features.shape, lambda h: (0, 0)),
        pl.BlockSpec((count, HEAD_DIM), lambda h: (0, h)),
        pl.BlockSpec((count, 1), lambda h: (0, 0)),
        pl.BlockSpec((1,) + expand.shape[1:], lambda h: (h, 0, 0)),
        pl.BlockSpec(rows.shape, lambda h: (0, 0)),
    ]
    block = pl.BlockSpec((1, STATE, HEAD_DIM), lambda h: (h, 0, 0))
    args = [features, values, keep, expand, rows]
    if before is not None:
        specs.append(block)
        args.append(before)
    return pl.pallas_call(
        functools.partial(state_kernel, before is not None),
        grid=(heads,),
        in_specs=specs,
        out_specs=block,
        out_shape=jax.ShapeDtypeStruct((heads, STATE, HEAD_DIM), F32 if before is None else BF16),
        compiler_params=params(),
    )(*args)


def attention_kernel(
    feat_low, feat_high, val_low, val_high, win_low, win_high, tail_win, tail_val, bounds, pick,
    inner, windowed, query, key
):
    half = feat_low.shape[0]
    rows = 2 * half
    for part, ref in enumerate((feat_low, feat_high)):
        both = jnp.dot(ref[...], pick[0], preferred_element_type=F32).astype(BF16)
        query[part * half : (part + 1) * half] = both[:, :128]
        key[part * half : (part + 1) * half] = both[:, 128:]

    def rows_of(low, high, start, size):
        if start >= half:
            return high[start - half : start - half + size]
        if start + size <= half:
            return low[start : start + size]
        return jnp.concatenate([low[start:half], high[0 : start + size - half]], 0)

    tile = min(256, half)
    for q in range(rows // tile):
        here = slice(q * tile, (q + 1) * tile)
        first = bounds[here, 0:1]
        total = jnp.zeros((tile, HEAD_DIM), F32)
        for k in range(q + 1):
            dots = lax.dot_general(
                query[here], key[k * tile : (k + 1) * tile], (((1,), (1,)), ((), ())),
                preferred_element_type=F32,
            )
            score = dots * (dots * (0.5 / FEAT) + FEAT**-0.5) + 1.0
            at = lax.broadcasted_iota(jnp.int32, (tile, tile), 1) + k * tile
            good = at >= first
            if k == q:
                good &= at <= lax.broadcasted_iota(jnp.int32, (tile, tile), 0) + q * tile
            score = jnp.where(good, score, 0.0).astype(BF16)
            total += jnp.dot(
                score, rows_of(val_low, val_high, k * tile, tile), preferred_element_type=F32
            )
        inner[here] = total

    tile = min(128, half)
    for q in range(rows // tile):
        here = slice(q * tile, (q + 1) * tile)
        start = q * tile - WIN
        wide = tile + WIN
        queries = rows_of(win_low, win_high, q * tile, tile)[:, :HEAD_DIM]
        if q:
            keys = rows_of(win_low, win_high, start, wide)[:, HEAD_DIM:]
            values = rows_of(val_low, val_high, start, wide)
        else:
            keys = jnp.concatenate([tail_win[...], win_low[0:tile]], 0)[:, HEAD_DIM:]
            values = jnp.concatenate([tail_val[...], val_low[0:tile]], 0)
        logits = lax.dot_general(
            queries, keys, (((1,), (1,)), ((), ())), preferred_element_type=F32
        ) * HEAD_DIM**-0.5
        at = lax.broadcasted_iota(jnp.int32, (tile, wide), 1)
        row = lax.broadcasted_iota(jnp.int32, (tile, wide), 0)
        good = (at >= bounds[here, 1:2] - start) & (at <= row + WIN)
        logits = jnp.where(good, logits, -1e30)
        top = jnp.max(logits, 1, keepdims=True)
        weight = jnp.where(good, jnp.exp(logits - top), 0.0)
        probs = (weight / jnp.sum(weight, 1, keepdims=True)).astype(BF16)
        windowed[here] = jnp.dot(probs, values, preferred_element_type=F32)


def attention(feats, vals, wins, tail_win, tail_val, bounds, pick):
    half, columns = vals[0].shape
    heads = columns // HEAD_DIM
    rows = 2 * half

    def full(a):
        return pl.BlockSpec(a.shape, lambda h: (0,) * a.ndim)

    value = pl.BlockSpec((half, HEAD_DIM), lambda h: (0, h))
    window = pl.BlockSpec((half, 2 * HEAD_DIM), lambda h: (0, h))
    out = pl.BlockSpec((rows, HEAD_DIM), lambda h: (0, h))
    return pl.pallas_call(
        attention_kernel,
        grid=(heads,),
        in_specs=[
            full(feats[0]), full(feats[1]), value, value, window, window,
            pl.BlockSpec((WIN, 2 * HEAD_DIM), lambda h: (0, h)),
            pl.BlockSpec((WIN, HEAD_DIM), lambda h: (0, h)),
            full(bounds),
            pl.BlockSpec((1,) + pick.shape[1:], lambda h: (h, 0, 0)),
        ],
        out_specs=[out, out],
        out_shape=[jax.ShapeDtypeStruct((rows, columns), F32)] * 2,
        scratch_shapes=[pltpu.VMEM((rows, 128), BF16)] * 2,
        compiler_params=params(),
    )(*feats, *vals, *wins, tail_win, tail_val, bounds, pick)


def finish_kernel(shifts, chosen, feat_low, feat_high, uses, expand, rows, inner, windowed, *refs):
    half = feat_low.shape[0]
    states, outs = refs[:shifts], refs[shifts:]
    incoming = jnp.zeros((STATE, HEAD_DIM), F32)
    for k in range(shifts):
        incoming += jnp.where(chosen[k] > 0, states[k][0].astype(F32), 0.0)
    incoming = jnp.concatenate([incoming, jnp.zeros((WIDE - STATE, HEAD_DIM), F32)], 0).astype(BF16)
    for part, ref in enumerate((feat_low, feat_high)):
        here = slice(part * half, (part + 1) * half)
        phi_query = phi(ref[...], expand[0], rows[...])
        carried = jnp.dot(phi_query, incoming, preferred_element_type=F32)
        linear = inner[here] + jnp.where(uses[here] == 0, carried, 0.0)
        mean = jnp.mean(linear * linear, 1, keepdims=True)
        outs[part][...] = (linear * lax.rsqrt(mean + 1e-5) + windowed[here]).astype(BF16)


def finish(chosen, feats, uses, expand, rows, inner, windowed, states):
    count, columns = inner.shape
    half = count // 2
    heads = columns // HEAD_DIM

    def full(a):
        return pl.BlockSpec(a.shape, lambda h, _: (0,) * a.ndim)

    block = pl.BlockSpec((count, HEAD_DIM), lambda h, _: (0, h))
    out = pl.BlockSpec((half, HEAD_DIM), lambda h, _: (0, h))
    state = pl.BlockSpec((1, STATE, HEAD_DIM), lambda h, _: (h, 0, 0))
    return pl.pallas_call(
        functools.partial(finish_kernel, len(states)),
        grid_spec=pltpu.PrefetchScalarGridSpec(
            num_scalar_prefetch=1,
            grid=(heads,),
            in_specs=[
                full(feats[0]), full(feats[1]), full(uses),
                pl.BlockSpec((1,) + expand.shape[1:], lambda h, _: (h, 0, 0)),
                full(rows), block, block,
            ] + [state] * len(states),
            out_specs=[out, out],
        ),
        out_shape=[jax.ShapeDtypeStruct((half, columns), BF16)] * 2,
        compiler_params=params(),
    )(chosen, *feats, uses, expand, rows, inner, windowed, *states)


def shards(tokens, doc_ids, w_feat, w_value, w_window, w_out):
    rows = tokens.shape[0]
    half = rows // 2
    heads = w_value.shape[1] // HEAD_DIM
    count = lax.axis_size("head") // 2
    blocks = lax.axis_size("ctx")
    me = lax.axis_index("head")
    z, c = me // 2, me % 2
    place = jnp.stack([z, c]).astype(jnp.int32)

    high_mine, high_theirs = gather_pieces(tokens[half:], count)
    low_mine, low_theirs = gather_pieces(tokens[:half], count)

    docs = doc_ids.astype(F32)
    doc_tails = [
        lax.ppermute(docs[rows - WIN :] + 1.0, "ctx", [(i, i + k) for i in range(blocks - k)])
        for k in range(1, blocks)
    ]
    chosen = jnp.stack([t[WIN - 1] == docs[0] + 1.0 for t in doc_tails]).astype(jnp.int32)
    first = jnp.sum((docs[None, :] < docs[:, None]).astype(F32), 1).astype(jnp.int32)
    in_tail = jnp.sum((doc_tails[0] == docs[0] + 1.0).astype(jnp.int32))
    at = jnp.arange(rows, dtype=jnp.int32)
    window_first = jnp.maximum(jnp.where(first == 0, -in_tail, first), at - (WIN - 1))
    bounds = jnp.stack([first, window_first], 1)
    uses = first[:, None]
    keep = (docs == docs[-1]).astype(jnp.int32)[:, None]

    maps, scale_rows = expansions(heads)
    query_map, key_map = jnp.asarray(maps[0]), jnp.asarray(maps[1])
    scale_rows = jnp.asarray(scale_rows)
    pick = jnp.asarray(picks(heads))

    features_out = w_out.shape[1] // (2 * count)
    split_out = w_out.reshape(w_out.shape[0], count, 2, features_out)
    my_out = lax.dynamic_index_in_dim(split_out, c, 2, keepdims=False)
    their_out = swap(lax.dynamic_index_in_dim(split_out, 1 - c, 2, keepdims=False), count)
    chip_out = jnp.concatenate([my_out, their_out], 0)

    def out_for(chip):
        return lax.dynamic_index_in_dim(chip_out, jnp.clip(chip, 0, count - 1), 1, keepdims=False)

    out_up = [out_for(z + count - s) for s in range(1, count)]
    out_down = [out_for(z - count + s) for s in range(1, count)]
    out_here = out_for(z)

    value_high, feat_high = project(place, high_mine, high_theirs, w_value, w_feat)
    (win_high,) = project(place, high_mine, high_theirs, w_window)
    tail_win, tail_val = (
        lax.ppermute(a[half - WIN :], "ctx", [(i, i + 1) for i in range(blocks - 1)])
        for a in (win_high, value_high)
    )
    state_high = local_state(feat_high, value_high, keep[half:], key_map, scale_rows)

    value_low, feat_low = project(place, low_mine, low_theirs, w_value, w_feat)
    state = local_state(feat_low, value_low, keep[:half], key_map, scale_rows, state_high)
    states = [
        lax.ppermute(state, "ctx", [(i, i + k) for i in range(blocks - k)])
        for k in range(1, blocks)
    ]
    (win_low,) = project(place, low_mine, low_theirs, w_window)
    feats = (feat_low, feat_high)
    inner, windowed = attention(
        feats, (value_low, value_high), (win_low, win_high), tail_win, tail_val, bounds, pick
    )
    mixed = finish(chosen, feats, uses, query_map, scale_rows, inner, windowed, states)

    outs = []
    for mine in mixed:
        chip = jnp.concatenate([mine, swap(mine, count)], 1)

        def partial(weight, *received):
            total = jnp.dot(chip, weight, preferred_element_type=F32)
            for r in received:
                total += r.astype(F32)
            return total.astype(BF16)

        up, down = (), ()
        for s in range(1, count):
            up = (
                lax.ppermute(
                    partial(out_up[s - 1], *up), "head", line(count, 1, range(0, s))
                ),
            )
            down = (
                lax.ppermute(
                    partial(out_down[s - 1], *down), "head", line(count, -1, range(count - s, count))
                ),
            )
        outs.append(partial(out_here, *up, *down))
    return jnp.concatenate(outs, 0)


def solution(mesh):
    return jax.shard_map(
        shards,
        mesh=mesh,
        in_specs=(
            P("ctx", "head"),
            P("ctx"),
            P(None, "head"),
            P(None, "head"),
            P(None, "head"),
            P("head", None),
        ),
        out_specs=P("ctx", "head"),
        check_vma=False,
    )
```

```python
import functools

import jax
import jax.numpy as jnp
import numpy as np
from jax import lax
from jax.experimental import pallas as pl
from jax.experimental.pallas import tpu as pltpu
from jax.sharding import PartitionSpec as P

HEAD_DIM = 128
FEAT = 16
WIN = 64
PAIRS = [(i, j) for i in range(FEAT) for j in range(i, FEAT)]
WIDE = 256
CHUNK = 256
GROUP = 2
STATE = -(-(len(PAIRS) + FEAT + 1) // 16) * 16
VMEM = 60 * 1024 * 1024
F32 = jnp.float32
BF16 = jnp.bfloat16


def params():
    return pltpu.CompilerParams(vmem_limit_bytes=VMEM, dimension_semantics=("arbitrary",))


def line(count, step, sources):
    return [(2 * z + c, 2 * (z + step) + c) for z in sources for c in (0, 1) if 0 <= z + step < count]


def swap(x, count):
    return lax.ppermute(x, "head", [(h, h ^ 1) for h in range(2 * count)])


def project_kernel(parts, first, last, place, mine, theirs, *refs):
    weights, before = refs[:parts], refs[parts : 2 * parts] if first else ()
    outs, sums = refs[-2 * parts : -parts], refs[-parts:]
    width = mine.shape[1]
    step = pl.program_id(0)

    @pl.when(step == 0)
    def _():
        for n in range(parts):
            sums[n][...] = before[n][...] if first else jnp.zeros_like(sums[n])

    c = place[1]
    own = pl.ds(pl.multiple_of(c * width, width), width)
    other = pl.ds(pl.multiple_of((1 - c) * width, width), width)
    for n in range(parts):
        sums[n][...] += jnp.dot(mine[...], weights[n][own, :], preferred_element_type=F32)
        sums[n][...] += jnp.dot(theirs[...], weights[n][other, :], preferred_element_type=F32)

    @pl.when(step == pl.num_programs(0) - 1)
    def _():
        for n in range(parts):
            outs[n][...] = sums[n][...].astype(outs[n].dtype)


def project(place, chips, mine, theirs, weights, before=None, dtype=BF16):
    rows = mine.shape[0]
    width = mine.shape[1] // len(chips)
    count = weights[0].shape[0] // (2 * width)
    if len(chips) == 1:
        pick = lambda j, p: p[0] + chips[0]
    else:
        early = chips == (0, 1, count - 1)
        pick = lambda j, p: p[0] + (jnp.where(j == 2, count - 1, j) if early else j + chips[0])
    piece = pl.BlockSpec((rows, width), lambda j, p: (0, j))
    specs = [piece, piece]
    specs += [
        pl.BlockSpec((2 * width, w.shape[1]), lambda j, p: (lax.rem(pick(j, p), count), 0))
        for w in weights
    ]
    wholes = [pl.BlockSpec((rows, w.shape[1]), lambda j, p: (0, 0)) for w in weights]
    args = [mine, theirs, *weights]
    if before is not None:
        specs += wholes
        args += list(before)
    return pl.pallas_call(
        functools.partial(project_kernel, len(weights), before is not None, dtype == BF16),
        grid_spec=pltpu.PrefetchScalarGridSpec(
            num_scalar_prefetch=1,
            grid=(len(chips),),
            in_specs=specs,
            out_specs=wholes,
            scratch_shapes=[pltpu.VMEM((rows, w.shape[1]), F32) for w in weights],
        ),
        out_shape=[jax.ShapeDtypeStruct((rows, w.shape[1]), dtype) for w in weights],
        compiler_params=params(),
    )(place, *args)


def expansions(heads):
    lanes = heads * 2 * FEAT
    maps = np.zeros((2, heads, lanes, 2 * WIDE), np.float32)
    rows = np.zeros((3, WIDE), np.float32)
    for h in range(heads):
        for side in (0, 1):
            base = h * 2 * FEAT + side * FEAT
            for n, (i, j) in enumerate(PAIRS):
                maps[side, h, base + i, n] = 1.0
                maps[side, h, base + j, WIDE + n] = 1.0
            for i in range(FEAT):
                maps[side, h, base + i, len(PAIRS) + i] = 1.0
    for n, (i, j) in enumerate(PAIRS):
        rows[2, n] = (2.0 * FEAT) ** -0.5 * (1.0 if i == j else 2.0**0.5)
    rows[1, len(PAIRS) : len(PAIRS) + FEAT + 1] = 1.0
    rows[0, len(PAIRS) + FEAT] = 1.0
    rows[2, len(PAIRS) : len(PAIRS) + FEAT] = FEAT**-0.25
    rows[2, len(PAIRS) + FEAT] = 1.0
    return maps.astype(jnp.bfloat16), rows


def picks(heads):
    lanes = heads * 2 * FEAT
    maps = np.zeros((heads, lanes, 256), np.float32)
    for h in range(heads):
        for i in range(FEAT):
            maps[h, h * 2 * FEAT + i, i] = 1.0
            maps[h, h * 2 * FEAT + FEAT + i, 128 + i] = 1.0
    return maps.astype(jnp.bfloat16)


def phi(features, expand, rows):
    factors = jnp.dot(features, expand, preferred_element_type=F32)
    left = factors[:, :WIDE] + rows[0:1]
    right = factors[:, WIDE:] + rows[1:2]
    return (left * right * rows[2:3]).astype(BF16)


def chunk_sums(limits, start, features, values, expand, rows, heads):
    sums = []
    for n in range(features.shape[0] // CHUNK):
        here = slice(n * CHUNK, (n + 1) * CHUNK)
        at = lax.broadcasted_iota(jnp.int32, (CHUNK, HEAD_DIM), 0) + (start + n) * CHUNK
        good = at >= limits[start + n]
        one = []
        for h in range(heads):
            phi_key = phi(features[here], expand[h], rows[...])
            kept = jnp.where(good, values[here, h * HEAD_DIM : (h + 1) * HEAD_DIM].astype(F32), 0.0)
            one.append(
                lax.dot_general(
                    phi_key, kept.astype(BF16), (((0,), (0,)), ((), ())), preferred_element_type=F32
                )[:STATE]
            )
        sums.append(one)
    return sums


def high_sums_kernel(start, limits, features, values, expand, rows, out):
    heads = out.shape[1]
    for n, one in enumerate(chunk_sums(limits, start, features, values, expand, rows, heads)):
        for h in range(heads):
            out[n, h] = one[h]


def low_sums_kernel(limits, features, values, expand, rows, high, prefix, end):
    heads = high.shape[1]
    low = chunk_sums(limits, 0, features, values, expand, rows, heads)
    for h in range(heads):
        state = jnp.zeros((STATE, HEAD_DIM), F32)
        for n in range(len(low) + high.shape[0]):
            prefix[n, h] = state
            chunk = low[n][h] if n < len(low) else high[n - len(low), h]
            state = chunk + jnp.where(limits[n] <= n * CHUNK, state, 0.0)
        end[h] = state.astype(BF16)


def sums(limits, features, values, expand, rows, high=None):
    count, columns = values.shape
    heads = columns // HEAD_DIM
    chunks = count // CHUNK
    shape = jax.ShapeDtypeStruct((chunks, heads, STATE, HEAD_DIM), F32)
    vmem = pl.BlockSpec(memory_space=pltpu.VMEM)
    smem = pl.BlockSpec(memory_space=pltpu.SMEM)
    if high is None:
        return pl.pallas_call(
            functools.partial(high_sums_kernel, chunks),
            in_specs=[smem] + [vmem] * 4,
            out_specs=vmem,
            out_shape=shape,
            compiler_params=pltpu.CompilerParams(vmem_limit_bytes=VMEM),
        )(limits, features, values, expand, rows)
    return pl.pallas_call(
        low_sums_kernel,
        in_specs=[smem] + [vmem] * 5,
        out_specs=[vmem, vmem],
        out_shape=[
            jax.ShapeDtypeStruct((2 * chunks, heads, STATE, HEAD_DIM), F32),
            jax.ShapeDtypeStruct((heads, STATE, HEAD_DIM), BF16),
        ],
        compiler_params=pltpu.CompilerParams(vmem_limit_bytes=VMEM),
    )(limits, features, values, expand, rows, high)


TILE = 128


def window_tile(queries, keys, values, window_first, start):
    wide = TILE + WIN
    logits = lax.dot_general(
        queries, keys, (((1,), (1,)), ((), ())), preferred_element_type=F32
    ) * HEAD_DIM**-0.5
    at = lax.broadcasted_iota(jnp.int32, (TILE, wide), 1)
    row = lax.broadcasted_iota(jnp.int32, (TILE, wide), 0)
    good = (at >= window_first - start) & (at <= row + WIN)
    logits = jnp.where(good, logits, -1e30)
    top = jnp.max(logits, 1, keepdims=True)
    weight = jnp.where(good, jnp.exp(logits - top), 0.0)
    probs = (weight / jnp.sum(weight, 1, keepdims=True)).astype(BF16)
    return jnp.dot(probs, values, preferred_element_type=F32)


def local_kernel(low, features, values, window, bounds, pick, expand, rows, *refs):
    if low:
        tail_values, tail_window, next_values, next_window = refs[:4]
        inner, windowed, phi_query, next_windowed = refs[4:]
    else:
        inner, windowed, phi_query = refs
    half = features.shape[0]
    base = 0 if low else half
    for h in range(values.shape[1] // HEAD_DIM):
        column = slice(h * HEAD_DIM, (h + 1) * HEAD_DIM)
        query = slice(2 * h * HEAD_DIM, (2 * h + 1) * HEAD_DIM)
        key = slice((2 * h + 1) * HEAD_DIM, (2 * h + 2) * HEAD_DIM)
        phi_query[:, h * WIDE : (h + 1) * WIDE] = phi(features[...], expand[h], rows[...])
        for n in range(half // CHUNK):
            here = slice(n * CHUNK, (n + 1) * CHUNK)
            both = jnp.dot(features[here], pick[h], preferred_element_type=F32).astype(BF16)
            dots = lax.dot_general(
                both[:, :128], both[:, 128:], (((1,), (1,)), ((), ())), preferred_element_type=F32
            )
            score = dots * (dots * (0.5 / FEAT) + FEAT**-0.5) + 1.0
            at = lax.broadcasted_iota(jnp.int32, (CHUNK, CHUNK), 1)
            row = lax.broadcasted_iota(jnp.int32, (CHUNK, CHUNK), 0)
            first = bounds[base + n * CHUNK : base + (n + 1) * CHUNK, 0:1] - (base + n * CHUNK)
            score = jnp.where((at >= first) & (at <= row), score, 0.0).astype(BF16)
            inner[here, column] = jnp.dot(
                score, values[here, column], preferred_element_type=F32
            )
        for n in range(half // TILE):
            here = slice(n * TILE, (n + 1) * TILE)
            near = slice(n * TILE - WIN, (n + 1) * TILE)
            start = base + n * TILE - WIN
            first = bounds[base + n * TILE : base + (n + 1) * TILE, 1:2]
            if n:
                keys, vals = window[near, key], values[near, column]
            elif low:
                keys = jnp.concatenate([tail_window[:, key], window[:TILE, key]], 0)
                vals = jnp.concatenate([tail_values[:, column], values[:TILE, column]], 0)
            else:
                continue
            windowed[here, column] = window_tile(window[here, query], keys, vals, first, start)
        if low:
            keys = jnp.concatenate([window[half - WIN :, key], next_window[:, key]], 0)
            vals = jnp.concatenate([values[half - WIN :, column], next_values[:, column]], 0)
            first = bounds[half : half + TILE, 1:2]
            next_windowed[:, column] = window_tile(
                next_window[:, query], keys, vals, first, half - WIN
            )


def local(low, features, values, window, bounds, pick, expand, rows, tails=(), after=()):
    half, columns = values.shape
    heads = columns // HEAD_DIM
    group = min(GROUP, heads)

    def full(a):
        return pl.BlockSpec(a.shape, lambda g: (0,) * a.ndim)

    def some(count, width):
        return pl.BlockSpec((count, group * width), lambda g: (0, g))

    def per_head(a):
        return pl.BlockSpec((group,) + a.shape[1:], lambda g: (g, 0, 0))

    specs = [
        full(features), some(half, HEAD_DIM), some(half, 2 * HEAD_DIM), full(bounds),
        per_head(pick), per_head(expand), full(rows),
    ]
    out_specs = [some(half, HEAD_DIM), some(half, HEAD_DIM), some(half, WIDE)]
    shapes = [
        jax.ShapeDtypeStruct((half, columns), F32),
        jax.ShapeDtypeStruct((half, columns), F32),
        jax.ShapeDtypeStruct((half, heads * WIDE), BF16),
    ]
    if low:
        specs += [
            some(WIN, HEAD_DIM), some(WIN, 2 * HEAD_DIM), some(TILE, HEAD_DIM), some(TILE, 2 * HEAD_DIM)
        ]
        out_specs.append(some(TILE, HEAD_DIM))
        shapes.append(jax.ShapeDtypeStruct((TILE, columns), F32))
    return pl.pallas_call(
        functools.partial(local_kernel, low),
        grid=(heads // group,),
        in_specs=specs,
        out_specs=out_specs,
        out_shape=shapes,
        compiler_params=params(),
    )(features, values, window, bounds, pick, expand, rows, *tails, *after)


def finish_kernel(start, shifts, limits, chosen, phi_query, bounds, inner, windowed, prefix, *refs):
    states, out = refs[:shifts], refs[-1]
    head_first = refs[shifts] if len(refs) == shifts + 2 else None
    for h in range(inner.shape[1] // HEAD_DIM):
        column = slice(h * HEAD_DIM, (h + 1) * HEAD_DIM)
        incoming = jnp.zeros((STATE, HEAD_DIM), F32)
        for k in range(shifts):
            incoming += jnp.where(chosen[k] > 0, states[k][h].astype(F32), 0.0)
        for n in range(inner.shape[0] // CHUNK):
            here = slice(n * CHUNK, (n + 1) * CHUNK)
            chunk = start + n
            state = incoming
            if chunk:
                state = jnp.where(limits[chunk - 1] <= 0, incoming, 0.0) + prefix[n, h]
            state = jnp.concatenate([state, jnp.zeros((WIDE - STATE, HEAD_DIM), F32)], 0)
            carried = jnp.dot(
                phi_query[here, h * WIDE : (h + 1) * WIDE], state.astype(BF16),
                preferred_element_type=F32,
            )
            first = bounds[chunk * CHUNK : (chunk + 1) * CHUNK, 0:1]
            linear = inner[here, column] + jnp.where(first <= chunk * CHUNK, carried, 0.0)
            mean = jnp.mean(linear * linear, 1, keepdims=True)
            normed = linear * lax.rsqrt(mean + 1e-5)
            if n == 0 and head_first is not None:
                out[:TILE, column] = (normed[:TILE] + head_first[:, column]).astype(BF16)
                out[TILE:CHUNK, column] = (normed[TILE:] + windowed[TILE:CHUNK, column]).astype(BF16)
            else:
                out[here, column] = (normed + windowed[here, column]).astype(BF16)


def finish(start, limits, chosen, phi_query, bounds, inner, windowed, prefix, states, head_first=None):
    half, columns = inner.shape
    heads = columns // HEAD_DIM
    group = min(GROUP, heads)
    chunks = half // CHUNK

    def some(count, width):
        return pl.BlockSpec((count, group * width), lambda g, *_: (0, g))

    specs = [
        some(half, WIDE), pl.BlockSpec(bounds.shape, lambda g, *_: (0, 0)),
        some(half, HEAD_DIM), some(half, HEAD_DIM),
        pl.BlockSpec((chunks, group, STATE, HEAD_DIM), lambda g, *_: (start // chunks, g, 0, 0)),
    ]
    specs += [pl.BlockSpec((group, STATE, HEAD_DIM), lambda g, *_: (g, 0, 0))] * len(states)
    args = [phi_query, bounds, inner, windowed, prefix, *states]
    if head_first is not None:
        specs.append(some(TILE, HEAD_DIM))
        args.append(head_first)
    return pl.pallas_call(
        functools.partial(finish_kernel, start, len(states)),
        grid_spec=pltpu.PrefetchScalarGridSpec(
            num_scalar_prefetch=2,
            grid=(heads // group,),
            in_specs=specs,
            out_specs=some(half, HEAD_DIM),
        ),
        out_shape=jax.ShapeDtypeStruct((half, columns), BF16),
        compiler_params=params(),
    )(limits, chosen, *args)


def output_kernel(received, place, mine, theirs, own_rows, other_rows, *refs):
    total = jnp.dot(mine[...], own_rows[...], preferred_element_type=F32)
    total += jnp.dot(theirs[...], other_rows[...], preferred_element_type=F32)
    for n in range(received):
        total += refs[n][...].astype(F32)
    refs[-1][...] = total.astype(BF16)


def output(where, mine, theirs, own_rows, other_rows, received):
    rows, depth = mine.shape
    width = other_rows.shape[2]
    tile = min(256, width)
    cuts = width // tile
    result = pl.BlockSpec((rows, tile), lambda j, p: (0, j))
    whole = pl.BlockSpec((rows, depth), lambda j, p: (0, 0))
    return pl.pallas_call(
        functools.partial(output_kernel, len(received)),
        grid_spec=pltpu.PrefetchScalarGridSpec(
            num_scalar_prefetch=1,
            grid=(cuts,),
            in_specs=[
                whole, whole,
                pl.BlockSpec((depth, tile), lambda j, p: (0, (2 * p[0] + p[1]) * cuts + j)),
                pl.BlockSpec((None, depth, tile), lambda j, p: (p[0], 0, j)),
            ] + [result] * len(received),
            out_specs=result,
        ),
        out_shape=jax.ShapeDtypeStruct((rows, width), BF16),
        compiler_params=params(),
    )(where, mine, theirs, own_rows, other_rows, *received)


def after(x, *others):
    return lax.optimization_barrier((x, *others))[0]


def shards(tokens, doc_ids, w_feat, w_value, w_window, w_out):
    rows = tokens.shape[0]
    half = rows // 2
    chunks = rows // CHUNK
    heads = w_value.shape[1] // HEAD_DIM
    count = lax.axis_size("head") // 2
    blocks = lax.axis_size("ctx")
    me = lax.axis_index("head")
    z, c = me // 2, me % 2
    place = jnp.stack([z, c]).astype(jnp.int32)

    def hop(x, step, sources):
        return lax.ppermute(x, "head", line(count, step, sources))

    def near(x):
        return hop(x, 1, range(count)), hop(x, -1, range(count))

    def far(x):
        return hop(x, count - 1, [0]), hop(x, 1 - count, [count - 1])

    def chain(up, down):
        ups, downs = [up], [down]
        for s in range(2, count - 1):
            ups.append(hop(ups[-1], 1, range(s - 1, count)))
            downs.append(hop(downs[-1], -1, range(0, count - s + 1)))
        return ups, downs

    def early_pieces(x, up, down, far_up, far_down):
        mine = jnp.concatenate([x, down + far_up, far_down + up], 1)
        return mine, swap(mine, count)

    def late_pieces(ups, downs):
        mine = jnp.concatenate(
            [downs[s - 1] + ups[count - s - 1] for s in range(2, count - 1)], 1
        )
        return mine, swap(mine, count)

    high, low = tokens[half:], tokens[:half]
    high_near = near(high)
    high_far = far(high)

    docs = doc_ids.astype(F32)
    doc_tails = [
        lax.ppermute(docs[rows - WIN :] + 1.0, "ctx", [(i, i + k) for i in range(blocks - k)])
        for k in range(1, blocks)
    ]
    chosen = jnp.stack([t[WIN - 1] == docs[0] + 1.0 for t in doc_tails]).astype(jnp.int32)
    first = jnp.sum((docs[None, :] < docs[:, None]).astype(F32), 1).astype(jnp.int32)
    in_tail = jnp.sum((doc_tails[0] == docs[0] + 1.0).astype(jnp.int32))
    at = jnp.arange(rows, dtype=jnp.int32)
    window_first = jnp.maximum(jnp.where(first == 0, -in_tail, first), at - (WIN - 1))
    bounds = jnp.stack([first, window_first], 1)
    limits = jnp.stack([first[min((n + 1) * CHUNK, rows - 1)] for n in range(chunks)])

    maps, scale_rows = expansions(heads)
    query_map, key_map = jnp.asarray(maps[0]), jnp.asarray(maps[1])
    scale_rows = jnp.asarray(scale_rows)
    pick = jnp.asarray(picks(heads))

    depth, columns = w_out.shape
    width = columns // (2 * count)
    other_rows = swap(
        jnp.stack(
            [
                lax.dynamic_slice(w_out, (0, (2 * chip + 1 - c) * width), (depth, width))
                for chip in range(count)
            ]
        ),
        count,
    )

    weights = (w_feat, w_value, w_window)
    early = (0, 1, count - 1)
    late = tuple(range(2, count - 1))

    high_ups, high_downs = chain(*high_near)
    low_far = far(after(low, *high_near))
    mine, theirs = early_pieces(high, *high_near, *high_far)
    part = project(place, early, mine, theirs, weights, None, F32)
    high_ups[-1], high_downs[-1], other_rows, bounds, chosen = lax.optimization_barrier(
        (high_ups[-1], high_downs[-1], other_rows, bounds, chosen, part[0])
    )[:5]
    low_near = near(after(low, high_ups[-1], high_downs[-1], other_rows, bounds, chosen))
    mine, theirs = late_pieces(high_ups, high_downs)
    feat_high, value_high, win_high = project(place, late, mine, theirs, weights, part)
    tail_win, tail_value = (
        lax.ppermute(a[half - WIN :], "ctx", [(i, i + 1) for i in range(blocks - 1)])
        for a in (win_high, value_high)
    )
    high_sums = sums(limits, feat_high, value_high, key_map, scale_rows)
    inner_high, windowed_high, phi_high = local(
        False, feat_high, value_high, win_high, bounds, pick, query_map, scale_rows
    )

    *low_near, far_up, far_down, tail_win, tail_value = lax.optimization_barrier(
        (*low_near, *low_far, tail_win, tail_value, inner_high, high_sums)
    )[:6]
    low_ups, low_downs = chain(*low_near)
    mine, theirs = early_pieces(low, *low_near, far_up, far_down)
    part = project(place, early, mine, theirs, weights, None, F32)
    low_ups[-1], low_downs[-1] = lax.optimization_barrier((low_ups[-1], low_downs[-1], part[0]))[:2]
    mine, theirs = late_pieces(low_ups, low_downs)
    feat_low, value_low = project(place, late, mine, theirs, weights[:2], part[:2])
    prefix, state = sums(limits, feat_low, value_low, key_map, scale_rows, high_sums)
    states = [
        lax.ppermute(state, "ctx", [(i, i + k) for i in range(blocks - k)])
        for k in range(1, blocks)
    ]
    (win_low,) = project(place, late, after(mine, state), theirs, weights[2:], part[2:])
    inner_low, windowed_low, phi_low, windowed_next = local(
        True, feat_low, value_low, win_low, bounds, pick, query_map, scale_rows,
        (tail_value, tail_win), (value_high, win_high),
    )
    mixed_high = finish(
        chunks // 2, limits, chosen, phi_high, bounds, inner_high, windowed_high, prefix, states,
        windowed_next,
    )
    mixed_low = finish(
        0, limits, chosen, phi_low, bounds, inner_low, windowed_low, prefix, states
    )

    outs = []
    for mixed in (mixed_low, mixed_high):
        swapped = swap(mixed, count)

        def part_of(chip, *received):
            where = jnp.stack([jnp.clip(chip, 0, count - 1), c]).astype(jnp.int32)
            return output(where, mixed, swapped, w_out, other_rows, received)

        up, down = (), ()
        for s in range(1, count):
            up = (hop(part_of(z + count - s, *up), 1, range(0, s)),)
            down = (hop(part_of(z - count + s, *down), -1, range(count - s, count)),)
        outs.append(part_of(z, *up, *down))
    return jnp.concatenate(outs, 0)


def solution(mesh):
    return jax.shard_map(
        shards,
        mesh=mesh,
        in_specs=(
            P("ctx", "head"),
            P("ctx"),
            P(None, "head"),
            P(None, "head"),
            P(None, "head"),
            P("head", None),
        ),
        out_specs=P("ctx", "head"),
        check_vma=False,
    )
```

```python
import functools

import jax
import jax.numpy as jnp
import numpy as np
from jax import lax
from jax.experimental import pallas as pl
from jax.experimental.pallas import tpu as pltpu
from jax.sharding import PartitionSpec as P

HEAD_DIM = 128
FEAT = 16
WIN = 64
PAIRS = [(i, j) for i in range(FEAT) for j in range(i, FEAT)]
WIDE = 256
CHUNK = 256
GROUP = 2
STATE = -(-(len(PAIRS) + FEAT + 1) // 16) * 16
VMEM = 60 * 1024 * 1024
F32 = jnp.float32
BF16 = jnp.bfloat16


def params():
    return pltpu.CompilerParams(vmem_limit_bytes=VMEM, dimension_semantics=("arbitrary",))


def line(count, step, sources):
    return [(2 * z + c, 2 * (z + step) + c) for z in sources for c in (0, 1) if 0 <= z + step < count]


def swap(x, count):
    return lax.ppermute(x, "head", [(h, h ^ 1) for h in range(2 * count)])


def project_kernel(parts, place, mine, theirs, mine_late, theirs_late, *refs):
    weights, outs = refs[:parts], refs[parts : 2 * parts]
    sums, both = refs[2 * parts : -1], refs[-1]
    width = mine.shape[1]
    step = pl.program_id(0)
    c = place[1]
    own = pl.ds(pl.multiple_of(c * width, width), width)
    other = pl.ds(pl.multiple_of((1 - c) * width, width), width)

    @pl.when(step < 3)
    def _():
        both[:, own] = mine[...]
        both[:, other] = theirs[...]

    @pl.when(step >= 3)
    def _():
        both[:, own] = mine_late[...]
        both[:, other] = theirs_late[...]

    @pl.when(step == 0)
    def _():
        for n in range(parts):
            sums[n][...] = jnp.dot(both[...], weights[n][...], preferred_element_type=F32)

    @pl.when(step > 0)
    def _():
        for n in range(parts):
            sums[n][...] += jnp.dot(both[...], weights[n][...], preferred_element_type=F32)

    @pl.when(step == pl.num_programs(0) - 1)
    def _():
        for n in range(parts):
            outs[n][...] = sums[n][...].astype(outs[n].dtype)


def project(place, early, late, weights):
    rows = early[0].shape[0]
    width = early[0].shape[1] // 3
    count = weights[0].shape[0] // (2 * width)

    def chip(j, p):
        away = jnp.where(j < 2, j, jnp.where(j == 2, count - 1, j - 1))
        return lax.rem(p[0] + away, count), 0

    piece = pl.BlockSpec((rows, width), lambda j, p: (0, jnp.minimum(j, 2)))
    later = pl.BlockSpec((rows, width), lambda j, p: (0, jnp.maximum(j - 3, 0)))
    return pl.pallas_call(
        functools.partial(project_kernel, len(weights)),
        grid_spec=pltpu.PrefetchScalarGridSpec(
            num_scalar_prefetch=1,
            grid=(count,),
            in_specs=[piece, piece, later, later]
            + [pl.BlockSpec((2 * width, w.shape[1]), chip) for w in weights],
            out_specs=[pl.BlockSpec((rows, w.shape[1]), lambda j, p: (0, 0)) for w in weights],
            scratch_shapes=[pltpu.VMEM((rows, w.shape[1]), F32) for w in weights]
            + [pltpu.VMEM((rows, 2 * width), BF16)],
        ),
        out_shape=[jax.ShapeDtypeStruct((rows, w.shape[1]), BF16) for w in weights],
        compiler_params=params(),
    )(place, *early, *late, *weights)


def expansions(heads):
    lanes = heads * 2 * FEAT
    maps = np.zeros((2, heads, lanes, 2 * WIDE), np.float32)
    rows = np.zeros((3, WIDE), np.float32)
    for h in range(heads):
        for side in (0, 1):
            base = h * 2 * FEAT + side * FEAT
            for n, (i, j) in enumerate(PAIRS):
                maps[side, h, base + i, n] = 1.0
                maps[side, h, base + j, WIDE + n] = 1.0
            for i in range(FEAT):
                maps[side, h, base + i, len(PAIRS) + i] = 1.0
    for n, (i, j) in enumerate(PAIRS):
        rows[2, n] = (2.0 * FEAT) ** -0.5 * (1.0 if i == j else 2.0**0.5)
    rows[1, len(PAIRS) : len(PAIRS) + FEAT + 1] = 1.0
    rows[0, len(PAIRS) + FEAT] = 1.0
    rows[2, len(PAIRS) : len(PAIRS) + FEAT] = FEAT**-0.25
    rows[2, len(PAIRS) + FEAT] = 1.0
    return maps.astype(jnp.bfloat16), rows


def picks(heads):
    lanes = heads * 2 * FEAT
    maps = np.zeros((heads, lanes, 256), np.float32)
    for h in range(heads):
        for i in range(FEAT):
            maps[h, h * 2 * FEAT + i, i] = 1.0
            maps[h, h * 2 * FEAT + FEAT + i, 128 + i] = 1.0
    return maps.astype(jnp.bfloat16)


def phi(features, expand, rows):
    factors = jnp.dot(features, expand, preferred_element_type=F32)
    left = factors[:, :WIDE] + rows[0:1]
    right = factors[:, WIDE:] + rows[1:2]
    return (left * right * rows[2:3]).astype(BF16)


def chunk_sums(limits, start, features, values, expand, rows, heads):
    sums = []
    for n in range(features.shape[0] // CHUNK):
        here = slice(n * CHUNK, (n + 1) * CHUNK)
        at = lax.broadcasted_iota(jnp.int32, (CHUNK, HEAD_DIM), 0) + (start + n) * CHUNK
        good = at >= limits[start + n]
        one = []
        for h in range(heads):
            phi_key = phi(features[here], expand[h], rows[...])
            kept = jnp.where(good, values[here, h * HEAD_DIM : (h + 1) * HEAD_DIM].astype(F32), 0.0)
            one.append(
                lax.dot_general(
                    phi_key, kept.astype(BF16), (((0,), (0,)), ((), ())), preferred_element_type=F32
                )[:STATE]
            )
        sums.append(one)
    return sums


def high_sums_kernel(start, limits, features, values, expand, rows, out):
    heads = out.shape[1]
    for n, one in enumerate(chunk_sums(limits, start, features, values, expand, rows, heads)):
        for h in range(heads):
            out[n, h] = one[h]


def low_sums_kernel(limits, features, values, expand, rows, high, prefix, end):
    mark = lax.broadcasted_iota(jnp.int32, (STATE, HEAD_DIM), 0) == STATE - 1
    heads = high.shape[1]
    low = chunk_sums(limits, 0, features, values, expand, rows, heads)
    for h in range(heads):
        state = jnp.zeros((STATE, HEAD_DIM), F32)
        for n in range(len(low) + high.shape[0]):
            prefix[n, h] = state
            chunk = low[n][h] if n < len(low) else high[n - len(low), h]
            state = chunk + jnp.where(limits[n] <= n * CHUNK, state, 0.0)
        end[h] = jnp.where(mark, (limits[2 * len(low)] + 1).astype(F32), state).astype(BF16)


def sums(limits, features, values, expand, rows, high=None):
    count, columns = values.shape
    heads = columns // HEAD_DIM
    chunks = count // CHUNK
    shape = jax.ShapeDtypeStruct((chunks, heads, STATE, HEAD_DIM), F32)
    vmem = pl.BlockSpec(memory_space=pltpu.VMEM)
    smem = pl.BlockSpec(memory_space=pltpu.SMEM)
    if high is None:
        return pl.pallas_call(
            functools.partial(high_sums_kernel, chunks),
            in_specs=[smem] + [vmem] * 4,
            out_specs=vmem,
            out_shape=shape,
            compiler_params=pltpu.CompilerParams(vmem_limit_bytes=VMEM),
        )(limits, features, values, expand, rows)
    return pl.pallas_call(
        low_sums_kernel,
        in_specs=[smem] + [vmem] * 5,
        out_specs=[vmem, vmem],
        out_shape=[
            jax.ShapeDtypeStruct((2 * chunks, heads, STATE, HEAD_DIM), F32),
            jax.ShapeDtypeStruct((heads, STATE, HEAD_DIM), BF16),
        ],
        compiler_params=pltpu.CompilerParams(vmem_limit_bytes=VMEM),
    )(limits, features, values, expand, rows, high)


TILE = 128


def windows(tiles):
    wide = TILE + WIN
    logits = jnp.concatenate(
        [
            lax.dot_general(q, k, (((1,), (1,)), ((), ())), preferred_element_type=F32)
            for q, k, _, _, _ in tiles
        ],
        0,
    )
    at = lax.broadcasted_iota(jnp.int32, (TILE, wide), 1)
    row = lax.broadcasted_iota(jnp.int32, (TILE, wide), 0)
    near = (at <= row + WIN) & (at > row)
    good = jnp.concatenate([near & (at >= first - start) for _, _, _, first, start in tiles], 0)
    logits = jnp.where(good, logits * HEAD_DIM**-0.5, -1e30)
    top = jnp.max(logits, 1, keepdims=True)
    weight = jnp.where(good, jnp.exp(logits - top), 0.0)
    probs = (weight / jnp.sum(weight, 1, keepdims=True)).astype(BF16)
    return [
        jnp.dot(probs[n * TILE : (n + 1) * TILE], tile[2], preferred_element_type=F32)
        for n, tile in enumerate(tiles)
    ]


def local_kernel(low, features, values, window, bounds, pick, expand, rows, *refs):
    if low:
        tail, tail_docs, first_doc, next_values, next_window = refs[:5]
        inner, windowed, phi_query, next_windowed = refs[5:]
        same = jnp.where(tail_docs[...].astype(F32) == first_doc[0:1, 0:1] + 1.0, 1.0, 0.0)
        in_tail = jnp.sum(same, 0, keepdims=True)[:, 0:1].astype(jnp.int32)
    else:
        inner, windowed, phi_query = refs
    half = features.shape[0]
    base = 0 if low else half
    chunks = half // CHUNK
    at = lax.broadcasted_iota(jnp.int32, (CHUNK, CHUNK), 1)
    row = lax.broadcasted_iota(jnp.int32, (CHUNK, CHUNK), 0)
    good = jnp.concatenate(
        [
            (at <= row) & (at >= bounds[base + n * CHUNK : base + (n + 1) * CHUNK] - (base + n * CHUNK))
            for n in range(chunks)
        ],
        0,
    )
    heads = values.shape[1] // HEAD_DIM
    for h in range(heads):
        column = slice(h * HEAD_DIM, (h + 1) * HEAD_DIM)
        query = slice(2 * h * HEAD_DIM, (2 * h + 1) * HEAD_DIM)
        key = slice((2 * h + 1) * HEAD_DIM, (2 * h + 2) * HEAD_DIM)
        both = jnp.dot(features[...], pick[h], preferred_element_type=F32).astype(BF16)
        dots = jnp.concatenate(
            [
                lax.dot_general(
                    both[n * CHUNK : (n + 1) * CHUNK, :128], both[n * CHUNK : (n + 1) * CHUNK, 128:],
                    (((1,), (1,)), ((), ())), preferred_element_type=F32,
                )
                for n in range(chunks)
            ],
            0,
        )
        tiles, targets = [], []
        for n in range(half // TILE):
            here = slice(n * TILE, (n + 1) * TILE)
            near = slice(n * TILE - WIN, (n + 1) * TILE)
            start = base + n * TILE - WIN
            first = bounds[base + n * TILE : base + (n + 1) * TILE]
            if n:
                keys, vals = window[near, key], values[near, column]
            elif low:
                skip = 2 * heads * HEAD_DIM
                keys = jnp.concatenate([tail[:, key], window[:TILE, key]], 0)
                vals = jnp.concatenate(
                    [tail[:, skip + h * HEAD_DIM : skip + (h + 1) * HEAD_DIM], values[:TILE, column]], 0
                )
                first = jnp.where(first == 0, -in_tail, first)
            else:
                continue
            tiles.append((window[here, query], keys, vals, first, start))
            targets.append((windowed, here))
        if low:
            keys = jnp.concatenate([window[half - WIN :, key], next_window[:, key]], 0)
            vals = jnp.concatenate([values[half - WIN :, column], next_values[:, column]], 0)
            first = bounds[half : half + TILE]
            tiles.append((next_window[:, query], keys, vals, first, half - WIN))
            targets.append((next_windowed, slice(0, TILE)))
        results = windows(tiles)
        score = dots * (dots * (0.5 / FEAT) + FEAT**-0.5) + 1.0
        score = jnp.where(good, score, 0.0).astype(BF16)
        phi_query[:, h * WIDE : (h + 1) * WIDE] = phi(features[...], expand[h], rows[...])
        for n in range(chunks):
            here = slice(n * CHUNK, (n + 1) * CHUNK)
            inner[here, column] = jnp.dot(
                score[here], values[here, column], preferred_element_type=F32
            )
        for (ref, here), result in zip(targets, results):
            ref[here, column] = result


def local(low, features, values, window, bounds, pick, expand, rows, tails=(), after=()):
    half, columns = values.shape
    heads = columns // HEAD_DIM
    group = min(GROUP, heads)

    def full(a):
        return pl.BlockSpec(a.shape, lambda g: (0,) * a.ndim)

    def some(count, width):
        return pl.BlockSpec((count, group * width), lambda g: (0, g))

    def per_head(a):
        return pl.BlockSpec((group,) + a.shape[1:], lambda g: (g, 0, 0))

    specs = [
        full(features), some(half, HEAD_DIM), some(half, 2 * HEAD_DIM), full(bounds),
        per_head(pick), per_head(expand), full(rows),
    ]
    out_specs = [some(half, HEAD_DIM), some(half, HEAD_DIM), some(half, WIDE)]
    shapes = [
        jax.ShapeDtypeStruct((half, columns), F32),
        jax.ShapeDtypeStruct((half, columns), F32),
        jax.ShapeDtypeStruct((half, heads * WIDE), BF16),
    ]
    if low:
        specs += [
            some(WIN, 3 * HEAD_DIM),
            pl.BlockSpec((WIN, HEAD_DIM), lambda g: (0, 3 * heads)),
            full(tails[-1]),
            some(TILE, HEAD_DIM), some(TILE, 2 * HEAD_DIM),
        ]
        out_specs.append(some(TILE, HEAD_DIM))
        shapes.append(jax.ShapeDtypeStruct((TILE, columns), F32))
    return pl.pallas_call(
        functools.partial(local_kernel, low),
        grid=(heads // group,),
        in_specs=specs,
        out_specs=out_specs,
        out_shape=shapes,
        compiler_params=params(),
    )(features, values, window, bounds, pick, expand, rows, *tails, *after)


def finish_kernel(start, shifts, limits, first_doc, phi_query, bounds, inner, windowed, prefix, *refs):
    states, out = refs[:shifts], refs[-1]
    head_first = refs[shifts] if len(refs) == shifts + 2 else None
    unmarked = lax.broadcasted_iota(jnp.int32, (STATE, HEAD_DIM), 0) < STATE - 1
    for h in range(inner.shape[1] // HEAD_DIM):
        column = slice(h * HEAD_DIM, (h + 1) * HEAD_DIM)
        incoming = jnp.zeros((STATE, HEAD_DIM), F32)
        for k in range(shifts):
            sent = states[k][h].astype(F32)
            wanted = (sent[STATE - 1 :] == first_doc[0:1, :] + 1.0) & unmarked
            incoming += jnp.where(wanted, sent, 0.0)
        for n in range(inner.shape[0] // CHUNK):
            here = slice(n * CHUNK, (n + 1) * CHUNK)
            chunk = start + n
            state = incoming
            if chunk:
                state = jnp.where(limits[chunk - 1] <= 0, incoming, 0.0) + prefix[n, h]
            state = jnp.concatenate([state, jnp.zeros((WIDE - STATE, HEAD_DIM), F32)], 0)
            carried = jnp.dot(
                phi_query[here, h * WIDE : (h + 1) * WIDE], state.astype(BF16),
                preferred_element_type=F32,
            )
            first = bounds[chunk * CHUNK : (chunk + 1) * CHUNK, 0:1]
            linear = inner[here, column] + jnp.where(first <= chunk * CHUNK, carried, 0.0)
            mean = jnp.mean(linear * linear, 1, keepdims=True)
            normed = linear * lax.rsqrt(mean + 1e-5)
            if n == 0 and head_first is not None:
                out[:TILE, column] = (normed[:TILE] + head_first[:, column]).astype(BF16)
                out[TILE:CHUNK, column] = (normed[TILE:] + windowed[TILE:CHUNK, column]).astype(BF16)
            else:
                out[here, column] = (normed + windowed[here, column]).astype(BF16)


def finish(start, limits, first_doc, phi_query, bounds, inner, windowed, prefix, states, head_first=None):
    half, columns = inner.shape
    heads = columns // HEAD_DIM
    group = min(GROUP, heads)
    chunks = half // CHUNK

    def some(count, width):
        return pl.BlockSpec((count, group * width), lambda g, *_: (0, g))

    specs = [
        pl.BlockSpec(first_doc.shape, lambda g, *_: (0, 0)),
        some(half, WIDE), pl.BlockSpec(bounds.shape, lambda g, *_: (0, 0)),
        some(half, HEAD_DIM), some(half, HEAD_DIM),
        pl.BlockSpec((chunks, group, STATE, HEAD_DIM), lambda g, *_: (start // chunks, g, 0, 0)),
    ]
    specs += [pl.BlockSpec((group, STATE, HEAD_DIM), lambda g, *_: (g, 0, 0))] * len(states)
    args = [first_doc, phi_query, bounds, inner, windowed, prefix, *states]
    if head_first is not None:
        specs.append(some(TILE, HEAD_DIM))
        args.append(head_first)
    return pl.pallas_call(
        functools.partial(finish_kernel, start, len(states)),
        grid_spec=pltpu.PrefetchScalarGridSpec(
            num_scalar_prefetch=1,
            grid=(heads // group,),
            in_specs=specs,
            out_specs=some(half, HEAD_DIM),
        ),
        out_shape=jax.ShapeDtypeStruct((half, columns), BF16),
        compiler_params=params(),
    )(limits, *args)


def after(x, *others):
    return lax.optimization_barrier((x, *others))[0]


def shards(tokens, doc_ids, w_feat, w_value, w_window, w_out):
    rows = tokens.shape[0]
    half = rows // 2
    chunks = rows // CHUNK
    heads = w_value.shape[1] // HEAD_DIM
    count = lax.axis_size("head") // 2
    blocks = lax.axis_size("ctx")
    me = lax.axis_index("head")
    z, c = me // 2, me % 2
    place = jnp.stack([z, c]).astype(jnp.int32)

    def hop(x, step, sources):
        return lax.ppermute(x, "head", line(count, step, sources))

    def near(x):
        return hop(x, 1, range(count)), hop(x, -1, range(count))

    def far(x):
        return hop(x, count - 1, [0]), hop(x, 1 - count, [count - 1])

    def chain(up, down):
        ups, downs = [up], [down]
        for s in range(2, count - 1):
            ups.append(hop(ups[-1], 1, range(s - 1, count)))
            downs.append(hop(downs[-1], -1, range(0, count - s + 1)))
        return ups, downs

    def early_pieces(x, up, down, far_up, far_down):
        mine = jnp.concatenate([x, down + far_up, far_down + up], 1)
        return mine, swap(mine, count)

    def late_pieces(ups, downs):
        mine = jnp.concatenate(
            [downs[s - 1] + ups[count - s - 1] for s in range(2, count - 1)], 1
        )
        return mine, swap(mine, count)

    high, low = tokens[half:], tokens[:half]
    high_near = near(high)
    high_far = far(high)

    docs = doc_ids.astype(F32)
    ends = jnp.concatenate([docs[CHUNK::CHUNK], docs[rows - 1 :]])
    limits = jnp.sum((docs[None, :] < ends[:, None]).astype(F32), 1).astype(jnp.int32)
    limits = jnp.concatenate([limits, doc_ids[rows - 1 :]])
    first = jnp.sum((docs[None, :] < docs[:, None]).astype(F32), 1, keepdims=True)
    bounds = first.astype(jnp.int32)
    first_doc = jnp.broadcast_to(docs[:1], (8, HEAD_DIM))
    tail_docs = jnp.broadcast_to((docs[rows - WIN :] + 1.0).astype(BF16)[:, None], (WIN, HEAD_DIM))

    maps, scale_rows = expansions(heads)
    query_map, key_map = jnp.asarray(maps[0]), jnp.asarray(maps[1])
    scale_rows = jnp.asarray(scale_rows)
    pick = jnp.asarray(picks(heads))

    depth, columns = w_out.shape
    width = columns // (2 * count)

    def cut(rows_out, chip, core):
        return lax.dynamic_slice(rows_out, (0, (2 * chip + core) * width), (depth, width))

    ready = lax.optimization_barrier((*high_near, *high_far, limits, bounds, first_doc, tail_docs))
    high_near, high_far = ready[:2], ready[2:4]
    limits, bounds, first_doc, tail_docs = ready[4:]
    rows_out = after(w_out, *high_near)
    other_rows = jnp.stack([cut(rows_out, chip, 1 - c) for chip in range(count)])

    fv_weights = (w_value, w_feat)
    high_ups, high_downs = chain(*high_near)
    low_far = far(after(low, *high_near))
    *pieces, other_rows = lax.optimization_barrier((*high_near, *high_far, other_rows))
    high_early = early_pieces(high, *pieces)
    other_rows = swap(other_rows, count)
    high_ups[-1], high_downs[-1] = lax.optimization_barrier(
        (high_ups[-1], high_downs[-1], *high_early)
    )[:2]
    low_near = near(after(low, high_ups[-1], high_downs[-1]))
    high_late = late_pieces(high_ups, high_downs)
    value_high, feat_high, win_high = project(place, high_early, high_late, fv_weights + (w_window,))

    group = min(GROUP, heads)
    parts = []
    for g in range(0, heads, group):
        parts.append(win_high[half - WIN :, 2 * g * HEAD_DIM : 2 * (g + group) * HEAD_DIM])
        parts.append(value_high[half - WIN :, g * HEAD_DIM : (g + group) * HEAD_DIM])
    tail = lax.ppermute(
        jnp.concatenate(parts + [tail_docs], 1), "ctx", [(i, i + 1) for i in range(blocks - 1)]
    )
    high_sums = sums(limits, feat_high, value_high, key_map, scale_rows)
    inner_high, windowed_high, phi_high = local(
        False, feat_high, value_high, win_high, bounds, pick, query_map, scale_rows
    )

    *low_near, far_up, far_down, tail, other_rows = lax.optimization_barrier(
        (*low_near, *low_far, tail, other_rows, inner_high, high_sums)
    )[:6]
    low_ups, low_downs = chain(*low_near)
    rows_out = after(w_out, *low_near)

    def out_for(chip):
        chip = jnp.clip(chip, 0, count - 1)
        return jnp.concatenate(
            [cut(rows_out, chip, c), lax.dynamic_index_in_dim(other_rows, chip, 0, keepdims=False)], 0
        )

    out_up = [out_for(z + count - s) for s in range(1, count)]
    out_down = [out_for(z - count + s) for s in range(1, count)]
    *pieces, out_up[0], out_down[0] = lax.optimization_barrier(
        (*low_near, far_up, far_down, out_up[0], out_down[0])
    )
    low_early = early_pieces(low, *pieces)
    ready = lax.optimization_barrier((low_ups[-1], low_downs[-1], out_for(z), *out_up, *out_down))
    low_ups[-1], low_downs[-1], out_here = ready[:3]
    out_up, out_down = ready[3 : 2 + count], ready[2 + count :]
    low_late = late_pieces(low_ups, low_downs)
    value_low, feat_low = project(place, low_early, low_late, fv_weights)
    prefix, state = sums(limits, feat_low, value_low, key_map, scale_rows, high_sums)
    states = [
        lax.ppermute(state, "ctx", [(i, i + k) for i in range(blocks - k)])
        for k in range(1, blocks)
    ]
    (win_low,) = project(place, low_early, (after(low_late[0], state), low_late[1]), (w_window,))
    inner_low, windowed_low, phi_low, windowed_next = local(
        True, feat_low, value_low, win_low, bounds, pick, query_map, scale_rows,
        (tail, tail, first_doc), (value_high, win_high),
    )
    mixed_low = finish(
        0, limits, first_doc, phi_low, bounds, inner_low, windowed_low, prefix, states
    )
    mixed_high = finish(
        chunks // 2, limits, first_doc, phi_high, bounds, inner_high, windowed_high, prefix, states,
        windowed_next,
    )

    outs = []
    for mixed in (mixed_low, mixed_high):
        chip = jnp.concatenate([mixed, swap(mixed, count)], 1)

        def partial(weight, *received):
            total = jnp.dot(chip, weight, preferred_element_type=F32)
            for r in received:
                total += r.astype(F32)
            return total.astype(BF16)

        up, down = (), ()
        for s in range(1, count):
            up = (hop(partial(out_up[s - 1], *up), 1, range(0, s)),)
            down = (hop(partial(out_down[s - 1], *down), -1, range(count - s, count)),)
        outs.append(partial(out_here, *up, *down))
    return jnp.concatenate(outs, 0)


def solution(mesh):
    return jax.shard_map(
        shards,
        mesh=mesh,
        in_specs=(
            P("ctx", "head"),
            P("ctx"),
            P(None, "head"),
            P(None, "head"),
            P(None, "head"),
            P("head", None),
        ),
        out_specs=P("ctx", "head"),
        check_vma=False,
    )
```

```python
import functools

import jax
import jax.numpy as jnp
import numpy as np
from jax import lax
from jax.experimental import pallas as pl
from jax.experimental.pallas import tpu as pltpu
from jax.sharding import PartitionSpec as P

HEAD_DIM = 128
FEAT = 16
WIN = 64
PAIRS = [(i, j) for i in range(FEAT) for j in range(i, FEAT)]
WIDE = 256
CHUNK = 256
GROUP = 2
STATE = -(-(len(PAIRS) + FEAT + 1) // 16) * 16
VMEM = 40 * 1024 * 1024
TILE = 128
LANES = 128
F32 = jnp.float32
BF16 = jnp.bfloat16


def params():
    return pltpu.CompilerParams(vmem_limit_bytes=VMEM, dimension_semantics=("arbitrary",))


def line(count, step, sources):
    return [(2 * z + c, 2 * (z + step) + c) for z in sources for c in (0, 1) if 0 <= z + step < count]


def swap(x, count):
    return lax.ppermute(x, "head", [(h, h ^ 1) for h in range(2 * count)])


def project_kernel(chips, has_before, place, mine, theirs, *refs):
    weights, out, both = refs[:chips], refs[-2], refs[-1]
    width = mine.shape[1] // chips
    c = place[1]

    @pl.when(pl.program_id(0) == 0)
    def _():
        for n in range(chips):
            piece = slice(n * width, (n + 1) * width)
            own = pl.multiple_of((2 * n + c) * width, width)
            other = pl.multiple_of((2 * n + 1 - c) * width, width)
            both[:, pl.ds(own, width)] = mine[:, piece]
            both[:, pl.ds(other, width)] = theirs[:, piece]

    total = refs[chips][...] if has_before else None
    for n in range(chips):
        rows = both[:, 2 * n * width : 2 * (n + 1) * width]
        part = jnp.dot(rows, weights[n][...], preferred_element_type=F32)
        total = part if total is None else total + part
    out[...] = total.astype(out.dtype)


def project(place, chips, mine, theirs, weight, first, columns, before=None, dtype=F32):
    rows = mine.shape[0]
    width = mine.shape[1] // len(chips)
    count = weight.shape[0] // (2 * width)
    tile = 256
    start = first // tile
    whole = pl.BlockSpec(mine.shape, lambda j, p: (0, 0))
    specs = [whole, whole]
    for n in chips:
        specs.append(
            pl.BlockSpec(
                (2 * width, tile), lambda j, p, n=n: (lax.rem(p[0] + n, count), start + j)
            )
        )
    args = [mine, theirs] + [weight] * len(chips)
    if before is not None:
        specs.append(pl.BlockSpec((rows, tile), lambda j, p: (0, start + j)))
        args.append(before)
    return pl.pallas_call(
        functools.partial(project_kernel, len(chips), before is not None),
        grid_spec=pltpu.PrefetchScalarGridSpec(
            num_scalar_prefetch=1,
            grid=(columns // tile,),
            in_specs=specs,
            out_specs=pl.BlockSpec((rows, tile), lambda j, p: (0, j)),
            scratch_shapes=[pltpu.VMEM((rows, 2 * mine.shape[1]), BF16)],
        ),
        out_shape=jax.ShapeDtypeStruct((rows, columns), dtype),
        compiler_params=params(),
    )(place, *args)


def expansions(heads):
    lanes = -(-heads * 2 * FEAT // LANES) * LANES
    maps = np.zeros((2, heads, lanes, 2 * WIDE), np.float32)
    rows = np.zeros((3, WIDE), np.float32)
    for h in range(heads):
        for side in (0, 1):
            base = h * 2 * FEAT + side * FEAT
            for n, (i, j) in enumerate(PAIRS):
                maps[side, h, base + i, n] = 1.0
                maps[side, h, base + j, WIDE + n] = 1.0
            for i in range(FEAT):
                maps[side, h, base + i, len(PAIRS) + i] = 1.0
    for n, (i, j) in enumerate(PAIRS):
        rows[2, n] = (2.0 * FEAT) ** -0.5 * (1.0 if i == j else 2.0**0.5)
    rows[1, len(PAIRS) : len(PAIRS) + FEAT + 1] = 1.0
    rows[0, len(PAIRS) + FEAT] = 1.0
    rows[2, len(PAIRS) : len(PAIRS) + FEAT] = FEAT**-0.25
    rows[2, len(PAIRS) + FEAT] = 1.0
    return maps.astype(jnp.bfloat16), rows


def picks(heads):
    lanes = -(-heads * 2 * FEAT // LANES) * LANES
    maps = np.zeros((heads, lanes, 256), np.float32)
    for h in range(heads):
        for i in range(FEAT):
            maps[h, h * 2 * FEAT + i, i] = 1.0
            maps[h, h * 2 * FEAT + FEAT + i, 128 + i] = 1.0
    return maps.astype(jnp.bfloat16)


def phi(features, expand, rows):
    factors = jnp.dot(features, expand, preferred_element_type=F32)
    left = factors[:, :WIDE] + rows[0:1]
    right = factors[:, WIDE:] + rows[1:2]
    return (left * right * rows[2:3]).astype(BF16)


def sums_kernel(limits, values, features, expand, rows, prefix, end):
    chunks, heads = prefix.shape[:2]
    mark = lax.broadcasted_iota(jnp.int32, (STATE, HEAD_DIM), 0) == STATE - 1
    at = lax.broadcasted_iota(jnp.int32, (CHUNK, HEAD_DIM), 0)
    for h in range(heads):
        column = slice(h * HEAD_DIM, (h + 1) * HEAD_DIM)
        phi_key = phi(features[...], expand[h], rows[...])
        parts = []
        for n in range(chunks):
            here = slice(n * CHUNK, (n + 1) * CHUNK)
            kept = jnp.where(at + n * CHUNK >= limits[n], values[here, column].astype(F32), 0.0)
            parts.append(
                lax.dot_general(
                    phi_key[here], kept.astype(BF16), (((0,), (0,)), ((), ())),
                    preferred_element_type=F32,
                )[:STATE]
            )
        state = jnp.zeros((STATE, HEAD_DIM), F32)
        for n in range(chunks):
            prefix[n, h] = state
            state = parts[n] + jnp.where(limits[n] <= n * CHUNK, state, 0.0)
        end[h] = jnp.where(mark, (limits[chunks] + 1).astype(F32), state).astype(BF16)


def sums(limits, both, heads, expand, rows):
    chunks = both.shape[0] // CHUNK
    group = min(GROUP, heads)
    count = both.shape[0]
    return pl.pallas_call(
        sums_kernel,
        grid_spec=pltpu.PrefetchScalarGridSpec(
            num_scalar_prefetch=1,
            grid=(heads // group,),
            in_specs=[
                pl.BlockSpec((count, group * HEAD_DIM), lambda g, _: (0, g)),
                pl.BlockSpec((count, LANES), lambda g, _: (0, heads)),
                pl.BlockSpec((group,) + expand.shape[1:], lambda g, _: (g, 0, 0)),
                pl.BlockSpec(rows.shape, lambda g, _: (0, 0)),
            ],
            out_specs=[
                pl.BlockSpec((chunks, group, STATE, HEAD_DIM), lambda g, _: (0, g, 0, 0)),
                pl.BlockSpec((group, STATE, HEAD_DIM), lambda g, _: (g, 0, 0)),
            ],
        ),
        out_shape=[
            jax.ShapeDtypeStruct((chunks, heads, STATE, HEAD_DIM), F32),
            jax.ShapeDtypeStruct((heads, STATE, HEAD_DIM), BF16),
        ],
        compiler_params=params(),
    )(limits, both, both, expand, rows)


def windows(tiles):
    wide = TILE + WIN
    logits = jnp.concatenate(
        [
            lax.dot_general(q, k, (((1,), (1,)), ((), ())), preferred_element_type=F32)
            for q, k, _, _, _ in tiles
        ],
        0,
    )
    at = lax.broadcasted_iota(jnp.int32, (TILE, wide), 1)
    row = lax.broadcasted_iota(jnp.int32, (TILE, wide), 0)
    near = (at <= row + WIN) & (at > row)
    good = jnp.concatenate([near & (at >= first - start) for _, _, _, first, start in tiles], 0)
    logits = jnp.where(good, logits * HEAD_DIM**-0.5, -1e30)
    top = jnp.max(logits, 1, keepdims=True)
    weight = jnp.where(good, jnp.exp(logits - top), 0.0)
    probs = (weight / jnp.sum(weight, 1, keepdims=True)).astype(BF16)
    return [
        jnp.dot(probs[n * TILE : (n + 1) * TILE], tile[2], preferred_element_type=F32)
        for n, tile in enumerate(tiles)
    ]


def local_kernel(part, features, values, window, old_values, old_window, bounds, pick, expand, rows, *refs):
    inner, windowed, phi_query = refs[-3:]
    half = features.shape[0]
    base = part * half
    chunks = half // CHUNK
    if part == 0:
        tail_docs, first_doc = refs[:2]
        same = jnp.where(tail_docs[...].astype(F32) == first_doc[0:1, :] + 1.0, 1.0, 0.0)
        in_tail = jnp.sum(same, 0, keepdims=True)[:, 0:1].astype(jnp.int32)
    at = lax.broadcasted_iota(jnp.int32, (CHUNK, CHUNK), 1)
    row = lax.broadcasted_iota(jnp.int32, (CHUNK, CHUNK), 0)
    good = jnp.concatenate(
        [
            (at <= row) & (at >= bounds[n * CHUNK : (n + 1) * CHUNK] - (base + n * CHUNK))
            for n in range(chunks)
        ],
        0,
    )
    for h in range(values.shape[1] // HEAD_DIM):
        column = slice(h * HEAD_DIM, (h + 1) * HEAD_DIM)
        query = slice(2 * h * HEAD_DIM, (2 * h + 1) * HEAD_DIM)
        key = slice((2 * h + 1) * HEAD_DIM, (2 * h + 2) * HEAD_DIM)
        both = jnp.dot(features[...], pick[h], preferred_element_type=F32).astype(BF16)
        dots = jnp.concatenate(
            [
                lax.dot_general(
                    both[n * CHUNK : (n + 1) * CHUNK, :128], both[n * CHUNK : (n + 1) * CHUNK, 128:],
                    (((1,), (1,)), ((), ())), preferred_element_type=F32,
                )
                for n in range(chunks)
            ],
            0,
        )
        tiles = []
        for n in range(half // TILE):
            near = slice(n * TILE - WIN, (n + 1) * TILE)
            first = bounds[n * TILE : (n + 1) * TILE]
            if n:
                keys, vals = window[near, key], values[near, column]
            else:
                keys = jnp.concatenate([old_window[:, key], window[:TILE, key]], 0)
                vals = jnp.concatenate([old_values[:, column], values[:TILE, column]], 0)
                if part == 0:
                    first = jnp.where(first == 0, -in_tail, first)
            tiles.append(
                (window[n * TILE : (n + 1) * TILE, query], keys, vals, first, base + n * TILE - WIN)
            )
        results = windows(tiles)
        score = dots * (dots * (0.5 / FEAT) + FEAT**-0.5) + 1.0
        score = jnp.where(good, score, 0.0).astype(BF16)
        phi_query[:, h * WIDE : (h + 1) * WIDE] = phi(features[...], expand[h], rows[...])
        for n in range(chunks):
            here = slice(n * CHUNK, (n + 1) * CHUNK)
            inner[here, column] = jnp.dot(
                score[here], values[here, column], preferred_element_type=F32
            )
        for n, result in enumerate(results):
            windowed[n * TILE : (n + 1) * TILE, column] = result


def local(part, both, window, bounds, pick, expand, rows, heads, old=None, docs=()):
    half = both.shape[0] // 2
    group = min(GROUP, heads)

    def full(a):
        return pl.BlockSpec(a.shape, lambda g: (0,) * a.ndim)

    def some(count, width, at=0):
        return pl.BlockSpec((count, group * width), lambda g: (at, g))

    def per_head(a):
        return pl.BlockSpec((group,) + a.shape[1:], lambda g: (g, 0, 0))

    at = half // WIN - 1 if old is None else 0
    return pl.pallas_call(
        functools.partial(local_kernel, part),
        grid=(heads // group,),
        in_specs=[
            pl.BlockSpec((half, LANES), lambda g: (part, heads)),
            some(half, HEAD_DIM, part), some(half, 2 * HEAD_DIM, part),
            some(WIN, HEAD_DIM, at), some(WIN, 2 * HEAD_DIM, at),
            pl.BlockSpec((half, 1), lambda g: (part, 0)),
            per_head(pick), per_head(expand), full(rows),
        ]
        + [full(a) for a in docs],
        out_specs=[some(half, HEAD_DIM), some(half, HEAD_DIM), some(half, WIDE)],
        out_shape=[
            jax.ShapeDtypeStruct((half, heads * HEAD_DIM), F32),
            jax.ShapeDtypeStruct((half, heads * HEAD_DIM), F32),
            jax.ShapeDtypeStruct((half, heads * WIDE), BF16),
        ],
        compiler_params=params(),
    )(both, both, window, *(old or (both, window)), bounds, pick, expand, rows, *docs)


def finish_kernel(part, shifts, limits, first_doc, phi_query, bounds, inner, windowed, prefix, *refs):
    states, out = refs[:shifts], refs[-1]
    unmarked = lax.broadcasted_iota(jnp.int32, (STATE, HEAD_DIM), 0) < STATE - 1
    chunks = inner.shape[0] // CHUNK
    for h in range(inner.shape[1] // HEAD_DIM):
        column = slice(h * HEAD_DIM, (h + 1) * HEAD_DIM)
        incoming = jnp.zeros((STATE, HEAD_DIM), F32)
        for k in range(shifts):
            sent = states[k][h].astype(F32)
            wanted = (sent[STATE - 1 :] == first_doc[0:1, :] + 1.0) & unmarked
            incoming += jnp.where(wanted, sent, 0.0)
        carried = []
        for n in range(chunks):
            chunk = part * chunks + n
            state = incoming
            if chunk:
                state = jnp.where(limits[chunk - 1] <= 0, incoming, 0.0) + prefix[n, h]
            state = jnp.concatenate([state, jnp.zeros((WIDE - STATE, HEAD_DIM), F32)], 0)
            here = slice(n * CHUNK, (n + 1) * CHUNK)
            one = jnp.dot(
                phi_query[here, h * WIDE : (h + 1) * WIDE], state.astype(BF16),
                preferred_element_type=F32,
            )
            carried.append(jnp.where(bounds[here] <= chunk * CHUNK, one, 0.0))
        linear = inner[:, column] + jnp.concatenate(carried, 0)
        mean = jnp.mean(linear * linear, 1, keepdims=True)
        out[:, column] = (linear * lax.rsqrt(mean + 1e-5) + windowed[:, column]).astype(BF16)


def finish(part, limits, first_doc, bounds, prefix, parts, states):
    inner, windowed, phi_query = parts
    half, columns = inner.shape
    heads = columns // HEAD_DIM
    group = min(GROUP, heads)

    def some(count, width):
        return pl.BlockSpec((count, group * width), lambda g, *_: (0, g))

    return pl.pallas_call(
        functools.partial(finish_kernel, part, len(states)),
        grid_spec=pltpu.PrefetchScalarGridSpec(
            num_scalar_prefetch=1,
            grid=(heads // group,),
            in_specs=[
                pl.BlockSpec(first_doc.shape, lambda g, *_: (0, 0)),
                some(half, WIDE), pl.BlockSpec((half, 1), lambda g, *_: (part, 0)),
                some(half, HEAD_DIM), some(half, HEAD_DIM),
                pl.BlockSpec(
                    (prefix.shape[0] // 2, group, STATE, HEAD_DIM), lambda g, *_: (part, g, 0, 0)
                ),
            ]
            + [pl.BlockSpec((group, STATE, HEAD_DIM), lambda g, *_: (g, 0, 0))] * len(states),
            out_specs=some(half, HEAD_DIM),
        ),
        out_shape=jax.ShapeDtypeStruct((half, columns), BF16),
        compiler_params=params(),
    )(limits, first_doc, phi_query, bounds, inner, windowed, prefix, *states)


def after(x, *others):
    return lax.optimization_barrier((x, *others))[0]


def shards(tokens, doc_ids, w_feat, w_value, w_window, w_out):
    rows = tokens.shape[0]
    chunks = rows // CHUNK
    value_columns = w_value.shape[1]
    heads = value_columns // HEAD_DIM
    count = lax.axis_size("head") // 2
    blocks = lax.axis_size("ctx")
    me = lax.axis_index("head")
    z, c = me // 2, me % 2
    place = jnp.stack([z, c]).astype(jnp.int32)

    def hop(x, step, sources):
        return lax.ppermute(x, "head", line(count, step, sources))

    up, down = hop(tokens, 1, range(count)), hop(tokens, -1, range(count))
    far_up, far_down = hop(tokens, count - 1, [0]), hop(tokens, 1 - count, [count - 1])
    tokens_there = swap(tokens, count)

    docs = doc_ids.astype(F32)
    ends = jnp.concatenate([docs[CHUNK::CHUNK], docs[rows - 1 :]])
    limits = jnp.sum((docs[None, :] < ends[:, None]).astype(F32), 1).astype(jnp.int32)
    limits = jnp.concatenate([limits, doc_ids[rows - 1 :]])
    first = jnp.sum((docs[None, :] < docs[:, None]).astype(F32), 1, keepdims=True)
    bounds = first.astype(jnp.int32)
    first_doc = jnp.broadcast_to(docs[:1], (8, HEAD_DIM))
    tail_docs = jnp.broadcast_to((docs[rows - WIN :] + 1.0).astype(BF16)[:, None], (WIN, HEAD_DIM))
    onward = [(i, i + 1) for i in range(blocks - 1)]
    tail_docs = lax.ppermute(tail_docs, "ctx", onward)

    maps, scale_rows = expansions(heads)
    query_map, key_map = jnp.asarray(maps[0]), jnp.asarray(maps[1])
    scale_rows = jnp.asarray(scale_rows)
    pick = jnp.asarray(picks(heads))

    depth, columns = w_out.shape
    width = columns // (2 * count)

    def cut(chip, core):
        return lax.dynamic_slice(w_out, (0, (2 * chip + core) * width), (depth, width))

    other_rows = swap(jnp.stack([cut(chip, 1 - c) for chip in range(count)]), count)

    def out_for(chip):
        chip = jnp.clip(chip, 0, count - 1)
        return jnp.concatenate(
            [cut(chip, c), lax.dynamic_index_in_dim(other_rows, chip, 0, keepdims=False)], 0
        )

    out_up = [out_for(z + count - s) for s in range(1, count)]
    out_down = [out_for(z - count + s) for s in range(1, count)]
    out_here = out_for(z)

    used = value_columns + w_feat.shape[1]
    fv_columns = -(-used // 256) * 256
    weight = jnp.concatenate(
        [w_value, w_feat, jnp.zeros((w_value.shape[0], fv_columns - used), BF16), w_window], 1
    )
    all_columns = weight.shape[1]
    part = project(place, (0,), tokens, tokens_there, weight, 0, all_columns)

    ready = lax.optimization_barrier(
        (up, down, far_up, far_down, limits, bounds, first_doc, tail_docs, part, out_here, *out_up, *out_down)
    )
    up, down, far_up, far_down, limits, bounds, first_doc, tail_docs, part, out_here = ready[:10]
    out_up, out_down = ready[10 : 9 + count], ready[9 + count :]

    ups, downs = [up], [down]
    for s in range(2, count - 1):
        ups.append(hop(ups[-1], 1, range(s - 1, count)))
        downs.append(hop(downs[-1], -1, range(0, count - s + 1)))
    mine = jnp.concatenate([down + far_up, far_down + up], 1)
    part = project(
        place, (1, count - 1), mine, swap(mine, count), weight, 0, all_columns, part
    )
    ups[-1], downs[-1], part = lax.optimization_barrier((ups[-1], downs[-1], part))
    mine = jnp.concatenate([downs[s - 1] + ups[count - s - 1] for s in range(2, count - 1)], 1)
    late = tuple(range(2, count - 1))
    theirs = swap(mine, count)
    both = project(place, late, mine, theirs, weight, 0, fv_columns, part, BF16)
    prefix, state = sums(limits, both, heads, key_map, scale_rows)
    states = [
        lax.ppermute(state, "ctx", [(i, i + k) for i in range(blocks - k)])
        for k in range(1, blocks)
    ]
    window = project(
        place, late, after(mine, state), theirs, weight, fv_columns, all_columns - fv_columns, part,
        BF16,
    )
    local_high = local(1, both, window, bounds, pick, query_map, scale_rows, heads)
    tail = [
        lax.ppermute(a, "ctx", onward)
        for a in (after(both, window)[rows - WIN :, :value_columns], window[rows - WIN :])
    ]
    high = finish(1, limits, first_doc, bounds, prefix, local_high, states)
    def partial(chip, weight, *received):
        total = jnp.dot(chip, weight, preferred_element_type=F32)
        for r in received:
            total += r.astype(F32)
        return total.astype(BF16)

    def first_parts(mixed):
        chip = jnp.concatenate([mixed, swap(mixed, count)], 1)
        return chip, partial(chip, out_up[0]), partial(chip, out_down[0])

    def scattered(chip, up, down):
        for s in range(1, count):
            if s > 1:
                up, down = partial(chip, out_up[s - 1], up), partial(chip, out_down[s - 1], down)
            up = hop(up, 1, range(0, s))
            down = hop(down, -1, range(count - s, count))
        return partial(chip, out_here, up, down)

    high_parts = first_parts(high)
    local_low = local(
        0, after(both, *high_parts[1:]), window, bounds, pick, query_map, scale_rows, heads, tail,
        (tail_docs, first_doc),
    )
    low = finish(0, limits, first_doc, bounds, prefix, local_low, states)

    high_out = scattered(*high_parts)
    low_out = scattered(*first_parts(low))
    return jnp.concatenate([low_out, high_out], 0)


def solution(mesh):
    return jax.shard_map(
        shards,
        mesh=mesh,
        in_specs=(
            P("ctx", "head"),
            P("ctx"),
            P(None, "head"),
            P(None, "head"),
            P(None, "head"),
            P("head", None),
        ),
        out_specs=P("ctx", "head"),
        check_vma=False,
    )
```

```python
import functools

import jax
import jax.numpy as jnp
import numpy as np
from jax import lax
from jax.experimental import pallas as pl
from jax.experimental.pallas import tpu as pltpu
from jax.sharding import PartitionSpec as P

HEAD_DIM = 128
FEAT = 16
WIN = 64
PAIRS = [(i, j) for i in range(FEAT) for j in range(i, FEAT)]
WIDE = 256
CHUNK = 256
GROUP = 2
STATE = -(-(len(PAIRS) + FEAT + 1) // 16) * 16
VMEM = 40 * 1024 * 1024
TILE = 128
LANES = 128
F32 = jnp.float32
BF16 = jnp.bfloat16


def params(limit=VMEM):
    return pltpu.CompilerParams(vmem_limit_bytes=limit, dimension_semantics=("arbitrary",))


def ring(x, step, count):
    return lax.ppermute(
        x, "head", [(2 * z + c, 2 * ((z + step) % count) + c) for z in range(count) for c in (0, 1)]
    )


def swap(x, count):
    return lax.ppermute(x, "head", [(h, h ^ 1) for h in range(2 * count)])


def project_kernel(chips, has_before, place, *refs):
    mine, theirs, weights = refs[:chips], refs[chips : 2 * chips], refs[2 * chips : 3 * chips]
    out, both = refs[-2], refs[-1]
    width = mine[0].shape[1]
    c = place[1]

    @pl.when(pl.program_id(0) == 0)
    def _():
        for n in range(chips):
            own = pl.multiple_of((2 * n + c) * width, width)
            other = pl.multiple_of((2 * n + 1 - c) * width, width)
            both[:, pl.ds(own, width)] = mine[n][...]
            both[:, pl.ds(other, width)] = theirs[n][...]

    total = refs[3 * chips][...] if has_before else None
    for n in range(chips):
        rows = both[:, 2 * n * width : 2 * (n + 1) * width]
        part = jnp.dot(rows, weights[n][...], preferred_element_type=F32)
        total = part if total is None else total + part
    out[...] = total.astype(out.dtype)


def project(place, chips, mine, theirs, weight, first, columns, before=None, dtype=F32):
    rows, width = mine[0].shape
    count = weight.shape[0] // (2 * width)
    tile = 256
    start = first // tile
    specs = [pl.BlockSpec((rows, width), lambda j, p: (0, 0))] * (2 * len(chips))
    for n in chips:
        specs.append(
            pl.BlockSpec(
                (2 * width, tile), lambda j, p, n=n: (lax.rem(p[0] + n, count), start + j)
            )
        )
    args = [*mine, *theirs] + [weight] * len(chips)
    if before is not None:
        specs.append(pl.BlockSpec((rows, tile), lambda j, p: (0, start + j)))
        args.append(before)
    return pl.pallas_call(
        functools.partial(project_kernel, len(chips), before is not None),
        grid_spec=pltpu.PrefetchScalarGridSpec(
            num_scalar_prefetch=1,
            grid=(columns // tile,),
            in_specs=specs,
            out_specs=pl.BlockSpec((rows, tile), lambda j, p: (0, j)),
            scratch_shapes=[pltpu.VMEM((rows, 2 * width * len(chips)), BF16)],
        ),
        out_shape=jax.ShapeDtypeStruct((rows, columns), dtype),
        compiler_params=params(60 * 1024 * 1024),
    )(place, *args)


def expansions(heads):
    lanes = -(-heads * 2 * FEAT // LANES) * LANES
    maps = np.zeros((2, heads, lanes, 2 * WIDE), np.float32)
    rows = np.zeros((3, WIDE), np.float32)
    for h in range(heads):
        for side in (0, 1):
            base = h * 2 * FEAT + side * FEAT
            for n, (i, j) in enumerate(PAIRS):
                maps[side, h, base + i, n] = 1.0
                maps[side, h, base + j, WIDE + n] = 1.0
            for i in range(FEAT):
                maps[side, h, base + i, len(PAIRS) + i] = 1.0
    for n, (i, j) in enumerate(PAIRS):
        rows[2, n] = (2.0 * FEAT) ** -0.5 * (1.0 if i == j else 2.0**0.5)
    rows[1, len(PAIRS) : len(PAIRS) + FEAT + 1] = 1.0
    rows[0, len(PAIRS) + FEAT] = 1.0
    rows[2, len(PAIRS) : len(PAIRS) + FEAT] = FEAT**-0.25
    rows[2, len(PAIRS) + FEAT] = 1.0
    return maps.astype(jnp.bfloat16), rows


def picks(heads):
    lanes = -(-heads * 2 * FEAT // LANES) * LANES
    maps = np.zeros((heads, lanes, 256), np.float32)
    for h in range(heads):
        for i in range(FEAT):
            maps[h, h * 2 * FEAT + i, i] = 1.0
            maps[h, h * 2 * FEAT + FEAT + i, 128 + i] = 1.0
    return maps.astype(jnp.bfloat16)


def phi(features, expand, rows):
    factors = jnp.dot(features, expand, preferred_element_type=F32)
    left = factors[:, :WIDE] + rows[0:1]
    right = factors[:, WIDE:] + rows[1:2]
    return (left * right * rows[2:3]).astype(BF16)


def sums_kernel(limits, values, features, expand, rows, prefix, end):
    chunks, heads = prefix.shape[:2]
    mark = lax.broadcasted_iota(jnp.int32, (STATE, HEAD_DIM), 0) == STATE - 1
    at = lax.broadcasted_iota(jnp.int32, (CHUNK, HEAD_DIM), 0)
    for h in range(heads):
        column = slice(h * HEAD_DIM, (h + 1) * HEAD_DIM)
        phi_key = phi(features[...], expand[h], rows[...])
        parts = []
        for n in range(chunks):
            here = slice(n * CHUNK, (n + 1) * CHUNK)
            kept = jnp.where(at + n * CHUNK >= limits[n], values[here, column].astype(F32), 0.0)
            parts.append(
                lax.dot_general(
                    phi_key[here], kept.astype(BF16), (((0,), (0,)), ((), ())),
                    preferred_element_type=F32,
                )[:STATE]
            )
        state = jnp.zeros((STATE, HEAD_DIM), F32)
        for n in range(chunks):
            prefix[n, h] = state
            state = parts[n] + jnp.where(limits[n] <= n * CHUNK, state, 0.0)
        end[h] = jnp.where(mark, (limits[chunks] + 1).astype(F32), state).astype(BF16)


def sums(limits, both, heads, expand, rows):
    chunks = both.shape[0] // CHUNK
    group = min(GROUP, heads)
    count = both.shape[0]
    return pl.pallas_call(
        sums_kernel,
        grid_spec=pltpu.PrefetchScalarGridSpec(
            num_scalar_prefetch=1,
            grid=(heads // group,),
            in_specs=[
                pl.BlockSpec((count, group * HEAD_DIM), lambda g, _: (0, g)),
                pl.BlockSpec((count, LANES), lambda g, _: (0, heads)),
                pl.BlockSpec((group,) + expand.shape[1:], lambda g, _: (g, 0, 0)),
                pl.BlockSpec(rows.shape, lambda g, _: (0, 0)),
            ],
            out_specs=[
                pl.BlockSpec((chunks, group, STATE, HEAD_DIM), lambda g, _: (0, g, 0, 0)),
                pl.BlockSpec((group, STATE, HEAD_DIM), lambda g, _: (g, 0, 0)),
            ],
        ),
        out_shape=[
            jax.ShapeDtypeStruct((chunks, heads, STATE, HEAD_DIM), F32),
            jax.ShapeDtypeStruct((heads, STATE, HEAD_DIM), BF16),
        ],
        compiler_params=params(),
    )(limits, both, both, expand, rows)


def windows(tiles):
    wide = TILE + WIN
    logits = jnp.concatenate(
        [
            lax.dot_general(q, k, (((1,), (1,)), ((), ())), preferred_element_type=F32)
            for q, k, _, _, _ in tiles
        ],
        0,
    )
    at = lax.broadcasted_iota(jnp.int32, (TILE, wide), 1)
    row = lax.broadcasted_iota(jnp.int32, (TILE, wide), 0)
    near = (at <= row + WIN) & (at > row)
    good = jnp.concatenate([near & (at >= first - start) for _, _, _, first, start in tiles], 0)
    logits = jnp.where(good, logits * HEAD_DIM**-0.5, -1e30)
    top = jnp.max(logits, 1, keepdims=True)
    weight = jnp.where(good, jnp.exp(logits - top), 0.0)
    probs = (weight / jnp.sum(weight, 1, keepdims=True)).astype(BF16)
    return [
        jnp.dot(probs[n * TILE : (n + 1) * TILE], tile[2], preferred_element_type=F32)
        for n, tile in enumerate(tiles)
    ]


def local_kernel(part, features, values, window, old_values, old_window, bounds, pick, expand, rows, *refs):
    inner, windowed, phi_query = refs[-3:]
    half = features.shape[0]
    base = part * half
    chunks = half // CHUNK
    if part == 0:
        tail_docs, first_doc = refs[:2]
        same = jnp.where(tail_docs[...].astype(F32) == first_doc[0:1, :] + 1.0, 1.0, 0.0)
        in_tail = jnp.sum(same, 0, keepdims=True)[:, 0:1].astype(jnp.int32)
    at = lax.broadcasted_iota(jnp.int32, (CHUNK, CHUNK), 1)
    row = lax.broadcasted_iota(jnp.int32, (CHUNK, CHUNK), 0)
    good = jnp.concatenate(
        [
            (at <= row) & (at >= bounds[n * CHUNK : (n + 1) * CHUNK] - (base + n * CHUNK))
            for n in range(chunks)
        ],
        0,
    )
    for h in range(values.shape[1] // HEAD_DIM):
        column = slice(h * HEAD_DIM, (h + 1) * HEAD_DIM)
        query = slice(2 * h * HEAD_DIM, (2 * h + 1) * HEAD_DIM)
        key = slice((2 * h + 1) * HEAD_DIM, (2 * h + 2) * HEAD_DIM)
        both = jnp.dot(features[...], pick[h], preferred_element_type=F32).astype(BF16)
        dots = jnp.concatenate(
            [
                lax.dot_general(
                    both[n * CHUNK : (n + 1) * CHUNK, :128], both[n * CHUNK : (n + 1) * CHUNK, 128:],
                    (((1,), (1,)), ((), ())), preferred_element_type=F32,
                )
                for n in range(chunks)
            ],
            0,
        )
        tiles = []
        for n in range(half // TILE):
            near = slice(n * TILE - WIN, (n + 1) * TILE)
            first = bounds[n * TILE : (n + 1) * TILE]
            if n:
                keys, vals = window[near, key], values[near, column]
            else:
                keys = jnp.concatenate([old_window[:, key], window[:TILE, key]], 0)
                vals = jnp.concatenate([old_values[:, column], values[:TILE, column]], 0)
                if part == 0:
                    first = jnp.where(first == 0, -in_tail, first)
            tiles.append(
                (window[n * TILE : (n + 1) * TILE, query], keys, vals, first, base + n * TILE - WIN)
            )
        results = windows(tiles)
        score = dots * (dots * (0.5 / FEAT) + FEAT**-0.5) + 1.0
        score = jnp.where(good, score, 0.0).astype(BF16)
        phi_query[:, h * WIDE : (h + 1) * WIDE] = phi(features[...], expand[h], rows[...])
        for n in range(chunks):
            here = slice(n * CHUNK, (n + 1) * CHUNK)
            inner[here, column] = jnp.dot(
                score[here], values[here, column], preferred_element_type=F32
            )
        for n, result in enumerate(results):
            windowed[n * TILE : (n + 1) * TILE, column] = result


def local(part, both, window, bounds, pick, expand, rows, heads, old=None, docs=()):
    half = both.shape[0] // 2
    group = min(GROUP, heads)

    def full(a):
        return pl.BlockSpec(a.shape, lambda g: (0,) * a.ndim)

    def some(count, width, at=0):
        return pl.BlockSpec((count, group * width), lambda g: (at, g))

    def per_head(a):
        return pl.BlockSpec((group,) + a.shape[1:], lambda g: (g, 0, 0))

    at = half // WIN - 1 if old is None else 0
    return pl.pallas_call(
        functools.partial(local_kernel, part),
        grid=(heads // group,),
        in_specs=[
            pl.BlockSpec((half, LANES), lambda g: (part, heads)),
            some(half, HEAD_DIM, part), some(half, 2 * HEAD_DIM, part),
            some(WIN, HEAD_DIM, at), some(WIN, 2 * HEAD_DIM, at),
            pl.BlockSpec((half, 1), lambda g: (part, 0)),
            per_head(pick), per_head(expand), full(rows),
        ]
        + [full(a) for a in docs],
        out_specs=[some(half, HEAD_DIM), some(half, HEAD_DIM), some(half, WIDE)],
        out_shape=[
            jax.ShapeDtypeStruct((half, heads * HEAD_DIM), F32),
            jax.ShapeDtypeStruct((half, heads * HEAD_DIM), F32),
            jax.ShapeDtypeStruct((half, heads * WIDE), BF16),
        ],
        compiler_params=params(),
    )(both, both, window, *(old or (both, window)), bounds, pick, expand, rows, *docs)


def finish_kernel(part, shifts, limits, first_doc, phi_query, bounds, inner, windowed, prefix, *refs):
    states, out = refs[:shifts], refs[-1]
    unmarked = lax.broadcasted_iota(jnp.int32, (STATE, HEAD_DIM), 0) < STATE - 1
    chunks = inner.shape[0] // CHUNK
    for h in range(inner.shape[1] // HEAD_DIM):
        column = slice(h * HEAD_DIM, (h + 1) * HEAD_DIM)
        incoming = jnp.zeros((STATE, HEAD_DIM), F32)
        for k in range(shifts):
            sent = states[k][h].astype(F32)
            wanted = (sent[STATE - 1 :] == first_doc[0:1, :] + 1.0) & unmarked
            incoming += jnp.where(wanted, sent, 0.0)
        carried = []
        for n in range(chunks):
            chunk = part * chunks + n
            state = incoming
            if chunk:
                state = jnp.where(limits[chunk - 1] <= 0, incoming, 0.0) + prefix[n, h]
            state = jnp.concatenate([state, jnp.zeros((WIDE - STATE, HEAD_DIM), F32)], 0)
            here = slice(n * CHUNK, (n + 1) * CHUNK)
            one = jnp.dot(
                phi_query[here, h * WIDE : (h + 1) * WIDE], state.astype(BF16),
                preferred_element_type=F32,
            )
            carried.append(jnp.where(bounds[here] <= chunk * CHUNK, one, 0.0))
        linear = inner[:, column] + jnp.concatenate(carried, 0)
        mean = jnp.mean(linear * linear, 1, keepdims=True)
        out[:, column] = (linear * lax.rsqrt(mean + 1e-5) + windowed[:, column]).astype(BF16)


def finish(part, limits, first_doc, bounds, prefix, parts, states):
    inner, windowed, phi_query = parts
    half, columns = inner.shape
    heads = columns // HEAD_DIM
    group = min(GROUP, heads)

    def some(count, width):
        return pl.BlockSpec((count, group * width), lambda g, *_: (0, g))

    return pl.pallas_call(
        functools.partial(finish_kernel, part, len(states)),
        grid_spec=pltpu.PrefetchScalarGridSpec(
            num_scalar_prefetch=1,
            grid=(heads // group,),
            in_specs=[
                pl.BlockSpec(first_doc.shape, lambda g, *_: (0, 0)),
                some(half, WIDE), pl.BlockSpec((half, 1), lambda g, *_: (part, 0)),
                some(half, HEAD_DIM), some(half, HEAD_DIM),
                pl.BlockSpec(
                    (prefix.shape[0] // 2, group, STATE, HEAD_DIM), lambda g, *_: (part, g, 0, 0)
                ),
            ]
            + [pl.BlockSpec((group, STATE, HEAD_DIM), lambda g, *_: (g, 0, 0))] * len(states),
            out_specs=some(half, HEAD_DIM),
        ),
        out_shape=jax.ShapeDtypeStruct((half, columns), BF16),
        compiler_params=params(),
    )(limits, first_doc, phi_query, bounds, inner, windowed, prefix, *states)


def after(x, *others):
    return lax.optimization_barrier((x, *others))[0]


def shards(tokens, doc_ids, w_feat, w_value, w_window, w_out):
    rows = tokens.shape[0]
    chunks = rows // CHUNK
    value_columns = w_value.shape[1]
    heads = value_columns // HEAD_DIM
    count = lax.axis_size("head") // 2
    blocks = lax.axis_size("ctx")
    me = lax.axis_index("head")
    z, c = me // 2, me % 2
    place = jnp.stack([z, c]).astype(jnp.int32)

    pieces = {0: tokens, 1: ring(tokens, -1, count), count - 1: ring(tokens, 1, count)}
    tokens_there = swap(tokens, count)

    docs = doc_ids.astype(F32)
    ends = jnp.concatenate([docs[CHUNK::CHUNK], docs[rows - 1 :]])
    limits = jnp.sum((docs[None, :] < ends[:, None]).astype(F32), 1).astype(jnp.int32)
    limits = jnp.concatenate([limits, doc_ids[rows - 1 :]])
    first = jnp.sum((docs[None, :] < docs[:, None]).astype(F32), 1, keepdims=True)
    bounds = first.astype(jnp.int32)
    first_doc = jnp.broadcast_to(docs[:1], (8, HEAD_DIM))
    tail_docs = jnp.broadcast_to((docs[rows - WIN :] + 1.0).astype(BF16)[:, None], (WIN, HEAD_DIM))
    onward = [(i, i + 1) for i in range(blocks - 1)]
    tail_docs = lax.ppermute(tail_docs, "ctx", onward)

    maps, scale_rows = expansions(heads)
    query_map, key_map = jnp.asarray(maps[0]), jnp.asarray(maps[1])
    scale_rows = jnp.asarray(scale_rows)
    pick = jnp.asarray(picks(heads))

    depth, columns = w_out.shape
    width = columns // (2 * count)

    rows_out = after(w_out, tokens_there)

    def cut(chip, core):
        return lax.dynamic_slice(rows_out, (0, (2 * chip + core) * width), (depth, width))

    other_rows = swap(jnp.stack([cut(chip, 1 - c) for chip in range(count)]), count)
    out_rows = []
    for n in range(count):
        chip = lax.rem(z + n, count)
        theirs = lax.dynamic_index_in_dim(other_rows, chip, 0, keepdims=False)
        out_rows.append(jnp.concatenate([cut(chip, c), theirs], 0))

    used = value_columns + w_feat.shape[1]
    fv_columns = -(-used // 256) * 256
    weight = jnp.concatenate(
        [w_value, w_feat, jnp.zeros((w_value.shape[0], fv_columns - used), BF16), w_window], 1
    )
    all_columns = weight.shape[1]
    part = project(place, (0,), [tokens], [tokens_there], weight, 0, all_columns)

    ready = lax.optimization_barrier(
        (pieces[1], pieces[count - 1], limits, bounds, first_doc, tail_docs, part, *out_rows)
    )
    pieces[1], pieces[count - 1], limits, bounds, first_doc, tail_docs, part = ready[:7]
    out_rows = ready[7:]

    for n in range(2, count // 2 + 1):
        pieces[n] = ring(pieces[n - 1], -1, count)
    for n in range(count - 2, count // 2, -1):
        pieces[n] = ring(pieces[n + 1], 1, count)
    near = (1, count - 1)
    mine = [pieces[n] for n in near]
    part = project(
        place, near, mine, [swap(p, count) for p in mine], weight, 0, all_columns, part
    )
    late = tuple(range(2, count - 1))
    *mine, part = lax.optimization_barrier((*[pieces[n] for n in late], part))
    theirs = [swap(p, count) for p in mine]
    both = project(place, late, mine, theirs, weight, 0, fv_columns, part, BF16)
    prefix, state = sums(limits, both, heads, key_map, scale_rows)
    states = [
        lax.ppermute(state, "ctx", [(i, i + k) for i in range(blocks - k)])
        for k in range(1, blocks)
    ]
    window = project(
        place, late, [after(mine[0], state), *mine[1:]], theirs, weight, fv_columns, all_columns - fv_columns, part,
        BF16,
    )
    local_high = local(1, both, window, bounds, pick, query_map, scale_rows, heads)
    tail = [
        lax.ppermute(a, "ctx", onward)
        for a in (after(both, window)[rows - WIN :, :value_columns], window[rows - WIN :])
    ]
    high = finish(1, limits, first_doc, bounds, prefix, local_high, states)
    def partial(chip, weight, *received):
        total = jnp.dot(chip, weight, preferred_element_type=F32)
        for r in received:
            total += r.astype(F32)
        return total.astype(BF16)

    def first_part(mixed, step):
        chip = jnp.concatenate([mixed, swap(mixed, count)], 1)
        return chip, partial(chip, out_rows[-step % count])

    def scattered(chip, sent, step):
        for n in range(2, count + 1):
            sent = partial(chip, out_rows[-step * n % count], ring(sent, step, count))
        return sent

    high_parts = first_part(high, -1)
    local_low = local(
        0, after(both, high_parts[1]), window, bounds, pick, query_map, scale_rows, heads, tail,
        (tail_docs, first_doc),
    )
    low = finish(0, limits, first_doc, bounds, prefix, local_low, states)
    high_out = scattered(*high_parts, -1)
    low_out = scattered(*first_part(low, 1), 1)
    return jnp.concatenate([low_out, high_out], 0)


def solution(mesh):
    return jax.shard_map(
        shards,
        mesh=mesh,
        in_specs=(
            P("ctx", "head"),
            P("ctx"),
            P(None, "head"),
            P(None, "head"),
            P(None, "head"),
            P("head", None),
        ),
        out_specs=P("ctx", "head"),
        check_vma=False,
    )
```

```python
import functools

import jax
import jax.numpy as jnp
import numpy as np
from jax import lax
from jax.experimental import pallas as pl
from jax.experimental.pallas import tpu as pltpu
from jax.sharding import PartitionSpec as P

HEAD_DIM = 128
FEAT = 16
WIN = 64
PAIRS = [(i, j) for i in range(FEAT) for j in range(i, FEAT)]
WIDE = 256
CHUNK = 256
GROUP = 2
STATE = -(-(len(PAIRS) + FEAT + 1) // 16) * 16
VMEM = 24 * 1024 * 1024
TILE = 128
LANES = 128
F32 = jnp.float32
BF16 = jnp.bfloat16


def params():
    return pltpu.CompilerParams(vmem_limit_bytes=VMEM, dimension_semantics=("arbitrary",))


def ring(x, step, count):
    return lax.ppermute(
        x, "head", [(2 * z + c, 2 * ((z + step) % count) + c) for z in range(count) for c in (0, 1)]
    )


def swap(x, count):
    return lax.ppermute(x, "head", [(h, h ^ 1) for h in range(2 * count)])


def project_kernel(chips, cuts, has_before, tailed, place, *refs):
    mine, theirs, weights = refs[:chips], refs[chips : 2 * chips], refs[2 * chips : 3 * chips]
    before = refs[3 * chips : 3 * chips + len(cuts)] if has_before else None
    outs, both = refs[-1 - len(cuts) - tailed : -1], refs[-1]
    width = mine[0].shape[1]
    c = place[1]
    step = pl.program_id(0)

    @pl.when(step == 0)
    def _():
        for n in range(chips):
            own = pl.multiple_of((2 * n + c) * width, width)
            other = pl.multiple_of((2 * n + 1 - c) * width, width)
            both[:, pl.ds(own, width)] = mine[n][...]
            both[:, pl.ds(other, width)] = theirs[n][...]

    def tile(k):
        total = before[k][...] if has_before else None
        for n in range(chips):
            rows = both[:, 2 * n * width : 2 * (n + 1) * width]
            part = jnp.dot(rows, weights[n][...], preferred_element_type=F32)
            total = part if total is None else total + part
        outs[k][...] = total.astype(outs[k].dtype)
        if tailed:
            outs[-1][...] = total[total.shape[0] - WIN :].astype(outs[-1].dtype)

    if len(cuts) == 1:
        tile(0)
    else:

        @pl.when(step < cuts[0])
        def _():
            tile(0)

        @pl.when(step >= cuts[0])
        def _():
            tile(1)


def project(place, chips, mine, theirs, weight, first, columns, before=None, dtype=F32, tailed=False):
    rows, width = mine[0].shape
    count = weight.shape[0] // (2 * width)
    size = 256
    start = first // size
    cuts = [n // size for n in columns]
    specs = [pl.BlockSpec((rows, width), lambda j, p: (0, 0))] * (2 * len(chips))
    for n in chips:
        specs.append(
            pl.BlockSpec(
                (2 * width, size), lambda j, p, n=n: (lax.rem(p[0] + n, count), start + j)
            )
        )
    results = [
        pl.BlockSpec(
            (rows, size),
            lambda j, p, at=sum(cuts[:k]), n=cuts[k]: (0, jnp.clip(j - at, 0, n - 1)),
        )
        for k in range(len(cuts))
    ]
    args = [*mine, *theirs] + [weight] * len(chips)
    if before is not None:
        specs += results
        args += before
    shapes = [jax.ShapeDtypeStruct((rows, n), dtype) for n in columns]
    if tailed:
        results = results + [pl.BlockSpec((WIN, size), lambda j, p: (0, j))]
        shapes.append(jax.ShapeDtypeStruct((WIN, columns[0]), dtype))
    return pl.pallas_call(
        functools.partial(project_kernel, len(chips), cuts, before is not None, tailed),
        grid_spec=pltpu.PrefetchScalarGridSpec(
            num_scalar_prefetch=1,
            grid=(sum(cuts),),
            in_specs=specs,
            out_specs=results,
            scratch_shapes=[pltpu.VMEM((rows, 2 * width * len(chips)), BF16)],
        ),
        out_shape=shapes,
        compiler_params=params(),
    )(place, *args)


def expansions(heads):
    lanes = -(-heads * 2 * FEAT // LANES) * LANES
    maps = np.zeros((2, heads, lanes, 2 * WIDE), np.float32)
    rows = np.zeros((3, WIDE), np.float32)
    for h in range(heads):
        for side in (0, 1):
            base = h * 2 * FEAT + side * FEAT
            for n, (i, j) in enumerate(PAIRS):
                maps[side, h, base + i, n] = 1.0
                maps[side, h, base + j, WIDE + n] = 1.0
            for i in range(FEAT):
                maps[side, h, base + i, len(PAIRS) + i] = 1.0
    for n, (i, j) in enumerate(PAIRS):
        rows[2, n] = (2.0 * FEAT) ** -0.5 * (1.0 if i == j else 2.0**0.5)
    rows[1, len(PAIRS) : len(PAIRS) + FEAT + 1] = 1.0
    rows[0, len(PAIRS) + FEAT] = 1.0
    rows[2, len(PAIRS) : len(PAIRS) + FEAT] = FEAT**-0.25
    rows[2, len(PAIRS) + FEAT] = 1.0
    return maps.astype(jnp.bfloat16), rows


def picks(heads):
    lanes = -(-heads * 2 * FEAT // LANES) * LANES
    maps = np.zeros((heads, lanes, 256), np.float32)
    for h in range(heads):
        for i in range(FEAT):
            maps[h, h * 2 * FEAT + i, i] = 1.0
            maps[h, h * 2 * FEAT + FEAT + i, 128 + i] = 1.0
    return maps.astype(jnp.bfloat16)


def phi(features, expand, rows):
    factors = jnp.dot(features, expand, preferred_element_type=F32)
    left = factors[:, :WIDE] + rows[0:1]
    right = factors[:, WIDE:] + rows[1:2]
    return (left * right * rows[2:3]).astype(BF16)


def sums_kernel(limits, values, features, expand, rows, prefix, end):
    chunks, heads = prefix.shape[:2]
    mark = lax.broadcasted_iota(jnp.int32, (STATE, HEAD_DIM), 0) == STATE - 1
    at = lax.broadcasted_iota(jnp.int32, (CHUNK, HEAD_DIM), 0)
    for h in range(heads):
        column = slice(h * HEAD_DIM, (h + 1) * HEAD_DIM)
        phi_key = phi(features[...], expand[h], rows[...])
        parts = []
        for n in range(chunks):
            here = slice(n * CHUNK, (n + 1) * CHUNK)
            kept = jnp.where(at + n * CHUNK >= limits[n], values[here, column].astype(F32), 0.0)
            parts.append(
                lax.dot_general(
                    phi_key[here], kept.astype(BF16), (((0,), (0,)), ((), ())),
                    preferred_element_type=F32,
                )[:STATE]
            )
        state = jnp.zeros((STATE, HEAD_DIM), F32)
        for n in range(chunks):
            prefix[n, h] = state
            state = parts[n] + jnp.where(limits[n] <= n * CHUNK, state, 0.0)
        end[h, :STATE] = jnp.where(mark, (limits[chunks] + 1).astype(F32), state).astype(BF16)
        end[h, STATE:] = values[values.shape[0] - WIN :, column]


def sums(limits, both, heads, expand, rows):
    chunks = both.shape[0] // CHUNK
    group = min(GROUP, heads)
    count = both.shape[0]
    return pl.pallas_call(
        sums_kernel,
        grid_spec=pltpu.PrefetchScalarGridSpec(
            num_scalar_prefetch=1,
            grid=(heads // group,),
            in_specs=[
                pl.BlockSpec((count, group * HEAD_DIM), lambda g, _: (0, g)),
                pl.BlockSpec((count, LANES), lambda g, _: (0, heads)),
                pl.BlockSpec((group,) + expand.shape[1:], lambda g, _: (g, 0, 0)),
                pl.BlockSpec(rows.shape, lambda g, _: (0, 0)),
            ],
            out_specs=[
                pl.BlockSpec((chunks, group, STATE, HEAD_DIM), lambda g, _: (0, g, 0, 0)),
                pl.BlockSpec((group, STATE + WIN, HEAD_DIM), lambda g, _: (g, 0, 0)),
            ],
        ),
        out_shape=[
            jax.ShapeDtypeStruct((chunks, heads, STATE, HEAD_DIM), F32),
            jax.ShapeDtypeStruct((heads, STATE + WIN, HEAD_DIM), BF16),
        ],
        compiler_params=params(),
    )(limits, both, both, expand, rows)


def windows(tiles):
    wide = TILE + WIN
    logits = jnp.concatenate(
        [
            lax.dot_general(q, k, (((1,), (1,)), ((), ())), preferred_element_type=F32)
            for q, k, _, _, _ in tiles
        ],
        0,
    )
    at = lax.broadcasted_iota(jnp.int32, (TILE, wide), 1)
    row = lax.broadcasted_iota(jnp.int32, (TILE, wide), 0)
    near = (at <= row + WIN) & (at > row)
    good = jnp.concatenate([near & (at >= first - start) for _, _, _, first, start in tiles], 0)
    logits = jnp.where(good, logits * HEAD_DIM**-0.5, -1e30)
    top = jnp.max(logits, 1, keepdims=True)
    weight = jnp.where(good, jnp.exp(logits - top), 0.0)
    probs = (weight / jnp.sum(weight, 1, keepdims=True)).astype(BF16)
    return [
        jnp.dot(probs[n * TILE : (n + 1) * TILE], tile[2], preferred_element_type=F32)
        for n, tile in enumerate(tiles)
    ]


def local_kernel(part, features, values, window, old_values, old_window, bounds, pick, expand, rows, *refs):
    inner, windowed, phi_query = refs[-3:]
    half = features.shape[0]
    base = part * half
    chunks = half // CHUNK
    if part == 0:
        tail_docs, first_doc = refs[:2]
        same = jnp.where(tail_docs[...].astype(F32) == first_doc[0:1, :] + 1.0, 1.0, 0.0)
        in_tail = jnp.sum(same, 0, keepdims=True)[:, 0:1].astype(jnp.int32)
    at = lax.broadcasted_iota(jnp.int32, (CHUNK, CHUNK), 1)
    row = lax.broadcasted_iota(jnp.int32, (CHUNK, CHUNK), 0)
    good = jnp.concatenate(
        [
            (at <= row) & (at >= bounds[n * CHUNK : (n + 1) * CHUNK] - (base + n * CHUNK))
            for n in range(chunks)
        ],
        0,
    )
    for h in range(values.shape[1] // HEAD_DIM):
        column = slice(h * HEAD_DIM, (h + 1) * HEAD_DIM)
        query = slice(2 * h * HEAD_DIM, (2 * h + 1) * HEAD_DIM)
        key = slice((2 * h + 1) * HEAD_DIM, (2 * h + 2) * HEAD_DIM)
        both = jnp.dot(features[...], pick[h], preferred_element_type=F32).astype(BF16)
        dots = jnp.concatenate(
            [
                lax.dot_general(
                    both[n * CHUNK : (n + 1) * CHUNK, :128], both[n * CHUNK : (n + 1) * CHUNK, 128:],
                    (((1,), (1,)), ((), ())), preferred_element_type=F32,
                )
                for n in range(chunks)
            ],
            0,
        )
        tiles = []
        for n in range(half // TILE):
            near = slice(n * TILE - WIN, (n + 1) * TILE)
            first = bounds[n * TILE : (n + 1) * TILE]
            if n:
                keys, vals = window[near, key], values[near, column]
            else:
                keys = jnp.concatenate([old_window[:, key], window[:TILE, key]], 0)
                old = old_values[:, column] if part else old_values[h, STATE:]
                vals = jnp.concatenate([old, values[:TILE, column]], 0)
                if part == 0:
                    first = jnp.where(first == 0, -in_tail, first)
            tiles.append(
                (window[n * TILE : (n + 1) * TILE, query], keys, vals, first, base + n * TILE - WIN)
            )
        results = windows(tiles)
        score = dots * (dots * (0.5 / FEAT) + FEAT**-0.5) + 1.0
        score = jnp.where(good, score, 0.0).astype(BF16)
        phi_query[:, h * WIDE : (h + 1) * WIDE] = phi(features[...], expand[h], rows[...])
        for n in range(chunks):
            here = slice(n * CHUNK, (n + 1) * CHUNK)
            inner[here, column] = jnp.dot(
                score[here], values[here, column], preferred_element_type=F32
            )
        for n, result in enumerate(results):
            windowed[n * TILE : (n + 1) * TILE, column] = result


def local(part, both, window, bounds, pick, expand, rows, heads, old=None, docs=()):
    half = both.shape[0] // 2
    group = min(GROUP, heads)

    def full(a):
        return pl.BlockSpec(a.shape, lambda g: (0,) * a.ndim)

    def some(count, width, at=0):
        return pl.BlockSpec((count, group * width), lambda g: (at, g))

    def per_head(a):
        return pl.BlockSpec((group,) + a.shape[1:], lambda g: (g, 0, 0))

    at = half // WIN - 1 if old is None else 0
    return pl.pallas_call(
        functools.partial(local_kernel, part),
        grid=(heads // group,),
        in_specs=[
            pl.BlockSpec((half, LANES), lambda g: (part, heads)),
            some(half, HEAD_DIM, part), some(half, 2 * HEAD_DIM, part),
            some(WIN, HEAD_DIM, at)
            if old is None
            else pl.BlockSpec((group, STATE + WIN, HEAD_DIM), lambda g: (g, 0, 0)),
            some(WIN, 2 * HEAD_DIM, at),
            pl.BlockSpec((half, 1), lambda g: (part, 0)),
            per_head(pick), per_head(expand), full(rows),
        ]
        + [full(a) for a in docs],
        out_specs=[some(half, HEAD_DIM), some(half, HEAD_DIM), some(half, WIDE)],
        out_shape=[
            jax.ShapeDtypeStruct((half, heads * HEAD_DIM), F32),
            jax.ShapeDtypeStruct((half, heads * HEAD_DIM), F32),
            jax.ShapeDtypeStruct((half, heads * WIDE), BF16),
        ],
        compiler_params=params(),
    )(both, both, window, *(old or (both, window)), bounds, pick, expand, rows, *docs)


def finish_kernel(shifts, limits, first_doc, bounds, prefix, *refs):
    halves, states, outs = (refs[:3], refs[3:6]), refs[6 : 6 + shifts], refs[6 + shifts :]
    unmarked = lax.broadcasted_iota(jnp.int32, (STATE, HEAD_DIM), 0) < STATE - 1
    chunks = outs[0].shape[0] // CHUNK
    for h in range(outs[0].shape[1] // HEAD_DIM):
        column = slice(h * HEAD_DIM, (h + 1) * HEAD_DIM)
        incoming = jnp.zeros((STATE, HEAD_DIM), F32)
        for k in range(shifts):
            sent = states[k][h, :STATE].astype(F32)
            wanted = (sent[STATE - 1 :] == first_doc[0:1, :] + 1.0) & unmarked
            incoming += jnp.where(wanted, sent, 0.0)
        for part, (inner, windowed, phi_query) in enumerate(halves):
            carried = []
            for n in range(chunks):
                chunk = part * chunks + n
                state = incoming
                if chunk:
                    state = jnp.where(limits[chunk - 1] <= 0, incoming, 0.0) + prefix[chunk, h]
                state = jnp.concatenate([state, jnp.zeros((WIDE - STATE, HEAD_DIM), F32)], 0)
                one = jnp.dot(
                    phi_query[n * CHUNK : (n + 1) * CHUNK, h * WIDE : (h + 1) * WIDE],
                    state.astype(BF16), preferred_element_type=F32,
                )
                first = bounds[chunk * CHUNK : (chunk + 1) * CHUNK]
                carried.append(jnp.where(first <= chunk * CHUNK, one, 0.0))
            linear = inner[:, column] + jnp.concatenate(carried, 0)
            mean = jnp.mean(linear * linear, 1, keepdims=True)
            normed = linear * lax.rsqrt(mean + 1e-5)
            outs[part][:, column] = (normed + windowed[:, column]).astype(BF16)


def finish(limits, first_doc, bounds, prefix, low, high, states):
    half, columns = low[0].shape
    heads = columns // HEAD_DIM
    group = min(GROUP, heads)

    def some(count, width):
        return pl.BlockSpec((count, group * width), lambda g, *_: (0, g))

    return pl.pallas_call(
        functools.partial(finish_kernel, len(states)),
        grid_spec=pltpu.PrefetchScalarGridSpec(
            num_scalar_prefetch=1,
            grid=(heads // group,),
            in_specs=[
                pl.BlockSpec(first_doc.shape, lambda g, *_: (0, 0)),
                pl.BlockSpec(bounds.shape, lambda g, *_: (0, 0)),
                pl.BlockSpec((prefix.shape[0], group, STATE, HEAD_DIM), lambda g, *_: (0, g, 0, 0)),
            ]
            + [some(half, HEAD_DIM), some(half, HEAD_DIM), some(half, WIDE)] * 2
            + [pl.BlockSpec((group, STATE + WIN, HEAD_DIM), lambda g, *_: (g, 0, 0))] * len(states),
            out_specs=[some(half, HEAD_DIM)] * 2,
        ),
        out_shape=[jax.ShapeDtypeStruct((half, columns), BF16)] * 2,
        compiler_params=params(),
    )(limits, first_doc, bounds, prefix, *low, *high, *states)


def after(x, *others):
    return lax.optimization_barrier((x, *others))[0]


def shards(tokens, doc_ids, w_feat, w_value, w_window, w_out):
    rows = tokens.shape[0]
    chunks = rows // CHUNK
    value_columns = w_value.shape[1]
    heads = value_columns // HEAD_DIM
    count = lax.axis_size("head") // 2
    blocks = lax.axis_size("ctx")
    me = lax.axis_index("head")
    z, c = me // 2, me % 2
    place = jnp.stack([z, c]).astype(jnp.int32)

    pieces = {0: tokens, 1: ring(tokens, -1, count), count - 1: ring(tokens, 1, count)}
    tokens_there = swap(tokens, count)

    docs = doc_ids.astype(F32)
    ends = jnp.concatenate([docs[CHUNK::CHUNK], docs[rows - 1 :]])
    limits = jnp.sum((docs[None, :] < ends[:, None]).astype(F32), 1).astype(jnp.int32)
    limits = jnp.concatenate([limits, doc_ids[rows - 1 :]])
    first = jnp.sum((docs[None, :] < docs[:, None]).astype(F32), 1, keepdims=True)
    bounds = first.astype(jnp.int32)
    first_doc = jnp.broadcast_to(docs[:1], (8, HEAD_DIM))
    tail_docs = jnp.broadcast_to((docs[rows - WIN :] + 1.0).astype(BF16)[:, None], (WIN, HEAD_DIM))
    onward = [(i, i + 1) for i in range(blocks - 1)]
    tail_docs = lax.ppermute(tail_docs, "ctx", onward)

    maps, scale_rows = expansions(heads)
    query_map, key_map = jnp.asarray(maps[0]), jnp.asarray(maps[1])
    scale_rows = jnp.asarray(scale_rows)
    pick = jnp.asarray(picks(heads))

    depth, columns = w_out.shape
    width = columns // (2 * count)

    rows_out = after(w_out, tokens_there)

    def cut(chip, core):
        return lax.dynamic_slice(rows_out, (0, (2 * chip + core) * width), (depth, width))

    other_rows = swap(jnp.stack([cut(chip, 1 - c) for chip in range(count)]), count)
    out_rows = []
    for n in range(count):
        chip = lax.rem(z + n, count)
        theirs = lax.dynamic_index_in_dim(other_rows, chip, 0, keepdims=False)
        out_rows += [cut(chip, c), theirs]

    used = value_columns + w_feat.shape[1]
    fv_columns = -(-used // 256) * 256
    weight = jnp.concatenate(
        [w_value, w_feat, jnp.zeros((w_value.shape[0], fv_columns - used), BF16), w_window], 1
    )
    all_columns = weight.shape[1]
    widths = (fv_columns, all_columns - fv_columns)
    part = project(place, (0,), [tokens], [tokens_there], weight, 0, widths)

    ready = lax.optimization_barrier(
        (pieces[1], pieces[count - 1], limits, bounds, first_doc, tail_docs, *part, *out_rows)
    )
    pieces[1], pieces[count - 1], limits, bounds, first_doc, tail_docs = ready[:6]
    part, out_rows = ready[6:8], ready[8:]

    for n in range(2, count // 2 + 1):
        pieces[n] = ring(pieces[n - 1], -1, count)
    for n in range(count - 2, count // 2, -1):
        pieces[n] = ring(pieces[n + 1], 1, count)
    near = (1, count - 1)
    mine = [pieces[n] for n in near]
    part = project(
        place, near, mine, [swap(p, count) for p in mine], weight, 0, widths, part
    )
    late = tuple(range(2, count - 1))
    *mine, fv_part, win_part = lax.optimization_barrier((*[pieces[n] for n in late], *part))
    theirs = [swap(p, count) for p in mine]
    (both,) = project(place, late, mine, theirs, weight, 0, widths[:1], [fv_part], BF16)
    prefix, state = sums(limits, both, heads, key_map, scale_rows)
    states = [
        lax.ppermute(state, "ctx", [(i, i + k) for i in range(blocks - k)])
        for k in range(1, blocks)
    ]
    window, tail = project(
        place, late, [after(mine[0], state), *mine[1:]], theirs, weight, fv_columns, widths[1:],
        [win_part], BF16, True,
    )
    tail = lax.ppermute(tail, "ctx", onward)
    common = (window, bounds, pick, query_map, scale_rows, heads)
    local_high = local(1, both, *common)
    local_low = local(
        0, after(both, local_high[0]), *common, (states[0], tail), (tail_docs, first_doc)
    )
    low, high = finish(limits, first_doc, bounds, prefix, local_low, local_high, states)

    def scattered(mixed, step):
        swapped = swap(mixed, count)
        sent = None
        for n in range(1, count + 1):
            at = 2 * (-step * n % count)
            total = jnp.dot(mixed, out_rows[at], preferred_element_type=F32)
            total += jnp.dot(swapped, out_rows[at + 1], preferred_element_type=F32)
            if sent is not None:
                total += ring(sent, step, count).astype(F32)
            sent = total.astype(BF16)
        return sent

    high_out = scattered(high, -1)
    low_out = scattered(low, 1)
    return jnp.concatenate([low_out, high_out], 0)


def solution(mesh):
    return jax.shard_map(
        shards,
        mesh=mesh,
        in_specs=(
            P("ctx", "head"),
            P("ctx"),
            P(None, "head"),
            P(None, "head"),
            P(None, "head"),
            P("head", None),
        ),
        out_specs=P("ctx", "head"),
        check_vma=False,
    )
```

```python
import functools

import jax
import jax.numpy as jnp
import numpy as np
from jax import lax
from jax.experimental import pallas as pl
from jax.experimental.pallas import tpu as pltpu
from jax.sharding import PartitionSpec as P

HEAD_DIM = 128
FEAT = 16
WIN = 64
PAIRS = [(i, j) for i in range(FEAT) for j in range(i, FEAT)]
WIDE = 256
CHUNK = 256
GROUP = 4
STATE = -(-(len(PAIRS) + FEAT + 1) // 16) * 16
SENT = STATE + 2 * WIN
VMEM = 24 * 1024 * 1024
TILE = 128
LANES = 128
F32 = jnp.float32
BF16 = jnp.bfloat16


def params():
    return pltpu.CompilerParams(vmem_limit_bytes=VMEM, dimension_semantics=("arbitrary",))


def ring(x, step, count):
    return lax.ppermute(
        x, "head", [(2 * z + c, 2 * ((z + step) % count) + c) for z in range(count) for c in (0, 1)]
    )


def swap(x, count):
    return lax.ppermute(x, "head", [(h, h ^ 1) for h in range(2 * count)])


def by_column(c, mine, theirs, both):
    width = mine[0].shape[1]
    for n in range(len(mine)):
        own = pl.multiple_of((2 * n + c) * width, width)
        other = pl.multiple_of((2 * n + 1 - c) * width, width)
        both[:, pl.ds(own, width)] = mine[n][...]
        both[:, pl.ds(other, width)] = theirs[n][...]


def project_kernel(chips, cuts, has_before, place, *refs):
    mine, theirs, weights = refs[:chips], refs[chips : 2 * chips], refs[2 * chips : 3 * chips]
    before = refs[3 * chips : 3 * chips + len(cuts)] if has_before else None
    outs, both = refs[-1 - len(cuts) : -1], refs[-1]
    width = mine[0].shape[1]
    c = place[1]
    step = pl.program_id(0)

    @pl.when(step == 0)
    def _():
        by_column(c, mine, theirs, both)

    def tile(k):
        total = before[k][...] if has_before else None
        for n in range(chips):
            rows = both[:, 2 * n * width : 2 * (n + 1) * width]
            part = jnp.dot(rows, weights[n][...], preferred_element_type=F32)
            total = part if total is None else total + part
        outs[k][...] = total.astype(outs[k].dtype)

    if len(cuts) == 1:
        tile(0)
    else:

        @pl.when(step < cuts[0])
        def _():
            tile(0)

        @pl.when(step >= cuts[0])
        def _():
            tile(1)


def project(place, chips, mine, theirs, weight, first, columns, before=None, dtype=F32):
    rows, width = mine[0].shape
    count = weight.shape[0] // (2 * width)
    size = 256
    start = first // size
    cuts = [n // size for n in columns]
    specs = [pl.BlockSpec((rows, width), lambda j, p: (0, 0))] * (2 * len(chips))
    for n in chips:
        specs.append(
            pl.BlockSpec(
                (2 * width, size), lambda j, p, n=n: (lax.rem(p[0] + n, count), start + j)
            )
        )
    results = [
        pl.BlockSpec(
            (rows, size),
            lambda j, p, at=sum(cuts[:k]), n=cuts[k]: (0, jnp.clip(j - at, 0, n - 1)),
        )
        for k in range(len(cuts))
    ]
    args = [*mine, *theirs] + [weight] * len(chips)
    if before is not None:
        specs += results
        args += before
    shapes = [jax.ShapeDtypeStruct((rows, n), dtype) for n in columns]
    return pl.pallas_call(
        functools.partial(project_kernel, len(chips), cuts, before is not None),
        grid_spec=pltpu.PrefetchScalarGridSpec(
            num_scalar_prefetch=1,
            grid=(sum(cuts),),
            in_specs=specs,
            out_specs=results,
            scratch_shapes=[pltpu.VMEM((rows, 2 * width * len(chips)), BF16)],
        ),
        out_shape=shapes,
        compiler_params=params(),
    )(place, *args)


def late_kernel(chips, heads, place, *refs):
    mine, theirs, weights = refs[:chips], refs[chips : 2 * chips], refs[2 * chips : 3 * chips]
    key_weights = refs[3 * chips : (3 + heads) * chips]
    before, *key_before = refs[(3 + heads) * chips : (3 + heads) * chips + 1 + heads]
    out, keys, both = refs[-3:]
    width = 2 * mine[0].shape[1]
    step = pl.program_id(0)

    @pl.when(step == 0)
    def _():
        by_column(place[1], mine, theirs, both)

    total = before[...]
    for n in range(chips):
        rows = both[:, n * width : (n + 1) * width]
        total += jnp.dot(rows, weights[n][...], preferred_element_type=F32)
    out[...] = total.astype(BF16)

    @pl.when(step == pl.num_programs(0) - 1)
    def _():
        last = slice(out.shape[0] - WIN, out.shape[0])
        for h in range(heads):
            tail = key_before[h][...]
            for n in range(chips):
                tail += jnp.dot(
                    both[last, n * width : (n + 1) * width], key_weights[n * heads + h][...],
                    preferred_element_type=F32,
                )
            keys[h] = tail.astype(BF16)


def project_late(place, chips, mine, theirs, weight, heads, before, window_before):
    rows, width = mine[0].shape
    count = weight.shape[0] // (2 * width)
    columns = before.shape[1]
    size = 256
    first = columns // HEAD_DIM + 1
    specs = [pl.BlockSpec((rows, width), lambda j, p: (0, 0))] * (2 * len(chips))
    for n in chips:
        specs.append(
            pl.BlockSpec((2 * width, size), lambda j, p, n=n: (lax.rem(p[0] + n, count), j))
        )
    for n in chips:
        for h in range(heads):
            specs.append(
                pl.BlockSpec(
                    (2 * width, HEAD_DIM),
                    lambda j, p, n=n, h=h: (lax.rem(p[0] + n, count), first + 2 * h),
                )
            )
    block = pl.BlockSpec((rows, size), lambda j, p: (0, j))
    specs.append(block)
    for h in range(heads):
        specs.append(pl.BlockSpec((WIN, HEAD_DIM), lambda j, p, h=h: (rows // WIN - 1, 2 * h + 1)))
    return pl.pallas_call(
        functools.partial(late_kernel, len(chips), heads),
        grid_spec=pltpu.PrefetchScalarGridSpec(
            num_scalar_prefetch=1,
            grid=(columns // size,),
            in_specs=specs,
            out_specs=[block, pl.BlockSpec((heads, WIN, HEAD_DIM), lambda j, p: (0, 0, 0))],
            scratch_shapes=[pltpu.VMEM((rows, 2 * width * len(chips)), BF16)],
        ),
        out_shape=[
            jax.ShapeDtypeStruct((rows, columns), BF16),
            jax.ShapeDtypeStruct((heads, WIN, HEAD_DIM), BF16),
        ],
        compiler_params=params(),
    )(place, *mine, *theirs, *[weight] * (len(chips) * (1 + heads)), before, *[window_before] * heads)


def expansions(heads):
    lanes = -(-heads * 2 * FEAT // LANES) * LANES
    maps = np.zeros((2, heads, lanes, 2 * WIDE), np.float32)
    rows = np.zeros((3, WIDE), np.float32)
    for h in range(heads):
        for side in (0, 1):
            base = h * 2 * FEAT + side * FEAT
            for n, (i, j) in enumerate(PAIRS):
                maps[side, h, base + i, n] = 1.0
                maps[side, h, base + j, WIDE + n] = 1.0
            for i in range(FEAT):
                maps[side, h, base + i, len(PAIRS) + i] = 1.0
    for n, (i, j) in enumerate(PAIRS):
        rows[2, n] = (2.0 * FEAT) ** -0.5 * (1.0 if i == j else 2.0**0.5)
    rows[1, len(PAIRS) : len(PAIRS) + FEAT + 1] = 1.0
    rows[0, len(PAIRS) + FEAT] = 1.0
    rows[2, len(PAIRS) : len(PAIRS) + FEAT] = FEAT**-0.25
    rows[2, len(PAIRS) + FEAT] = 1.0
    return maps.astype(jnp.bfloat16), rows


def picks(heads):
    lanes = -(-heads * 2 * FEAT // LANES) * LANES
    maps = np.zeros((heads, lanes, 256), np.float32)
    for h in range(heads):
        for i in range(FEAT):
            maps[h, h * 2 * FEAT + i, i] = 1.0
            maps[h, h * 2 * FEAT + FEAT + i, 128 + i] = 1.0
    return maps.astype(jnp.bfloat16)


def phi(features, expand, rows):
    factors = jnp.dot(features, expand, preferred_element_type=F32)
    left = factors[:, :WIDE] + rows[0:1]
    right = factors[:, WIDE:] + rows[1:2]
    return (left * right * rows[2:3]).astype(BF16)


def sums_kernel(limits, values, features, expand, rows, keys, prefix, end):
    chunks, heads = prefix.shape[:2]
    mark = lax.broadcasted_iota(jnp.int32, (STATE, HEAD_DIM), 0) == STATE - 1
    at = lax.broadcasted_iota(jnp.int32, (CHUNK, HEAD_DIM), 0)
    for h in range(heads):
        column = slice(h * HEAD_DIM, (h + 1) * HEAD_DIM)
        phi_key = phi(features[...], expand[h], rows[...])
        parts = []
        for n in range(chunks):
            here = slice(n * CHUNK, (n + 1) * CHUNK)
            kept = jnp.where(at + n * CHUNK >= limits[n], values[here, column].astype(F32), 0.0)
            parts.append(
                lax.dot_general(
                    phi_key[here], kept.astype(BF16), (((0,), (0,)), ((), ())),
                    preferred_element_type=F32,
                )[:STATE]
            )
        state = jnp.zeros((STATE, HEAD_DIM), F32)
        for n in range(chunks):
            prefix[n, h] = state
            state = parts[n] + jnp.where(limits[n] <= n * CHUNK, state, 0.0)
        end[h, :STATE] = jnp.where(mark, (limits[chunks] + 1).astype(F32), state).astype(BF16)
        end[h, STATE : STATE + WIN] = values[values.shape[0] - WIN :, column]
        end[h, STATE + WIN :] = keys[h]


def sums(limits, both, keys, expand, rows):
    heads = keys.shape[0]
    chunks = both.shape[0] // CHUNK
    group = min(GROUP, heads)
    count = both.shape[0]
    return pl.pallas_call(
        sums_kernel,
        grid_spec=pltpu.PrefetchScalarGridSpec(
            num_scalar_prefetch=1,
            grid=(heads // group,),
            in_specs=[
                pl.BlockSpec((count, group * HEAD_DIM), lambda g, _: (0, g)),
                pl.BlockSpec((count, LANES), lambda g, _: (0, heads)),
                pl.BlockSpec((group,) + expand.shape[1:], lambda g, _: (g, 0, 0)),
                pl.BlockSpec(rows.shape, lambda g, _: (0, 0)),
                pl.BlockSpec((group, WIN, HEAD_DIM), lambda g, _: (g, 0, 0)),
            ],
            out_specs=[
                pl.BlockSpec((chunks, group, STATE, HEAD_DIM), lambda g, _: (0, g, 0, 0)),
                pl.BlockSpec((group, SENT, HEAD_DIM), lambda g, _: (g, 0, 0)),
            ],
        ),
        out_shape=[
            jax.ShapeDtypeStruct((chunks, heads, STATE, HEAD_DIM), F32),
            jax.ShapeDtypeStruct((heads, SENT, HEAD_DIM), BF16),
        ],
        compiler_params=params(),
    )(limits, both, both, expand, rows, keys)


def windows(tiles):
    wide = TILE + WIN
    logits = jnp.concatenate(
        [
            lax.dot_general(q, k, (((1,), (1,)), ((), ())), preferred_element_type=F32)
            for q, k, _, _, _ in tiles
        ],
        0,
    )
    at = lax.broadcasted_iota(jnp.int32, (TILE, wide), 1)
    row = lax.broadcasted_iota(jnp.int32, (TILE, wide), 0)
    near = (at <= row + WIN) & (at > row)
    good = jnp.concatenate([near & (at >= first - start) for _, _, _, first, start in tiles], 0)
    logits = jnp.where(good, logits * HEAD_DIM**-0.5, -1e30)
    top = jnp.max(logits, 1, keepdims=True)
    weight = jnp.where(good, jnp.exp(logits - top), 0.0)
    probs = (weight / jnp.sum(weight, 1, keepdims=True)).astype(BF16)
    return [
        jnp.dot(probs[n * TILE : (n + 1) * TILE], tile[2], preferred_element_type=F32)
        for n, tile in enumerate(tiles)
    ]


def mix_kernel(
    chips, shifts, place, limits, values, features, window_before, bounds, pick, expand, rows, prefix,
    tail_docs, first_doc, *refs
):
    mine, theirs, weights = refs[:chips], refs[chips : 2 * chips], refs[2 * chips : 3 * chips]
    states = refs[3 * chips : 3 * chips + shifts]
    *outs, both, window = refs[3 * chips + shifts :]
    width = 2 * mine[0].shape[1]
    count = values.shape[0]
    half = count // 2

    @pl.when(pl.program_id(0) == 0)
    def _():
        by_column(place[1], mine, theirs, both)

    total = window_before[...]
    for n in range(chips):
        total += jnp.dot(
            both[:, n * width : (n + 1) * width], weights[n][...], preferred_element_type=F32
        )
    window[...] = total.astype(BF16)

    pair = jnp.dot(features[...], pick[0], preferred_element_type=F32).astype(BF16)
    phi_query = phi(features[...], expand[0], rows[...])
    chunks = count // CHUNK
    at = lax.broadcasted_iota(jnp.int32, (CHUNK, CHUNK), 1)
    row = lax.broadcasted_iota(jnp.int32, (CHUNK, CHUNK), 0)
    dots, good = [], []
    for n in range(chunks):
        here = slice(n * CHUNK, (n + 1) * CHUNK)
        dots.append(
            lax.dot_general(
                pair[here, :128], pair[here, 128:], (((1,), (1,)), ((), ())),
                preferred_element_type=F32,
            )
        )
        good.append((at <= row) & (at >= bounds[here] - n * CHUNK))
    dots, good = jnp.concatenate(dots, 0), jnp.concatenate(good, 0)
    score = dots * (dots * (0.5 / FEAT) + FEAT**-0.5) + 1.0
    score = jnp.where(good, score, 0.0).astype(BF16)

    same = jnp.where(tail_docs[...].astype(F32) == first_doc[0:1, :] + 1.0, 1.0, 0.0)
    in_tail = jnp.sum(same, 0, keepdims=True)[:, 0:1].astype(jnp.int32)
    tiles = []
    for n in range(count // TILE):
        near = slice(n * TILE - WIN, (n + 1) * TILE)
        first = bounds[n * TILE : (n + 1) * TILE]
        if n:
            keys, vals = window[near, HEAD_DIM:], values[near]
        else:
            keys = jnp.concatenate([states[0][0, STATE + WIN :], window[:TILE, HEAD_DIM:]], 0)
            vals = jnp.concatenate([states[0][0, STATE : STATE + WIN], values[:TILE]], 0)
            first = jnp.where(first == 0, -in_tail, first)
        tiles.append(
            (window[n * TILE : (n + 1) * TILE, :HEAD_DIM], keys, vals, first, n * TILE - WIN)
        )
    windowed = jnp.concatenate(windows(tiles), 0)

    unmarked = lax.broadcasted_iota(jnp.int32, (STATE, HEAD_DIM), 0) < STATE - 1
    incoming = jnp.zeros((STATE, HEAD_DIM), F32)
    for k in range(shifts):
        sent = states[k][0, :STATE].astype(F32)
        wanted = (sent[STATE - 1 :] == first_doc[0:1, :] + 1.0) & unmarked
        incoming += jnp.where(wanted, sent, 0.0)
    linear = []
    for n in range(chunks):
        here = slice(n * CHUNK, (n + 1) * CHUNK)
        state = incoming
        if n:
            state = jnp.where(limits[n - 1] <= 0, incoming, 0.0) + prefix[n, 0]
        state = jnp.concatenate([state, jnp.zeros((WIDE - STATE, HEAD_DIM), F32)], 0)
        carried = jnp.dot(phi_query[here], state.astype(BF16), preferred_element_type=F32)
        inner = jnp.dot(score[here], values[here], preferred_element_type=F32)
        linear.append(inner + jnp.where(bounds[here] <= n * CHUNK, carried, 0.0))
    linear = jnp.concatenate(linear, 0)
    mean = jnp.mean(linear * linear, 1, keepdims=True)
    mixed = (linear * lax.rsqrt(mean + 1e-5) + windowed).astype(BF16)
    outs[0][...] = mixed[:half]
    outs[1][...] = mixed[half:]


def mix(place, limits, chips, mine, theirs, weight, both, window_before, bounds, pick, expand, rows, prefix,
        tail_docs, first_doc, states):
    count, width = mine[0].shape
    heads = states[0].shape[0]
    half = count // 2
    ring_size = weight.shape[0] // (2 * width)
    tile = 2 * HEAD_DIM
    first = both.shape[1] // tile

    def full(a):
        return pl.BlockSpec(a.shape, lambda h, *_: (0,) * a.ndim)

    def per_head(a):
        return pl.BlockSpec((1,) + a.shape[1:], lambda h, *_: (h, 0, 0))

    specs = [
        pl.BlockSpec((count, HEAD_DIM), lambda h, *_: (0, h)),
        pl.BlockSpec((count, LANES), lambda h, *_: (0, heads)),
        pl.BlockSpec((count, tile), lambda h, *_: (0, h)),
        full(bounds), per_head(pick), per_head(expand), full(rows),
        pl.BlockSpec((prefix.shape[0], 1, STATE, HEAD_DIM), lambda h, *_: (0, h, 0, 0)),
        full(tail_docs), full(first_doc),
    ]
    specs += [full(mine[0])] * (2 * len(chips))
    for n in chips:
        specs.append(
            pl.BlockSpec(
                (2 * width, tile), lambda h, p, _, n=n: (lax.rem(p[0] + n, ring_size), first + h)
            )
        )
    specs += [per_head(a) for a in states]
    return pl.pallas_call(
        functools.partial(mix_kernel, len(chips), len(states)),
        grid_spec=pltpu.PrefetchScalarGridSpec(
            num_scalar_prefetch=2,
            grid=(heads,),
            in_specs=specs,
            out_specs=[pl.BlockSpec((half, HEAD_DIM), lambda h, *_: (0, h))] * 2,
            scratch_shapes=[
                pltpu.VMEM((count, 2 * width * len(chips)), BF16),
                pltpu.VMEM((count, tile), BF16),
            ],
        ),
        out_shape=[jax.ShapeDtypeStruct((half, heads * HEAD_DIM), BF16)] * 2,
        compiler_params=params(),
    )(place, limits, both, both, window_before, bounds, pick, expand, rows, prefix, tail_docs, first_doc,
      *mine, *theirs, *[weight] * len(chips), *states)


def after(x, *others):
    return lax.optimization_barrier((x, *others))[0]


def shards(tokens, doc_ids, w_feat, w_value, w_window, w_out):
    rows = tokens.shape[0]
    chunks = rows // CHUNK
    value_columns = w_value.shape[1]
    heads = value_columns // HEAD_DIM
    count = lax.axis_size("head") // 2
    blocks = lax.axis_size("ctx")
    me = lax.axis_index("head")
    z, c = me // 2, me % 2
    place = jnp.stack([z, c]).astype(jnp.int32)

    pieces = {0: tokens, 1: ring(tokens, -1, count), count - 1: ring(tokens, 1, count)}
    tokens_there = swap(tokens, count)

    docs = doc_ids.astype(F32)
    ends = jnp.concatenate([docs[CHUNK::CHUNK], docs[rows - 1 :]])
    limits = jnp.sum((docs[None, :] < ends[:, None]).astype(F32), 1).astype(jnp.int32)
    limits = jnp.concatenate([limits, doc_ids[rows - 1 :]])
    first = jnp.sum((docs[None, :] < docs[:, None]).astype(F32), 1, keepdims=True)
    bounds = first.astype(jnp.int32)
    first_doc = jnp.broadcast_to(docs[:1], (8, HEAD_DIM))
    tail_docs = jnp.broadcast_to((docs[rows - WIN :] + 1.0).astype(BF16)[:, None], (WIN, HEAD_DIM))
    onward = [(i, i + 1) for i in range(blocks - 1)]
    tail_docs = lax.ppermute(tail_docs, "ctx", onward)

    maps, scale_rows = expansions(heads)
    query_map, key_map = jnp.asarray(maps[0]), jnp.asarray(maps[1])
    scale_rows = jnp.asarray(scale_rows)
    pick = jnp.asarray(picks(heads))

    depth, columns = w_out.shape
    width = columns // (2 * count)

    rows_out = after(w_out, tokens_there)

    def cut(chip, core):
        return lax.dynamic_slice(rows_out, (0, (2 * chip + core) * width), (depth, width))

    other_rows = swap(jnp.stack([cut(chip, 1 - c) for chip in range(count)]), count)
    out_rows = []
    for n in range(count):
        chip = lax.rem(z + n, count)
        theirs = lax.dynamic_index_in_dim(other_rows, chip, 0, keepdims=False)
        out_rows += [cut(chip, c), theirs]

    used = value_columns + w_feat.shape[1]
    fv_columns = -(-used // 256) * 256
    weight = jnp.concatenate(
        [w_value, w_feat, jnp.zeros((w_value.shape[0], fv_columns - used), BF16), w_window], 1
    )
    all_columns = weight.shape[1]
    widths = (fv_columns, all_columns - fv_columns)
    part = project(place, (0,), [tokens], [tokens_there], weight, 0, widths)

    ready = lax.optimization_barrier(
        (pieces[1], pieces[count - 1], limits, bounds, first_doc, tail_docs, *part, *out_rows)
    )
    pieces[1], pieces[count - 1], limits, bounds, first_doc, tail_docs = ready[:6]
    part, out_rows = ready[6:8], ready[8:]

    for n in range(2, count // 2 + 1):
        pieces[n] = ring(pieces[n - 1], -1, count)
    for n in range(count - 2, count // 2, -1):
        pieces[n] = ring(pieces[n + 1], 1, count)
    near = (1, count - 1)
    mine = [pieces[n] for n in near]
    part = project(
        place, near, mine, [swap(p, count) for p in mine], weight, 0, widths, part
    )
    late = tuple(range(2, count - 1))
    *mine, fv_part, win_part = lax.optimization_barrier((*[pieces[n] for n in late], *part))
    theirs = [swap(p, count) for p in mine]
    both, keys = project_late(place, late, mine, theirs, weight, heads, fv_part, win_part)
    prefix, state = sums(limits, both, keys, key_map, scale_rows)
    states = [
        lax.ppermute(state, "ctx", [(i, i + k) for i in range(blocks - k)])
        for k in range(1, blocks)
    ]
    low, high = mix(
        place, limits, late, mine, theirs, weight, both, win_part, bounds, pick, query_map, scale_rows,
        prefix, tail_docs, first_doc, states,
    )

    def scattered(mixed, step):
        swapped = swap(mixed, count)
        sent = None
        for n in range(1, count + 1):
            at = 2 * (-step * n % count)
            total = jnp.dot(mixed, out_rows[at], preferred_element_type=F32)
            total += jnp.dot(swapped, out_rows[at + 1], preferred_element_type=F32)
            if sent is not None:
                total += ring(sent, step, count).astype(F32)
            sent = total.astype(BF16)
        return sent

    high_out = scattered(high, -1)
    low_out = scattered(low, 1)
    return jnp.concatenate([low_out, high_out], 0)


def solution(mesh):
    return jax.shard_map(
        shards,
        mesh=mesh,
        in_specs=(
            P("ctx", "head"),
            P("ctx"),
            P(None, "head"),
            P(None, "head"),
            P(None, "head"),
            P("head", None),
        ),
        out_specs=P("ctx", "head"),
        check_vma=False,
    )
```

```python
import functools

import jax
import jax.numpy as jnp
import numpy as np
from jax import lax
from jax.experimental import pallas as pl
from jax.experimental.pallas import tpu as pltpu
from jax.sharding import PartitionSpec as P

HEAD_DIM = 128
FEAT = 16
WIN = 64
PAIRS = [(i, j) for i in range(FEAT) for j in range(i, FEAT)]
WIDE = 256
CHUNK = 256
GROUP = 4
STATE = -(-(len(PAIRS) + FEAT + 1) // 16) * 16
SENT = STATE + 2 * WIN
VMEM = 24 * 1024 * 1024
TILE = 128
LANES = 128
F32 = jnp.float32
BF16 = jnp.bfloat16


def params(limit=VMEM):
    return pltpu.CompilerParams(vmem_limit_bytes=limit, dimension_semantics=("arbitrary",))


def ring(x, step, count):
    return lax.ppermute(
        x, "head", [(2 * z + c, 2 * ((z + step) % count) + c) for z in range(count) for c in (0, 1)]
    )


def swap(x, count):
    return lax.ppermute(x, "head", [(h, h ^ 1) for h in range(2 * count)])


def by_column(c, mine, theirs, both):
    width = mine[0].shape[1]
    for n in range(len(mine)):
        own = pl.multiple_of((2 * n + c) * width, width)
        other = pl.multiple_of((2 * n + 1 - c) * width, width)
        both[:, pl.ds(own, width)] = mine[n][...]
        both[:, pl.ds(other, width)] = theirs[n][...]


def project_kernel(chips, cuts, has_before, place, *refs):
    mine, theirs, weights = refs[:chips], refs[chips : 2 * chips], refs[2 * chips : 3 * chips]
    before = refs[3 * chips : 3 * chips + len(cuts)] if has_before else None
    outs, both = refs[-1 - len(cuts) : -1], refs[-1]
    width = mine[0].shape[1]
    c = place[1]
    step = pl.program_id(0)

    @pl.when(step == 0)
    def _():
        by_column(c, mine, theirs, both)

    def tile(k):
        total = before[k][...] if has_before else None
        for n in range(chips):
            rows = both[:, 2 * n * width : 2 * (n + 1) * width]
            part = jnp.dot(rows, weights[n][...], preferred_element_type=F32)
            total = part if total is None else total + part
        outs[k][...] = total.astype(outs[k].dtype)

    if len(cuts) == 1:
        tile(0)
    else:

        @pl.when(step < cuts[0])
        def _():
            tile(0)

        @pl.when(step >= cuts[0])
        def _():
            tile(1)


def project(place, chips, mine, theirs, weight, first, columns, before=None, dtype=F32, limit=VMEM):
    rows, width = mine[0].shape
    count = weight.shape[0] // (2 * width)
    size = 256
    start = first // size
    cuts = [n // size for n in columns]
    specs = [pl.BlockSpec((rows, width), lambda j, p: (0, 0))] * (2 * len(chips))
    for n in chips:
        specs.append(
            pl.BlockSpec(
                (2 * width, size), lambda j, p, n=n: (lax.rem(p[0] + n, count), start + j)
            )
        )
    results = [
        pl.BlockSpec(
            (rows, size),
            lambda j, p, at=sum(cuts[:k]), n=cuts[k]: (0, jnp.clip(j - at, 0, n - 1)),
        )
        for k in range(len(cuts))
    ]
    args = [*mine, *theirs] + [weight] * len(chips)
    if before is not None:
        specs += results
        args += before
    shapes = [jax.ShapeDtypeStruct((rows, n), dtype) for n in columns]
    return pl.pallas_call(
        functools.partial(project_kernel, len(chips), cuts, before is not None),
        grid_spec=pltpu.PrefetchScalarGridSpec(
            num_scalar_prefetch=1,
            grid=(sum(cuts),),
            in_specs=specs,
            out_specs=results,
            scratch_shapes=[pltpu.VMEM((rows, 2 * width * len(chips)), BF16)],
        ),
        out_shape=shapes,
        compiler_params=params(limit),
    )(place, *args)


def late_kernel(chips, heads, place, *refs):
    mine, theirs, weights = refs[:chips], refs[chips : 2 * chips], refs[2 * chips : 3 * chips]
    key_weights = refs[3 * chips : (3 + heads) * chips]
    before, *key_before = refs[(3 + heads) * chips : (3 + heads) * chips + 1 + heads]
    out, keys, both = refs[-3:]
    width = 2 * mine[0].shape[1]
    step = pl.program_id(0)

    @pl.when(step == 0)
    def _():
        by_column(place[1], mine, theirs, both)

    total = before[...]
    for n in range(chips):
        rows = both[:, n * width : (n + 1) * width]
        total += jnp.dot(rows, weights[n][...], preferred_element_type=F32)
    out[...] = total.astype(BF16)

    @pl.when(step == pl.num_programs(0) - 1)
    def _():
        last = slice(out.shape[0] - WIN, out.shape[0])
        for h in range(heads):
            tail = key_before[h][...]
            for n in range(chips):
                tail += jnp.dot(
                    both[last, n * width : (n + 1) * width], key_weights[n * heads + h][...],
                    preferred_element_type=F32,
                )
            keys[h] = tail.astype(BF16)


def project_late(place, chips, mine, theirs, weight, heads, before, window_before):
    rows, width = mine[0].shape
    count = weight.shape[0] // (2 * width)
    columns = before.shape[1]
    size = 256
    first = columns // HEAD_DIM + 1
    specs = [pl.BlockSpec((rows, width), lambda j, p: (0, 0))] * (2 * len(chips))
    for n in chips:
        specs.append(
            pl.BlockSpec((2 * width, size), lambda j, p, n=n: (lax.rem(p[0] + n, count), j))
        )
    for n in chips:
        for h in range(heads):
            specs.append(
                pl.BlockSpec(
                    (2 * width, HEAD_DIM),
                    lambda j, p, n=n, h=h: (lax.rem(p[0] + n, count), first + 2 * h),
                )
            )
    block = pl.BlockSpec((rows, size), lambda j, p: (0, j))
    specs.append(block)
    for h in range(heads):
        specs.append(pl.BlockSpec((WIN, HEAD_DIM), lambda j, p, h=h: (rows // WIN - 1, 2 * h + 1)))
    return pl.pallas_call(
        functools.partial(late_kernel, len(chips), heads),
        grid_spec=pltpu.PrefetchScalarGridSpec(
            num_scalar_prefetch=1,
            grid=(columns // size,),
            in_specs=specs,
            out_specs=[block, pl.BlockSpec((heads, WIN, HEAD_DIM), lambda j, p: (0, 0, 0))],
            scratch_shapes=[pltpu.VMEM((rows, 2 * width * len(chips)), BF16)],
        ),
        out_shape=[
            jax.ShapeDtypeStruct((rows, columns), BF16),
            jax.ShapeDtypeStruct((heads, WIN, HEAD_DIM), BF16),
        ],
        compiler_params=params(),
    )(place, *mine, *theirs, *[weight] * (len(chips) * (1 + heads)), before, *[window_before] * heads)


def expansions(heads):
    lanes = -(-heads * 2 * FEAT // LANES) * LANES
    maps = np.zeros((2, heads, lanes, 2 * WIDE), np.float32)
    rows = np.zeros((3, WIDE), np.float32)
    for h in range(heads):
        for side in (0, 1):
            base = h * 2 * FEAT + side * FEAT
            for n, (i, j) in enumerate(PAIRS):
                maps[side, h, base + i, n] = 1.0
                maps[side, h, base + j, WIDE + n] = 1.0
            for i in range(FEAT):
                maps[side, h, base + i, len(PAIRS) + i] = 1.0
    for n, (i, j) in enumerate(PAIRS):
        rows[2, n] = (2.0 * FEAT) ** -0.5 * (1.0 if i == j else 2.0**0.5)
    rows[1, len(PAIRS) : len(PAIRS) + FEAT + 1] = 1.0
    rows[0, len(PAIRS) + FEAT] = 1.0
    rows[2, len(PAIRS) : len(PAIRS) + FEAT] = FEAT**-0.25
    rows[2, len(PAIRS) + FEAT] = 1.0
    return maps.astype(jnp.bfloat16), rows


def picks(heads):
    lanes = -(-heads * 2 * FEAT // LANES) * LANES
    maps = np.zeros((heads, lanes, 256), np.float32)
    for h in range(heads):
        for i in range(FEAT):
            maps[h, h * 2 * FEAT + i, i] = 1.0
            maps[h, h * 2 * FEAT + FEAT + i, 128 + i] = 1.0
    return maps.astype(jnp.bfloat16)


def phi(features, expand, rows):
    factors = jnp.dot(features, expand, preferred_element_type=F32)
    left = factors[:, :WIDE] + rows[0:1]
    right = factors[:, WIDE:] + rows[1:2]
    return (left * right * rows[2:3]).astype(BF16)


def sums_kernel(limits, values, features, expand, rows, keys, prefix, end, both):
    chunks, heads = prefix.shape[:2]
    mark = lax.broadcasted_iota(jnp.int32, (STATE, HEAD_DIM), 0) == STATE - 1
    at = lax.broadcasted_iota(jnp.int32, (CHUNK, HEAD_DIM), 0)
    for h in range(heads):
        column = slice(h * HEAD_DIM, (h + 1) * HEAD_DIM)
        phi_key = phi(features[...], expand[h], rows[...])
        parts = []
        for n in range(chunks):
            here = slice(n * CHUNK, (n + 1) * CHUNK)
            kept = jnp.where(at + n * CHUNK >= limits[n], values[here, column].astype(F32), 0.0)
            parts.append(
                lax.dot_general(
                    phi_key[here], kept.astype(BF16), (((0,), (0,)), ((), ())),
                    preferred_element_type=F32,
                )[:STATE]
            )
        state = jnp.zeros((STATE, HEAD_DIM), F32)
        for n in range(chunks):
            prefix[n, h] = state
            state = parts[n] + jnp.where(limits[n] <= n * CHUNK, state, 0.0)
        sent = jnp.where(mark, (limits[chunks] + 1).astype(F32), state).astype(BF16)
        end[h] = sent
        both[h, :STATE] = sent
        both[h, STATE : STATE + WIN] = values[values.shape[0] - WIN :, column]
        both[h, STATE + WIN :] = keys[h]


def sums(limits, both, keys, expand, rows):
    heads = keys.shape[0]
    chunks = both.shape[0] // CHUNK
    group = min(GROUP, heads)
    count = both.shape[0]
    return pl.pallas_call(
        sums_kernel,
        grid_spec=pltpu.PrefetchScalarGridSpec(
            num_scalar_prefetch=1,
            grid=(heads // group,),
            in_specs=[
                pl.BlockSpec((count, group * HEAD_DIM), lambda g, _: (0, g)),
                pl.BlockSpec((count, LANES), lambda g, _: (0, heads)),
                pl.BlockSpec((group,) + expand.shape[1:], lambda g, _: (g, 0, 0)),
                pl.BlockSpec(rows.shape, lambda g, _: (0, 0)),
                pl.BlockSpec((group, WIN, HEAD_DIM), lambda g, _: (g, 0, 0)),
            ],
            out_specs=[
                pl.BlockSpec((chunks, group, STATE, HEAD_DIM), lambda g, _: (0, g, 0, 0)),
                pl.BlockSpec((group, STATE, HEAD_DIM), lambda g, _: (g, 0, 0)),
                pl.BlockSpec((group, SENT, HEAD_DIM), lambda g, _: (g, 0, 0)),
            ],
        ),
        out_shape=[
            jax.ShapeDtypeStruct((chunks, heads, STATE, HEAD_DIM), F32),
            jax.ShapeDtypeStruct((heads, STATE, HEAD_DIM), BF16),
            jax.ShapeDtypeStruct((heads, SENT, HEAD_DIM), BF16),
        ],
        compiler_params=params(),
    )(limits, both, both, expand, rows, keys)


def windows(tiles):
    wide = TILE + WIN
    logits = jnp.concatenate(
        [
            lax.dot_general(q, k, (((1,), (1,)), ((), ())), preferred_element_type=F32)
            for q, k, _, _, _ in tiles
        ],
        0,
    )
    at = lax.broadcasted_iota(jnp.int32, (TILE, wide), 1)
    row = lax.broadcasted_iota(jnp.int32, (TILE, wide), 0)
    near = (at <= row + WIN) & (at > row)
    good = jnp.concatenate([near & (at >= first - start) for _, _, _, first, start in tiles], 0)
    logits = jnp.where(good, logits * HEAD_DIM**-0.5, -1e30)
    top = jnp.max(logits, 1, keepdims=True)
    weight = jnp.where(good, jnp.exp(logits - top), 0.0)
    probs = (weight / jnp.sum(weight, 1, keepdims=True)).astype(BF16)
    return [
        jnp.dot(probs[n * TILE : (n + 1) * TILE], tile[2], preferred_element_type=F32)
        for n, tile in enumerate(tiles)
    ]


def mix_kernel(
    shifts, limits, values, features, window, bounds, pick, expand, rows, prefix, tail_docs, first_doc, *refs
):
    states, outs = refs[:shifts], refs[shifts:]
    count = values.shape[0]
    half = count // 2

    pair = jnp.dot(features[...], pick[0], preferred_element_type=F32).astype(BF16)
    phi_query = phi(features[...], expand[0], rows[...])
    chunks = count // CHUNK
    at = lax.broadcasted_iota(jnp.int32, (CHUNK, CHUNK), 1)
    row = lax.broadcasted_iota(jnp.int32, (CHUNK, CHUNK), 0)
    dots, good = [], []
    for n in range(chunks):
        here = slice(n * CHUNK, (n + 1) * CHUNK)
        dots.append(
            lax.dot_general(
                pair[here, :128], pair[here, 128:], (((1,), (1,)), ((), ())),
                preferred_element_type=F32,
            )
        )
        good.append((at <= row) & (at >= bounds[here] - n * CHUNK))
    dots, good = jnp.concatenate(dots, 0), jnp.concatenate(good, 0)
    score = dots * (dots * (0.5 / FEAT) + FEAT**-0.5) + 1.0
    score = jnp.where(good, score, 0.0).astype(BF16)

    same = jnp.where(tail_docs[...].astype(F32) == first_doc[0:1, :] + 1.0, 1.0, 0.0)
    in_tail = jnp.sum(same, 0, keepdims=True)[:, 0:1].astype(jnp.int32)
    tiles = []
    for n in range(count // TILE):
        near = slice(n * TILE - WIN, (n + 1) * TILE)
        first = bounds[n * TILE : (n + 1) * TILE]
        if n:
            keys, vals = window[near, HEAD_DIM:], values[near]
        else:
            keys = jnp.concatenate([states[0][0, STATE + WIN :], window[:TILE, HEAD_DIM:]], 0)
            vals = jnp.concatenate([states[0][0, STATE : STATE + WIN], values[:TILE]], 0)
            first = jnp.where(first == 0, -in_tail, first)
        tiles.append(
            (window[n * TILE : (n + 1) * TILE, :HEAD_DIM], keys, vals, first, n * TILE - WIN)
        )
    windowed = jnp.concatenate(windows(tiles), 0)

    unmarked = lax.broadcasted_iota(jnp.int32, (STATE, HEAD_DIM), 0) < STATE - 1
    incoming = jnp.zeros((STATE, HEAD_DIM), F32)
    for k in range(shifts):
        sent = states[k][0, :STATE].astype(F32)
        wanted = (sent[STATE - 1 :] == first_doc[0:1, :] + 1.0) & unmarked
        incoming += jnp.where(wanted, sent, 0.0)
    linear = []
    for n in range(chunks):
        here = slice(n * CHUNK, (n + 1) * CHUNK)
        state = incoming
        if n:
            state = jnp.where(limits[n - 1] <= 0, incoming, 0.0) + prefix[n, 0]
        state = jnp.concatenate([state, jnp.zeros((WIDE - STATE, HEAD_DIM), F32)], 0)
        carried = jnp.dot(phi_query[here], state.astype(BF16), preferred_element_type=F32)
        inner = jnp.dot(score[here], values[here], preferred_element_type=F32)
        linear.append(inner + jnp.where(bounds[here] <= n * CHUNK, carried, 0.0))
    linear = jnp.concatenate(linear, 0)
    mean = jnp.mean(linear * linear, 1, keepdims=True)
    mixed = (linear * lax.rsqrt(mean + 1e-5) + windowed).astype(BF16)
    outs[0][...] = mixed[:half]
    outs[1][...] = mixed[half:]


def mix(limits, both, window, bounds, pick, expand, rows, prefix, tail_docs, first_doc, states):
    count = both.shape[0]
    heads = states[0].shape[0]
    half = count // 2

    def full(a):
        return pl.BlockSpec(a.shape, lambda h, _: (0,) * a.ndim)

    def per_head(a):
        return pl.BlockSpec((1,) + a.shape[1:], lambda h, _: (h, 0, 0))

    return pl.pallas_call(
        functools.partial(mix_kernel, len(states)),
        grid_spec=pltpu.PrefetchScalarGridSpec(
            num_scalar_prefetch=1,
            grid=(heads,),
            in_specs=[
                pl.BlockSpec((count, HEAD_DIM), lambda h, _: (0, h)),
                pl.BlockSpec((count, LANES), lambda h, _: (0, heads)),
                pl.BlockSpec((count, 2 * HEAD_DIM), lambda h, _: (0, h)),
                full(bounds), per_head(pick), per_head(expand), full(rows),
                pl.BlockSpec((prefix.shape[0], 1, STATE, HEAD_DIM), lambda h, _: (0, h, 0, 0)),
                full(tail_docs), full(first_doc),
            ]
            + [per_head(a) for a in states],
            out_specs=[pl.BlockSpec((half, HEAD_DIM), lambda h, _: (0, h))] * 2,
        ),
        out_shape=[jax.ShapeDtypeStruct((half, heads * HEAD_DIM), BF16)] * 2,
        compiler_params=params(40 * 1024 * 1024),
    )(limits, both, both, window, bounds, pick, expand, rows, prefix, tail_docs, first_doc, *states)


def after(x, *others):
    return lax.optimization_barrier((x, *others))[0]


def shards(tokens, doc_ids, w_feat, w_value, w_window, w_out):
    rows = tokens.shape[0]
    chunks = rows // CHUNK
    value_columns = w_value.shape[1]
    heads = value_columns // HEAD_DIM
    count = lax.axis_size("head") // 2
    blocks = lax.axis_size("ctx")
    me = lax.axis_index("head")
    z, c = me // 2, me % 2
    place = jnp.stack([z, c]).astype(jnp.int32)

    pieces = {0: tokens, 1: ring(tokens, -1, count), count - 1: ring(tokens, 1, count)}
    tokens_there = swap(tokens, count)

    docs = doc_ids.astype(F32)
    ends = jnp.concatenate([docs[CHUNK::CHUNK], docs[rows - 1 :]])
    limits = jnp.sum((docs[None, :] < ends[:, None]).astype(F32), 1).astype(jnp.int32)
    limits = jnp.concatenate([limits, doc_ids[rows - 1 :]])
    first = jnp.sum((docs[None, :] < docs[:, None]).astype(F32), 1, keepdims=True)
    bounds = first.astype(jnp.int32)
    first_doc = jnp.broadcast_to(docs[:1], (8, HEAD_DIM))
    tail_docs = jnp.broadcast_to((docs[rows - WIN :] + 1.0).astype(BF16)[:, None], (WIN, HEAD_DIM))
    onward = [(i, i + 1) for i in range(blocks - 1)]
    tail_docs = lax.ppermute(tail_docs, "ctx", onward)

    maps, scale_rows = expansions(heads)
    query_map, key_map = jnp.asarray(maps[0]), jnp.asarray(maps[1])
    scale_rows = jnp.asarray(scale_rows)
    pick = jnp.asarray(picks(heads))

    depth, columns = w_out.shape
    width = columns // (2 * count)

    rows_out = after(w_out, tokens_there)

    def cut(chip, core):
        return lax.dynamic_slice(rows_out, (0, (2 * chip + core) * width), (depth, width))

    other_rows = swap(jnp.stack([cut(chip, 1 - c) for chip in range(count)]), count)
    out_rows = []
    for n in range(count):
        chip = lax.rem(z + n, count)
        theirs = lax.dynamic_index_in_dim(other_rows, chip, 0, keepdims=False)
        out_rows += [cut(chip, c), theirs]

    used = value_columns + w_feat.shape[1]
    fv_columns = -(-used // 256) * 256
    weight = jnp.concatenate(
        [w_value, w_feat, jnp.zeros((w_value.shape[0], fv_columns - used), BF16), w_window], 1
    )
    all_columns = weight.shape[1]
    widths = (fv_columns, all_columns - fv_columns)
    part = project(place, (0,), [tokens], [tokens_there], weight, 0, widths)

    ready = lax.optimization_barrier(
        (pieces[1], pieces[count - 1], limits, bounds, first_doc, tail_docs, *part, *out_rows)
    )
    pieces[1], pieces[count - 1], limits, bounds, first_doc, tail_docs = ready[:6]
    part, out_rows = ready[6:8], ready[8:]

    for n in range(2, count // 2 + 1):
        pieces[n] = ring(pieces[n - 1], -1, count)
    for n in range(count - 2, count // 2, -1):
        pieces[n] = ring(pieces[n + 1], 1, count)
    near = (1, count - 1)
    mine = [pieces[n] for n in near]
    part = project(
        place, near, mine, [swap(p, count) for p in mine], weight, 0, widths, part
    )
    late = tuple(range(2, count - 1))
    *mine, fv_part, win_part = lax.optimization_barrier((*[pieces[n] for n in late], *part))
    theirs = [swap(p, count) for p in mine]
    both, keys = project_late(place, late, mine, theirs, weight, heads, fv_part, win_part)
    prefix, state, state_and_tail = sums(limits, both, keys, key_map, scale_rows)
    states = [
        lax.ppermute(
            state_and_tail if k == 1 else state, "ctx", [(i, i + k) for i in range(blocks - k)]
        )
        for k in range(1, blocks)
    ]
    (window,) = project(
        place, late, [after(mine[0], state), *mine[1:]], theirs, weight, fv_columns, widths[1:],
        [win_part], BF16, 40 * 1024 * 1024,
    )
    low, high = mix(
        limits, both, window, bounds, pick, query_map, scale_rows, prefix, tail_docs, first_doc, states
    )

    def scattered(mixed, step):
        swapped = swap(mixed, count)
        sent = None
        for n in range(1, count + 1):
            at = 2 * (-step * n % count)
            total = jnp.dot(mixed, out_rows[at], preferred_element_type=F32)
            total += jnp.dot(swapped, out_rows[at + 1], preferred_element_type=F32)
            if sent is not None:
                total += ring(sent, step, count).astype(F32)
            sent = total.astype(BF16)
        return sent

    high_out = scattered(high, -1)
    low_out = scattered(low, 1)
    return jnp.concatenate([low_out, high_out], 0)


def solution(mesh):
    return jax.shard_map(
        shards,
        mesh=mesh,
        in_specs=(
            P("ctx", "head"),
            P("ctx"),
            P(None, "head"),
            P(None, "head"),
            P(None, "head"),
            P("head", None),
        ),
        out_specs=P("ctx", "head"),
        check_vma=False,
    )
```

```python
import functools

import jax
import jax.numpy as jnp
import numpy as np
from jax import lax
from jax.experimental import pallas as pl
from jax.experimental.pallas import tpu as pltpu
from jax.sharding import PartitionSpec as P

HEAD_DIM = 128
FEAT = 16
WIN = 64
PAIRS = [(i, j) for i in range(FEAT) for j in range(i, FEAT)]
WIDE = 256
CHUNK = 256
GROUP = 4
STATE = -(-(len(PAIRS) + FEAT + 1) // 16) * 16
SENT = STATE + 2 * WIN
VMEM = 24 * 1024 * 1024
TILE = 128
LANES = 128
F32 = jnp.float32
BF16 = jnp.bfloat16


def params(limit=VMEM):
    return pltpu.CompilerParams(vmem_limit_bytes=limit, dimension_semantics=("arbitrary",))


def ring(x, step, count):
    return lax.ppermute(
        x, "head", [(2 * z + c, 2 * ((z + step) % count) + c) for z in range(count) for c in (0, 1)]
    )


def swap(x, count):
    return lax.ppermute(x, "head", [(h, h ^ 1) for h in range(2 * count)])


def by_column(c, mine, theirs, both):
    width = mine[0].shape[1]
    for n in range(len(mine)):
        own = pl.multiple_of((2 * n + c) * width, width)
        other = pl.multiple_of((2 * n + 1 - c) * width, width)
        both[:, pl.ds(own, width)] = mine[n][...]
        both[:, pl.ds(other, width)] = theirs[n][...]


def project_kernel(chips, cuts, has_before, place, *refs):
    mine, theirs, weights = refs[:chips], refs[chips : 2 * chips], refs[2 * chips : 3 * chips]
    before = refs[3 * chips : 3 * chips + len(cuts)] if has_before else None
    outs, both = refs[-1 - len(cuts) : -1], refs[-1]
    width = mine[0].shape[1]
    c = place[1]
    step = pl.program_id(0)

    @pl.when(step == 0)
    def _():
        by_column(c, mine, theirs, both)

    def tile(k):
        total = before[k][...] if has_before else None
        for n in range(chips):
            rows = both[:, 2 * n * width : 2 * (n + 1) * width]
            part = jnp.dot(rows, weights[n][...], preferred_element_type=F32)
            total = part if total is None else total + part
        outs[k][...] = total.astype(outs[k].dtype)

    if len(cuts) == 1:
        tile(0)
    else:

        @pl.when(step < cuts[0])
        def _():
            tile(0)

        @pl.when(step >= cuts[0])
        def _():
            tile(1)


def project(place, chips, mine, theirs, weight, first, columns, before=None, dtype=F32, limit=VMEM):
    rows, width = mine[0].shape
    count = weight.shape[0] // (2 * width)
    size = 256
    start = first // size
    cuts = [n // size for n in columns]
    specs = [pl.BlockSpec((rows, width), lambda j, p: (0, 0))] * (2 * len(chips))
    for n in chips:
        specs.append(
            pl.BlockSpec(
                (2 * width, size), lambda j, p, n=n: (lax.rem(p[0] + n, count), start + j)
            )
        )
    results = [
        pl.BlockSpec(
            (rows, size),
            lambda j, p, at=sum(cuts[:k]), n=cuts[k]: (0, jnp.clip(j - at, 0, n - 1)),
        )
        for k in range(len(cuts))
    ]
    args = [*mine, *theirs] + [weight] * len(chips)
    if before is not None:
        specs += results
        args += before
    shapes = [jax.ShapeDtypeStruct((rows, n), dtype) for n in columns]
    return pl.pallas_call(
        functools.partial(project_kernel, len(chips), cuts, before is not None),
        grid_spec=pltpu.PrefetchScalarGridSpec(
            num_scalar_prefetch=1,
            grid=(sum(cuts),),
            in_specs=specs,
            out_specs=results,
            scratch_shapes=[pltpu.VMEM((rows, 2 * width * len(chips)), BF16)],
        ),
        out_shape=shapes,
        compiler_params=params(limit),
    )(place, *args)


def late_kernel(chips, place, limits, *refs):
    mine, theirs, weights = refs[:chips], refs[chips : 2 * chips], refs[2 * chips : 3 * chips]
    out, prefix, end, with_tail, both = refs[-5:]
    chunks, heads = prefix.shape[:2]
    key_weights = refs[3 * chips : (3 + heads) * chips]
    before, *key_before = refs[(3 + heads) * chips : (3 + heads) * chips + 1 + heads]
    expand, rows = refs[-7:-5]
    width = 2 * mine[0].shape[1]
    size = before.shape[1]
    step = pl.program_id(0)

    @pl.when(step == 0)
    def _():
        by_column(place[1], mine, theirs, both)

    total = before[...]
    for n in range(chips):
        piece = both[:, n * width : (n + 1) * width]
        total += jnp.dot(piece, weights[n][...], preferred_element_type=F32)
    out[:, pl.ds(pl.multiple_of(step * size, size), size)] = total.astype(BF16)

    @pl.when(step == pl.num_programs(0) - 1)
    def _():
        last = slice(out.shape[0] - WIN, out.shape[0])
        features = out[:, heads * HEAD_DIM : heads * HEAD_DIM + LANES]
        mark = lax.broadcasted_iota(jnp.int32, (STATE, HEAD_DIM), 0) == STATE - 1
        at = lax.broadcasted_iota(jnp.int32, (CHUNK, HEAD_DIM), 0)
        for h in range(heads):
            tail = key_before[h][...]
            for n in range(chips):
                tail += jnp.dot(
                    both[last, n * width : (n + 1) * width], key_weights[n * heads + h][...],
                    preferred_element_type=F32,
                )
            column = slice(h * HEAD_DIM, (h + 1) * HEAD_DIM)
            phi_key = phi(features, expand[h], rows[...])
            parts = []
            for n in range(chunks):
                here = slice(n * CHUNK, (n + 1) * CHUNK)
                kept = jnp.where(at + n * CHUNK >= limits[n], out[here, column].astype(F32), 0.0)
                parts.append(
                    lax.dot_general(
                        phi_key[here], kept.astype(BF16), (((0,), (0,)), ((), ())),
                        preferred_element_type=F32,
                    )[:STATE]
                )
            state = jnp.zeros((STATE, HEAD_DIM), F32)
            for n in range(chunks):
                prefix[n, h] = state
                state = parts[n] + jnp.where(limits[n] <= n * CHUNK, state, 0.0)
            sent = jnp.where(mark, (limits[chunks] + 1).astype(F32), state).astype(BF16)
            end[h] = sent
            with_tail[h, :STATE] = sent
            with_tail[h, STATE : STATE + WIN] = out[last, column]
            with_tail[h, STATE + WIN :] = tail.astype(BF16)


def project_late(place, limits, chips, mine, theirs, weight, heads, before, window_before, expand, rows):
    count, width = mine[0].shape
    ring_size = weight.shape[0] // (2 * width)
    columns = before.shape[1]
    size = 256
    first = columns // HEAD_DIM + 1

    def full(a):
        return pl.BlockSpec(a.shape, lambda j, *_: (0,) * len(a.shape))

    specs = [full(mine[0])] * (2 * len(chips))
    for n in chips:
        specs.append(
            pl.BlockSpec((2 * width, size), lambda j, p, _, n=n: (lax.rem(p[0] + n, ring_size), j))
        )
    for n in chips:
        for h in range(heads):
            specs.append(
                pl.BlockSpec(
                    (2 * width, HEAD_DIM),
                    lambda j, p, _, n=n, h=h: (lax.rem(p[0] + n, ring_size), first + 2 * h),
                )
            )
    specs.append(pl.BlockSpec((count, size), lambda j, *_: (0, j)))
    for h in range(heads):
        specs.append(pl.BlockSpec((WIN, HEAD_DIM), lambda j, *_, h=h: (count // WIN - 1, 2 * h + 1)))
    specs += [full(expand), full(rows)]
    shapes = [
        jax.ShapeDtypeStruct((count, columns), BF16),
        jax.ShapeDtypeStruct((count // CHUNK, heads, STATE, HEAD_DIM), F32),
        jax.ShapeDtypeStruct((heads, STATE, HEAD_DIM), BF16),
        jax.ShapeDtypeStruct((heads, SENT, HEAD_DIM), BF16),
    ]
    return pl.pallas_call(
        functools.partial(late_kernel, len(chips)),
        grid_spec=pltpu.PrefetchScalarGridSpec(
            num_scalar_prefetch=2,
            grid=(columns // size,),
            in_specs=specs,
            out_specs=[full(a) for a in shapes],
            scratch_shapes=[pltpu.VMEM((count, 2 * width * len(chips)), BF16)],
        ),
        out_shape=shapes,
        compiler_params=params(50 * 1024 * 1024),
    )(place, limits, *mine, *theirs, *[weight] * (len(chips) * (1 + heads)), before,
      *[window_before] * heads, expand, rows)


def expansions(heads):
    lanes = -(-heads * 2 * FEAT // LANES) * LANES
    maps = np.zeros((2, heads, lanes, 2 * WIDE), np.float32)
    rows = np.zeros((3, WIDE), np.float32)
    for h in range(heads):
        for side in (0, 1):
            base = h * 2 * FEAT + side * FEAT
            for n, (i, j) in enumerate(PAIRS):
                maps[side, h, base + i, n] = 1.0
                maps[side, h, base + j, WIDE + n] = 1.0
            for i in range(FEAT):
                maps[side, h, base + i, len(PAIRS) + i] = 1.0
    for n, (i, j) in enumerate(PAIRS):
        rows[2, n] = (2.0 * FEAT) ** -0.5 * (1.0 if i == j else 2.0**0.5)
    rows[1, len(PAIRS) : len(PAIRS) + FEAT + 1] = 1.0
    rows[0, len(PAIRS) + FEAT] = 1.0
    rows[2, len(PAIRS) : len(PAIRS) + FEAT] = FEAT**-0.25
    rows[2, len(PAIRS) + FEAT] = 1.0
    return maps.astype(jnp.bfloat16), rows


def picks(heads):
    lanes = -(-heads * 2 * FEAT // LANES) * LANES
    maps = np.zeros((heads, lanes, 256), np.float32)
    for h in range(heads):
        for i in range(FEAT):
            maps[h, h * 2 * FEAT + i, i] = 1.0
            maps[h, h * 2 * FEAT + FEAT + i, 128 + i] = 1.0
    return maps.astype(jnp.bfloat16)


def phi(features, expand, rows):
    factors = jnp.dot(features, expand, preferred_element_type=F32)
    left = factors[:, :WIDE] + rows[0:1]
    right = factors[:, WIDE:] + rows[1:2]
    return (left * right * rows[2:3]).astype(BF16)


def windows(tiles):
    wide = TILE + WIN
    logits = jnp.concatenate(
        [
            lax.dot_general(q, k, (((1,), (1,)), ((), ())), preferred_element_type=F32)
            for q, k, _, _, _ in tiles
        ],
        0,
    )
    at = lax.broadcasted_iota(jnp.int32, (TILE, wide), 1)
    row = lax.broadcasted_iota(jnp.int32, (TILE, wide), 0)
    near = (at <= row + WIN) & (at > row)
    good = jnp.concatenate([near & (at >= first - start) for _, _, _, first, start in tiles], 0)
    logits = jnp.where(good, logits * HEAD_DIM**-0.5, -1e30)
    top = jnp.max(logits, 1, keepdims=True)
    weight = jnp.where(good, jnp.exp(logits - top), 0.0)
    probs = (weight / jnp.sum(weight, 1, keepdims=True)).astype(BF16)
    return [
        jnp.dot(probs[n * TILE : (n + 1) * TILE], tile[2], preferred_element_type=F32)
        for n, tile in enumerate(tiles)
    ]


def mix_kernel(
    shifts, limits, values, features, window, bounds, pick, expand, rows, prefix, tail_docs, first_doc, *refs
):
    states, outs = refs[:shifts], refs[shifts:]
    count = values.shape[0]
    half = count // 2

    pair = jnp.dot(features[...], pick[0], preferred_element_type=F32).astype(BF16)
    phi_query = phi(features[...], expand[0], rows[...])
    chunks = count // CHUNK
    at = lax.broadcasted_iota(jnp.int32, (CHUNK, CHUNK), 1)
    row = lax.broadcasted_iota(jnp.int32, (CHUNK, CHUNK), 0)
    dots, good = [], []
    for n in range(chunks):
        here = slice(n * CHUNK, (n + 1) * CHUNK)
        dots.append(
            lax.dot_general(
                pair[here, :128], pair[here, 128:], (((1,), (1,)), ((), ())),
                preferred_element_type=F32,
            )
        )
        good.append((at <= row) & (at >= bounds[here] - n * CHUNK))
    dots, good = jnp.concatenate(dots, 0), jnp.concatenate(good, 0)
    score = dots * (dots * (0.5 / FEAT) + FEAT**-0.5) + 1.0
    score = jnp.where(good, score, 0.0).astype(BF16)

    same = jnp.where(tail_docs[...].astype(F32) == first_doc[0:1, :] + 1.0, 1.0, 0.0)
    in_tail = jnp.sum(same, 0, keepdims=True)[:, 0:1].astype(jnp.int32)
    tiles = []
    for n in range(count // TILE):
        near = slice(n * TILE - WIN, (n + 1) * TILE)
        first = bounds[n * TILE : (n + 1) * TILE]
        if n:
            keys, vals = window[near, HEAD_DIM:], values[near]
        else:
            keys = jnp.concatenate([states[0][0, STATE + WIN :], window[:TILE, HEAD_DIM:]], 0)
            vals = jnp.concatenate([states[0][0, STATE : STATE + WIN], values[:TILE]], 0)
            first = jnp.where(first == 0, -in_tail, first)
        tiles.append(
            (window[n * TILE : (n + 1) * TILE, :HEAD_DIM], keys, vals, first, n * TILE - WIN)
        )
    windowed = jnp.concatenate(windows(tiles), 0)

    unmarked = lax.broadcasted_iota(jnp.int32, (STATE, HEAD_DIM), 0) < STATE - 1
    incoming = jnp.zeros((STATE, HEAD_DIM), F32)
    for k in range(shifts):
        sent = states[k][0, :STATE].astype(F32)
        wanted = (sent[STATE - 1 :] == first_doc[0:1, :] + 1.0) & unmarked
        incoming += jnp.where(wanted, sent, 0.0)
    linear = []
    for n in range(chunks):
        here = slice(n * CHUNK, (n + 1) * CHUNK)
        state = incoming
        if n:
            state = jnp.where(limits[n - 1] <= 0, incoming, 0.0) + prefix[n, 0]
        state = jnp.concatenate([state, jnp.zeros((WIDE - STATE, HEAD_DIM), F32)], 0)
        carried = jnp.dot(phi_query[here], state.astype(BF16), preferred_element_type=F32)
        inner = jnp.dot(score[here], values[here], preferred_element_type=F32)
        linear.append(inner + jnp.where(bounds[here] <= n * CHUNK, carried, 0.0))
    linear = jnp.concatenate(linear, 0)
    mean = jnp.mean(linear * linear, 1, keepdims=True)
    mixed = (linear * lax.rsqrt(mean + 1e-5) + windowed).astype(BF16)
    outs[0][...] = mixed[:half]
    outs[1][...] = mixed[half:]


def mix(limits, both, window, bounds, pick, expand, rows, prefix, tail_docs, first_doc, states):
    count = both.shape[0]
    heads = states[0].shape[0]
    half = count // 2

    def full(a):
        return pl.BlockSpec(a.shape, lambda h, _: (0,) * a.ndim)

    def per_head(a):
        return pl.BlockSpec((1,) + a.shape[1:], lambda h, _: (h, 0, 0))

    return pl.pallas_call(
        functools.partial(mix_kernel, len(states)),
        grid_spec=pltpu.PrefetchScalarGridSpec(
            num_scalar_prefetch=1,
            grid=(heads,),
            in_specs=[
                pl.BlockSpec((count, HEAD_DIM), lambda h, _: (0, h)),
                pl.BlockSpec((count, LANES), lambda h, _: (0, heads)),
                pl.BlockSpec((count, 2 * HEAD_DIM), lambda h, _: (0, h)),
                full(bounds), per_head(pick), per_head(expand), full(rows),
                pl.BlockSpec((prefix.shape[0], 1, STATE, HEAD_DIM), lambda h, _: (0, h, 0, 0)),
                full(tail_docs), full(first_doc),
            ]
            + [per_head(a) for a in states],
            out_specs=[pl.BlockSpec((half, HEAD_DIM), lambda h, _: (0, h))] * 2,
        ),
        out_shape=[jax.ShapeDtypeStruct((half, heads * HEAD_DIM), BF16)] * 2,
        compiler_params=params(40 * 1024 * 1024),
    )(limits, both, both, window, bounds, pick, expand, rows, prefix, tail_docs, first_doc, *states)


def after(x, *others):
    return lax.optimization_barrier((x, *others))[0]


def shards(tokens, doc_ids, w_feat, w_value, w_window, w_out):
    rows = tokens.shape[0]
    chunks = rows // CHUNK
    value_columns = w_value.shape[1]
    heads = value_columns // HEAD_DIM
    count = lax.axis_size("head") // 2
    blocks = lax.axis_size("ctx")
    me = lax.axis_index("head")
    z, c = me // 2, me % 2
    place = jnp.stack([z, c]).astype(jnp.int32)

    pieces = {0: tokens, 1: ring(tokens, -1, count), count - 1: ring(tokens, 1, count)}
    tokens_there = swap(tokens, count)

    docs = doc_ids.astype(F32)
    ends = jnp.concatenate([docs[CHUNK::CHUNK], docs[rows - 1 :]])
    limits = jnp.sum((docs[None, :] < ends[:, None]).astype(F32), 1).astype(jnp.int32)
    limits = jnp.concatenate([limits, doc_ids[rows - 1 :]])
    first = jnp.sum((docs[None, :] < docs[:, None]).astype(F32), 1, keepdims=True)
    bounds = first.astype(jnp.int32)
    first_doc = jnp.broadcast_to(docs[:1], (8, HEAD_DIM))
    tail_docs = jnp.broadcast_to((docs[rows - WIN :] + 1.0).astype(BF16)[:, None], (WIN, HEAD_DIM))
    onward = [(i, i + 1) for i in range(blocks - 1)]
    tail_docs = lax.ppermute(tail_docs, "ctx", onward)

    maps, scale_rows = expansions(heads)
    query_map, key_map = jnp.asarray(maps[0]), jnp.asarray(maps[1])
    scale_rows = jnp.asarray(scale_rows)
    pick = jnp.asarray(picks(heads))

    depth, columns = w_out.shape
    width = columns // (2 * count)

    rows_out = after(w_out, tokens_there)

    def cut(chip, core):
        return lax.dynamic_slice(rows_out, (0, (2 * chip + core) * width), (depth, width))

    other_rows = swap(jnp.stack([cut(chip, 1 - c) for chip in range(count)]), count)
    out_rows = []
    for n in range(count):
        chip = lax.rem(z + n, count)
        theirs = lax.dynamic_index_in_dim(other_rows, chip, 0, keepdims=False)
        out_rows += [cut(chip, c), theirs]

    used = value_columns + w_feat.shape[1]
    fv_columns = -(-used // 256) * 256
    weight = jnp.concatenate(
        [w_value, w_feat, jnp.zeros((w_value.shape[0], fv_columns - used), BF16), w_window], 1
    )
    all_columns = weight.shape[1]
    widths = (fv_columns, all_columns - fv_columns)
    part = project(place, (0,), [tokens], [tokens_there], weight, 0, widths)

    ready = lax.optimization_barrier(
        (pieces[1], pieces[count - 1], limits, bounds, first_doc, tail_docs, *part, *out_rows)
    )
    pieces[1], pieces[count - 1], limits, bounds, first_doc, tail_docs = ready[:6]
    part, out_rows = ready[6:8], ready[8:]

    for n in range(2, count // 2 + 1):
        pieces[n] = ring(pieces[n - 1], -1, count)
    for n in range(count - 2, count // 2, -1):
        pieces[n] = ring(pieces[n + 1], 1, count)
    near = (1, count - 1)
    mine = [pieces[n] for n in near]
    part = project(
        place, near, mine, [swap(p, count) for p in mine], weight, 0, widths, part
    )
    late = tuple(range(2, count - 1))
    *mine, fv_part, win_part = lax.optimization_barrier((*[pieces[n] for n in late], *part))
    theirs = [swap(p, count) for p in mine]
    both, prefix, state, state_and_tail = project_late(
        place, limits, late, mine, theirs, weight, heads, fv_part, win_part, key_map, scale_rows
    )
    states = [
        lax.ppermute(
            state_and_tail if k == 1 else state, "ctx", [(i, i + k) for i in range(blocks - k)]
        )
        for k in range(1, blocks)
    ]
    (window,) = project(
        place, late, [after(mine[0], state), *mine[1:]], theirs, weight, fv_columns, widths[1:],
        [win_part], BF16, 40 * 1024 * 1024,
    )
    low, high = mix(
        limits, both, window, bounds, pick, query_map, scale_rows, prefix, tail_docs, first_doc, states
    )

    def scattered(mixed, step):
        swapped = swap(mixed, count)
        sent = None
        for n in range(1, count + 1):
            at = 2 * (-step * n % count)
            total = jnp.dot(mixed, out_rows[at], preferred_element_type=F32)
            total += jnp.dot(swapped, out_rows[at + 1], preferred_element_type=F32)
            if sent is not None:
                total += ring(sent, step, count).astype(F32)
            sent = total.astype(BF16)
        return sent

    high_out = scattered(high, -1)
    low_out = scattered(low, 1)
    return jnp.concatenate([low_out, high_out], 0)


def solution(mesh):
    return jax.shard_map(
        shards,
        mesh=mesh,
        in_specs=(
            P("ctx", "head"),
            P("ctx"),
            P(None, "head"),
            P(None, "head"),
            P(None, "head"),
            P("head", None),
        ),
        out_specs=P("ctx", "head"),
        check_vma=False,
    )
```

```python
import functools

import jax
import jax.numpy as jnp
import numpy as np
from jax import lax
from jax.experimental import pallas as pl
from jax.experimental.pallas import tpu as pltpu
from jax.sharding import PartitionSpec as P

HEAD_DIM = 128
FEAT = 16
WIN = 64
PAIRS = [(i, j) for i in range(FEAT) for j in range(i, FEAT)]
WIDE = 256
CHUNK = 256
GROUP = 4
STATE = -(-(len(PAIRS) + FEAT + 1) // 16) * 16
SENT = STATE + 2 * WIN
VMEM = 24 * 1024 * 1024
TILE = 128
LANES = 128
F32 = jnp.float32
BF16 = jnp.bfloat16


def params(limit=VMEM):
    return pltpu.CompilerParams(vmem_limit_bytes=limit, dimension_semantics=("arbitrary",))


def ring(x, step, count):
    return lax.ppermute(
        x, "head", [(2 * z + c, 2 * ((z + step) % count) + c) for z in range(count) for c in (0, 1)]
    )


def swap(x, count):
    return lax.ppermute(x, "head", [(h, h ^ 1) for h in range(2 * count)])


def by_column(c, mine, theirs, both):
    width = mine[0].shape[1]
    for n in range(len(mine)):
        own = pl.multiple_of((2 * n + c) * width, width)
        other = pl.multiple_of((2 * n + 1 - c) * width, width)
        both[:, pl.ds(own, width)] = mine[n][...]
        both[:, pl.ds(other, width)] = theirs[n][...]


def project_kernel(chips, cuts, has_before, place, *refs):
    mine, theirs, weights = refs[:chips], refs[chips : 2 * chips], refs[2 * chips : 3 * chips]
    before = refs[3 * chips : 3 * chips + len(cuts)] if has_before else None
    outs, both = refs[-1 - len(cuts) : -1], refs[-1]
    width = mine[0].shape[1]
    c = place[1]
    step = pl.program_id(0)

    @pl.when(step == 0)
    def _():
        by_column(c, mine, theirs, both)

    def tile(k):
        total = before[k][...] if has_before else None
        for n in range(chips):
            rows = both[:, 2 * n * width : 2 * (n + 1) * width]
            part = jnp.dot(rows, weights[n][...], preferred_element_type=F32)
            total = part if total is None else total + part
        outs[k][...] = total.astype(outs[k].dtype)

    if len(cuts) == 1:
        tile(0)
    else:

        @pl.when(step < cuts[0])
        def _():
            tile(0)

        @pl.when(step >= cuts[0])
        def _():
            tile(1)


def project(place, chips, mine, theirs, weight, first, columns, before=None, dtype=F32, limit=VMEM):
    rows, width = mine[0].shape
    count = weight.shape[0] // (2 * width)
    size = 256
    start = first // size
    cuts = [n // size for n in columns]
    specs = [pl.BlockSpec((rows, width), lambda j, p: (0, 0))] * (2 * len(chips))
    for n in chips:
        specs.append(
            pl.BlockSpec(
                (2 * width, size), lambda j, p, n=n: (lax.rem(p[0] + n, count), start + j)
            )
        )
    results = [
        pl.BlockSpec(
            (rows, size),
            lambda j, p, at=sum(cuts[:k]), n=cuts[k]: (0, jnp.clip(j - at, 0, n - 1)),
        )
        for k in range(len(cuts))
    ]
    args = [*mine, *theirs] + [weight] * len(chips)
    if before is not None:
        specs += results
        args += before
    shapes = [jax.ShapeDtypeStruct((rows, n), dtype) for n in columns]
    return pl.pallas_call(
        functools.partial(project_kernel, len(chips), cuts, before is not None),
        grid_spec=pltpu.PrefetchScalarGridSpec(
            num_scalar_prefetch=1,
            grid=(sum(cuts),),
            in_specs=specs,
            out_specs=results,
            scratch_shapes=[pltpu.VMEM((rows, 2 * width * len(chips)), BF16)],
        ),
        out_shape=shapes,
        compiler_params=params(limit),
    )(place, *args)


def late_kernel(chips, place, limits, *refs):
    mine, theirs, weights = refs[:chips], refs[chips : 2 * chips], refs[2 * chips : 3 * chips]
    out, prefix, end, with_tail, both = refs[-5:]
    chunks, heads = prefix.shape[:2]
    key_weights = refs[3 * chips : (3 + heads) * chips]
    before, *key_before = refs[(3 + heads) * chips : (3 + heads) * chips + 1 + heads]
    expand, rows = refs[-7:-5]
    width = 2 * mine[0].shape[1]
    size = before.shape[1]
    step = pl.program_id(0)

    @pl.when(step == 0)
    def _():
        by_column(place[1], mine, theirs, both)

    total = before[...]
    for n in range(chips):
        piece = both[:, n * width : (n + 1) * width]
        total += jnp.dot(piece, weights[n][...], preferred_element_type=F32)
    out[:, pl.ds(pl.multiple_of(step * size, size), size)] = total.astype(BF16)

    @pl.when(step == pl.num_programs(0) - 1)
    def _():
        last = slice(out.shape[0] - WIN, out.shape[0])
        features = out[:, heads * HEAD_DIM : heads * HEAD_DIM + LANES]
        mark = lax.broadcasted_iota(jnp.int32, (STATE, HEAD_DIM), 0) == STATE - 1
        at = lax.broadcasted_iota(jnp.int32, (CHUNK, HEAD_DIM), 0)
        for h in range(heads):
            tail = key_before[h][...]
            for n in range(chips):
                tail += jnp.dot(
                    both[last, n * width : (n + 1) * width], key_weights[n * heads + h][...],
                    preferred_element_type=F32,
                )
            column = slice(h * HEAD_DIM, (h + 1) * HEAD_DIM)
            phi_key = phi(features, expand[h], rows[...])
            parts = []
            for n in range(chunks):
                here = slice(n * CHUNK, (n + 1) * CHUNK)
                kept = jnp.where(at + n * CHUNK >= limits[n], out[here, column].astype(F32), 0.0)
                parts.append(
                    lax.dot_general(
                        phi_key[here], kept.astype(BF16), (((0,), (0,)), ((), ())),
                        preferred_element_type=F32,
                    )[:STATE]
                )
            state = jnp.zeros((STATE, HEAD_DIM), F32)
            for n in range(chunks):
                prefix[n, h] = state
                state = parts[n] + jnp.where(limits[n] <= n * CHUNK, state, 0.0)
            sent = jnp.where(mark, (limits[chunks] + 1).astype(F32), state).astype(BF16)
            end[h] = sent
            with_tail[h, :STATE] = sent
            with_tail[h, STATE : STATE + WIN] = out[last, column]
            with_tail[h, STATE + WIN :] = tail.astype(BF16)


def project_late(place, limits, chips, mine, theirs, weight, heads, before, window_before, expand, rows):
    count, width = mine[0].shape
    ring_size = weight.shape[0] // (2 * width)
    columns = before.shape[1]
    size = 256
    first = columns // HEAD_DIM + 1

    def full(a):
        return pl.BlockSpec(a.shape, lambda j, *_: (0,) * len(a.shape))

    specs = [full(mine[0])] * (2 * len(chips))
    for n in chips:
        specs.append(
            pl.BlockSpec((2 * width, size), lambda j, p, _, n=n: (lax.rem(p[0] + n, ring_size), j))
        )
    for n in chips:
        for h in range(heads):
            specs.append(
                pl.BlockSpec(
                    (2 * width, HEAD_DIM),
                    lambda j, p, _, n=n, h=h: (lax.rem(p[0] + n, ring_size), first + 2 * h),
                )
            )
    specs.append(pl.BlockSpec((count, size), lambda j, *_: (0, j)))
    for h in range(heads):
        specs.append(pl.BlockSpec((WIN, HEAD_DIM), lambda j, *_, h=h: (count // WIN - 1, 2 * h + 1)))
    specs += [full(expand), full(rows)]
    shapes = [
        jax.ShapeDtypeStruct((count, columns), BF16),
        jax.ShapeDtypeStruct((count // CHUNK, heads, STATE, HEAD_DIM), F32),
        jax.ShapeDtypeStruct((heads, STATE, HEAD_DIM), BF16),
        jax.ShapeDtypeStruct((heads, SENT, HEAD_DIM), BF16),
    ]
    return pl.pallas_call(
        functools.partial(late_kernel, len(chips)),
        grid_spec=pltpu.PrefetchScalarGridSpec(
            num_scalar_prefetch=2,
            grid=(columns // size,),
            in_specs=specs,
            out_specs=[full(a) for a in shapes],
            scratch_shapes=[pltpu.VMEM((count, 2 * width * len(chips)), BF16)],
        ),
        out_shape=shapes,
        compiler_params=params(50 * 1024 * 1024),
    )(place, limits, *mine, *theirs, *[weight] * (len(chips) * (1 + heads)), before,
      *[window_before] * heads, expand, rows)


def expansions(heads):
    lanes = -(-heads * 2 * FEAT // LANES) * LANES
    maps = np.zeros((2, heads, lanes, 2 * WIDE), np.float32)
    rows = np.zeros((3, WIDE), np.float32)
    for h in range(heads):
        for side in (0, 1):
            base = h * 2 * FEAT + side * FEAT
            for n, (i, j) in enumerate(PAIRS):
                maps[side, h, base + i, n] = 1.0
                maps[side, h, base + j, WIDE + n] = 1.0
            for i in range(FEAT):
                maps[side, h, base + i, len(PAIRS) + i] = 1.0
    for n, (i, j) in enumerate(PAIRS):
        rows[2, n] = (2.0 * FEAT) ** -0.5 * (1.0 if i == j else 2.0**0.5)
    rows[1, len(PAIRS) : len(PAIRS) + FEAT + 1] = 1.0
    rows[0, len(PAIRS) + FEAT] = 1.0
    rows[2, len(PAIRS) : len(PAIRS) + FEAT] = FEAT**-0.25
    rows[2, len(PAIRS) + FEAT] = 1.0
    return maps.astype(jnp.bfloat16), rows


def picks(heads):
    lanes = -(-heads * 2 * FEAT // LANES) * LANES
    maps = np.zeros((heads, lanes, 256), np.float32)
    for h in range(heads):
        for i in range(FEAT):
            maps[h, h * 2 * FEAT + i, i] = 1.0
            maps[h, h * 2 * FEAT + FEAT + i, 128 + i] = 1.0
    return maps.astype(jnp.bfloat16)


def phi(features, expand, rows):
    factors = jnp.dot(features, expand, preferred_element_type=F32)
    left = factors[:, :WIDE] + rows[0:1]
    right = factors[:, WIDE:] + rows[1:2]
    return (left * right * rows[2:3]).astype(BF16)


def windows(tiles):
    wide = TILE + WIN
    logits = jnp.concatenate(
        [
            lax.dot_general(q, k, (((1,), (1,)), ((), ())), preferred_element_type=F32)
            for q, k, _, _, _ in tiles
        ],
        0,
    )
    at = lax.broadcasted_iota(jnp.int32, (TILE, wide), 1)
    row = lax.broadcasted_iota(jnp.int32, (TILE, wide), 0)
    near = (at <= row + WIN) & (at > row)
    good = jnp.concatenate([near & (at >= first - start) for _, _, _, first, start in tiles], 0)
    logits = jnp.where(good, logits * HEAD_DIM**-0.5, -1e30)
    top = jnp.max(logits, 1, keepdims=True)
    weight = jnp.where(good, jnp.exp(logits - top), 0.0)
    probs = (weight / jnp.sum(weight, 1, keepdims=True)).astype(BF16)
    return [
        jnp.dot(probs[n * TILE : (n + 1) * TILE], tile[2], preferred_element_type=F32)
        for n, tile in enumerate(tiles)
    ]


def mix_kernel(
    shifts, limits, values, features, window, bounds, pick, expand, rows, prefix, tail_docs, first_doc, *refs
):
    states, outs = refs[:shifts], refs[shifts:]
    count = values.shape[0]
    half = count // 2

    pair = jnp.dot(features[...], pick[0], preferred_element_type=F32).astype(BF16)
    phi_query = phi(features[...], expand[0], rows[...])
    chunks = count // CHUNK
    at = lax.broadcasted_iota(jnp.int32, (CHUNK, CHUNK), 1)
    row = lax.broadcasted_iota(jnp.int32, (CHUNK, CHUNK), 0)
    dots, good = [], []
    for n in range(chunks):
        here = slice(n * CHUNK, (n + 1) * CHUNK)
        dots.append(
            lax.dot_general(
                pair[here, :128], pair[here, 128:], (((1,), (1,)), ((), ())),
                preferred_element_type=F32,
            )
        )
        good.append((at <= row) & (at >= bounds[here] - n * CHUNK))
    dots, good = jnp.concatenate(dots, 0), jnp.concatenate(good, 0)
    score = dots * (dots * (0.5 / FEAT) + FEAT**-0.5) + 1.0
    score = jnp.where(good, score, 0.0).astype(BF16)

    same = jnp.where(tail_docs[...].astype(F32) == first_doc[0:1, :] + 1.0, 1.0, 0.0)
    in_tail = jnp.sum(same, 0, keepdims=True)[:, 0:1].astype(jnp.int32)
    tiles = []
    for n in range(count // TILE):
        near = slice(n * TILE - WIN, (n + 1) * TILE)
        first = bounds[n * TILE : (n + 1) * TILE]
        if n:
            keys, vals = window[near, HEAD_DIM:], values[near]
        else:
            keys = jnp.concatenate([states[0][0, STATE + WIN :], window[:TILE, HEAD_DIM:]], 0)
            vals = jnp.concatenate([states[0][0, STATE : STATE + WIN], values[:TILE]], 0)
            first = jnp.where(first == 0, -in_tail, first)
        tiles.append(
            (window[n * TILE : (n + 1) * TILE, :HEAD_DIM], keys, vals, first, n * TILE - WIN)
        )
    windowed = jnp.concatenate(windows(tiles), 0)

    unmarked = lax.broadcasted_iota(jnp.int32, (STATE, HEAD_DIM), 0) < STATE - 1
    incoming = jnp.zeros((STATE, HEAD_DIM), F32)
    for k in range(shifts):
        sent = states[k][0, :STATE].astype(F32)
        wanted = (sent[STATE - 1 :] == first_doc[0:1, :] + 1.0) & unmarked
        incoming += jnp.where(wanted, sent, 0.0)
    linear = []
    for n in range(chunks):
        here = slice(n * CHUNK, (n + 1) * CHUNK)
        state = incoming
        if n:
            state = jnp.where(limits[n - 1] <= 0, incoming, 0.0) + prefix[n, 0]
        state = jnp.concatenate([state, jnp.zeros((WIDE - STATE, HEAD_DIM), F32)], 0)
        carried = jnp.dot(phi_query[here], state.astype(BF16), preferred_element_type=F32)
        inner = jnp.dot(score[here], values[here], preferred_element_type=F32)
        linear.append(inner + jnp.where(bounds[here] <= n * CHUNK, carried, 0.0))
    linear = jnp.concatenate(linear, 0)
    mean = jnp.mean(linear * linear, 1, keepdims=True)
    mixed = (linear * lax.rsqrt(mean + 1e-5) + windowed).astype(BF16)
    outs[0][...] = mixed[:half]
    outs[1][...] = mixed[half:]


def mix(limits, both, window, bounds, pick, expand, rows, prefix, tail_docs, first_doc, states):
    count = both.shape[0]
    heads = states[0].shape[0]
    half = count // 2

    def full(a):
        return pl.BlockSpec(a.shape, lambda h, _: (0,) * a.ndim)

    def per_head(a):
        return pl.BlockSpec((1,) + a.shape[1:], lambda h, _: (h, 0, 0))

    return pl.pallas_call(
        functools.partial(mix_kernel, len(states)),
        grid_spec=pltpu.PrefetchScalarGridSpec(
            num_scalar_prefetch=1,
            grid=(heads,),
            in_specs=[
                pl.BlockSpec((count, HEAD_DIM), lambda h, _: (0, h)),
                pl.BlockSpec((count, LANES), lambda h, _: (0, heads)),
                pl.BlockSpec((count, 2 * HEAD_DIM), lambda h, _: (0, h)),
                full(bounds), per_head(pick), per_head(expand), full(rows),
                pl.BlockSpec((prefix.shape[0], 1, STATE, HEAD_DIM), lambda h, _: (0, h, 0, 0)),
                full(tail_docs), full(first_doc),
            ]
            + [per_head(a) for a in states],
            out_specs=[pl.BlockSpec((half, HEAD_DIM), lambda h, _: (0, h))] * 2,
        ),
        out_shape=[jax.ShapeDtypeStruct((half, heads * HEAD_DIM), BF16)] * 2,
        compiler_params=params(40 * 1024 * 1024),
    )(limits, both, both, window, bounds, pick, expand, rows, prefix, tail_docs, first_doc, *states)


def after(x, *others):
    return lax.optimization_barrier((x, *others))[0]


def shards(tokens, doc_ids, w_feat, w_value, w_window, w_out):
    rows = tokens.shape[0]
    chunks = rows // CHUNK
    value_columns = w_value.shape[1]
    heads = value_columns // HEAD_DIM
    count = lax.axis_size("head") // 2
    blocks = lax.axis_size("ctx")
    me = lax.axis_index("head")
    z, c = me // 2, me % 2
    place = jnp.stack([z, c]).astype(jnp.int32)

    pieces = {0: tokens, 1: ring(tokens, -1, count), count - 1: ring(tokens, 1, count)}
    tokens_there = swap(tokens, count)

    docs = doc_ids.astype(F32)
    ends = jnp.concatenate([docs[CHUNK::CHUNK], docs[rows - 1 :]])
    limits = jnp.sum((docs[None, :] < ends[:, None]).astype(F32), 1).astype(jnp.int32)
    limits = jnp.concatenate([limits, doc_ids[rows - 1 :]])
    first = jnp.sum((docs[None, :] < docs[:, None]).astype(F32), 1, keepdims=True)
    bounds = first.astype(jnp.int32)
    tail_docs = jnp.broadcast_to((docs[rows - WIN :] + 1.0).astype(BF16)[:, None], (WIN, HEAD_DIM))
    onward = [(i, i + 1) for i in range(blocks - 1)]
    tail_docs = lax.ppermute(tail_docs, "ctx", onward)

    maps, scale_rows = expansions(heads)
    query_map, key_map = jnp.asarray(maps[0]), jnp.asarray(maps[1])
    scale_rows = jnp.asarray(scale_rows)
    pick = jnp.asarray(picks(heads))

    depth, columns = w_out.shape
    width = columns // (2 * count)

    rows_out = after(w_out, tokens_there)

    def cut(chip, core):
        return lax.dynamic_slice(rows_out, (0, (2 * chip + core) * width), (depth, width))

    other_rows = swap(jnp.stack([cut(chip, 1 - c) for chip in range(count)]), count)
    out_rows = []
    for n in range(count):
        chip = lax.rem(z + n, count)
        theirs = lax.dynamic_index_in_dim(other_rows, chip, 0, keepdims=False)
        out_rows += [cut(chip, c), theirs]

    used = value_columns + w_feat.shape[1]
    fv_columns = -(-used // 256) * 256
    weight = jnp.concatenate(
        [w_value, w_feat, jnp.zeros((w_value.shape[0], fv_columns - used), BF16), w_window], 1
    )
    all_columns = weight.shape[1]
    widths = (fv_columns, all_columns - fv_columns)
    part = project(place, (0,), [tokens], [tokens_there], weight, 0, widths)

    ready = lax.optimization_barrier(
        (pieces[1], pieces[count - 1], limits, bounds, tail_docs, *part, *out_rows)
    )
    pieces[1], pieces[count - 1], limits, bounds, tail_docs = ready[:5]
    part, out_rows = ready[5:7], ready[7:]

    for n in range(2, count // 2 + 1):
        pieces[n] = ring(pieces[n - 1], -1, count)
    for n in range(count - 2, count // 2, -1):
        pieces[n] = ring(pieces[n + 1], 1, count)
    near = (1, count - 1)
    mine = [pieces[n] for n in near]
    part = project(
        place, near, mine, [swap(p, count) for p in mine], weight, 0, widths, part
    )
    late = tuple(range(2, count - 1))
    first_doc = jnp.broadcast_to(after(docs[:1], *part), (8, HEAD_DIM))
    *mine, fv_part, win_part, first_doc = lax.optimization_barrier(
        (*[pieces[n] for n in late], *part, first_doc)
    )
    theirs = [swap(p, count) for p in mine]
    both, prefix, state, state_and_tail = project_late(
        place, limits, late, mine, theirs, weight, heads, fv_part, win_part, key_map, scale_rows
    )
    states = [
        lax.ppermute(
            state_and_tail if k == 1 else state, "ctx", [(i, i + k) for i in range(blocks - k)]
        )
        for k in range(1, blocks)
    ]
    (window,) = project(
        place, late, [after(mine[0], state), *mine[1:]], theirs, weight, fv_columns, widths[1:],
        [win_part], BF16, 40 * 1024 * 1024,
    )
    low, high = mix(
        limits, both, window, bounds, pick, query_map, scale_rows, prefix, tail_docs, first_doc, states
    )

    def scattered(mixed, step):
        swapped = swap(mixed, count)
        sent = None
        for n in range(1, count + 1):
            at = 2 * (-step * n % count)
            total = jnp.dot(mixed, out_rows[at], preferred_element_type=F32)
            total += jnp.dot(swapped, out_rows[at + 1], preferred_element_type=F32)
            if sent is not None:
                total += ring(sent, step, count).astype(F32)
            sent = total.astype(BF16)
        return sent

    high_out = scattered(high, -1)
    low_out = scattered(low, 1)
    return jnp.concatenate([low_out, high_out], 0)


def solution(mesh):
    return jax.shard_map(
        shards,
        mesh=mesh,
        in_specs=(
            P("ctx", "head"),
            P("ctx"),
            P(None, "head"),
            P(None, "head"),
            P(None, "head"),
            P("head", None),
        ),
        out_specs=P("ctx", "head"),
        check_vma=False,
    )
```

```python
import functools

import jax
import jax.numpy as jnp
import numpy as np
from jax import lax
from jax.experimental import pallas as pl
from jax.experimental.pallas import tpu as pltpu
from jax.sharding import PartitionSpec as P

HEAD_DIM = 128
FEAT = 16
WIN = 64
PAIRS = [(i, j) for i in range(FEAT) for j in range(i, FEAT)]
WIDE = 256
CHUNK = 256
GROUP = 4
STATE = -(-(len(PAIRS) + FEAT + 1) // 16) * 16
SENT = STATE + 2 * WIN
VMEM = 24 * 1024 * 1024
TILE = 128
LANES = 128
F32 = jnp.float32
BF16 = jnp.bfloat16


def params(limit=VMEM):
    return pltpu.CompilerParams(vmem_limit_bytes=limit, dimension_semantics=("arbitrary",))


def ring(x, step, count):
    return lax.ppermute(
        x, "head", [(2 * z + c, 2 * ((z + step) % count) + c) for z in range(count) for c in (0, 1)]
    )


def swap(x, count):
    return lax.ppermute(x, "head", [(h, h ^ 1) for h in range(2 * count)])


def by_column(c, mine, theirs, both):
    width = mine[0].shape[1]
    for n in range(len(mine)):
        own = pl.multiple_of((2 * n + c) * width, width)
        other = pl.multiple_of((2 * n + 1 - c) * width, width)
        both[:, pl.ds(own, width)] = mine[n][...]
        both[:, pl.ds(other, width)] = theirs[n][...]


def project_kernel(chips, cuts, has_before, place, *refs):
    mine, theirs, weights = refs[:chips], refs[chips : 2 * chips], refs[2 * chips : 3 * chips]
    before = refs[3 * chips : 3 * chips + len(cuts)] if has_before else None
    outs, both = refs[-1 - len(cuts) : -1], refs[-1]
    width = mine[0].shape[1]
    c = place[1]
    step = pl.program_id(0)

    @pl.when(step == 0)
    def _():
        by_column(c, mine, theirs, both)

    def tile(k):
        total = before[k][...] if has_before else None
        for n in range(chips):
            rows = both[:, 2 * n * width : 2 * (n + 1) * width]
            part = jnp.dot(rows, weights[n][...], preferred_element_type=F32)
            total = part if total is None else total + part
        outs[k][...] = total.astype(outs[k].dtype)

    if len(cuts) == 1:
        tile(0)
    else:

        @pl.when(step < cuts[0])
        def _():
            tile(0)

        @pl.when(step >= cuts[0])
        def _():
            tile(1)


def project(place, chips, mine, theirs, weight, first, columns, before=None, dtype=F32, limit=VMEM):
    rows, width = mine[0].shape
    count = weight.shape[0] // (2 * width)
    size = 256
    start = first // size
    cuts = [n // size for n in columns]
    specs = [pl.BlockSpec((rows, width), lambda j, p: (0, 0))] * (2 * len(chips))
    for n in chips:
        specs.append(
            pl.BlockSpec(
                (2 * width, size), lambda j, p, n=n: (lax.rem(p[0] + n, count), start + j)
            )
        )
    results = [
        pl.BlockSpec(
            (rows, size),
            lambda j, p, at=sum(cuts[:k]), n=cuts[k]: (0, jnp.clip(j - at, 0, n - 1)),
        )
        for k in range(len(cuts))
    ]
    args = [*mine, *theirs] + [weight] * len(chips)
    if before is not None:
        specs += results
        args += before
    shapes = [jax.ShapeDtypeStruct((rows, n), dtype) for n in columns]
    return pl.pallas_call(
        functools.partial(project_kernel, len(chips), cuts, before is not None),
        grid_spec=pltpu.PrefetchScalarGridSpec(
            num_scalar_prefetch=1,
            grid=(sum(cuts),),
            in_specs=specs,
            out_specs=results,
            scratch_shapes=[pltpu.VMEM((rows, 2 * width * len(chips)), BF16)],
        ),
        out_shape=shapes,
        compiler_params=params(limit),
    )(place, *args)


def late_kernel(chips, place, limits, *refs):
    mine, theirs, weights = refs[:chips], refs[chips : 2 * chips], refs[2 * chips : 3 * chips]
    out, prefix, end, with_tail, both = refs[-5:]
    chunks, heads = prefix.shape[:2]
    key_weights = refs[3 * chips : (3 + heads) * chips]
    before, *key_before = refs[(3 + heads) * chips : (3 + heads) * chips + 1 + heads]
    expand, rows = refs[-7:-5]
    width = 2 * mine[0].shape[1]
    size = before.shape[1]
    step = pl.program_id(0)

    @pl.when(step == 0)
    def _():
        by_column(place[1], mine, theirs, both)

    total = before[...]
    for n in range(chips):
        piece = both[:, n * width : (n + 1) * width]
        total += jnp.dot(piece, weights[n][...], preferred_element_type=F32)
    out[:, pl.ds(pl.multiple_of(step * size, size), size)] = total.astype(BF16)

    @pl.when(step == pl.num_programs(0) - 1)
    def _():
        last = slice(out.shape[0] - WIN, out.shape[0])
        features = out[:, heads * HEAD_DIM : heads * HEAD_DIM + LANES]
        mark = lax.broadcasted_iota(jnp.int32, (STATE, HEAD_DIM), 0) == STATE - 1
        at = lax.broadcasted_iota(jnp.int32, (CHUNK, HEAD_DIM), 0)
        for h in range(heads):
            tail = key_before[h][...]
            for n in range(chips):
                tail += jnp.dot(
                    both[last, n * width : (n + 1) * width], key_weights[n * heads + h][...],
                    preferred_element_type=F32,
                )
            column = slice(h * HEAD_DIM, (h + 1) * HEAD_DIM)
            phi_key = phi(features, expand[h], rows[...])
            parts = []
            for n in range(chunks):
                here = slice(n * CHUNK, (n + 1) * CHUNK)
                kept = jnp.where(at + n * CHUNK >= limits[n], out[here, column].astype(F32), 0.0)
                parts.append(
                    lax.dot_general(
                        phi_key[here], kept.astype(BF16), (((0,), (0,)), ((), ())),
                        preferred_element_type=F32,
                    )[:STATE]
                )
            state = jnp.zeros((STATE, HEAD_DIM), F32)
            for n in range(chunks):
                prefix[n, h] = state
                state = parts[n] + jnp.where(limits[n] <= n * CHUNK, state, 0.0)
            sent = jnp.where(mark, (limits[chunks] + 1).astype(F32), state).astype(BF16)
            end[h] = sent
            with_tail[h, :STATE] = sent
            with_tail[h, STATE : STATE + WIN] = out[last, column]
            with_tail[h, STATE + WIN :] = tail.astype(BF16)


def project_late(place, limits, chips, mine, theirs, weight, heads, before, window_before, expand, rows):
    count, width = mine[0].shape
    ring_size = weight.shape[0] // (2 * width)
    columns = before.shape[1]
    size = 256
    first = columns // HEAD_DIM + 1

    def full(a):
        return pl.BlockSpec(a.shape, lambda j, *_: (0,) * len(a.shape))

    specs = [full(mine[0])] * (2 * len(chips))
    for n in chips:
        specs.append(
            pl.BlockSpec((2 * width, size), lambda j, p, _, n=n: (lax.rem(p[0] + n, ring_size), j))
        )
    for n in chips:
        for h in range(heads):
            specs.append(
                pl.BlockSpec(
                    (2 * width, HEAD_DIM),
                    lambda j, p, _, n=n, h=h: (lax.rem(p[0] + n, ring_size), first + 2 * h),
                )
            )
    specs.append(pl.BlockSpec((count, size), lambda j, *_: (0, j)))
    for h in range(heads):
        specs.append(pl.BlockSpec((WIN, HEAD_DIM), lambda j, *_, h=h: (count // WIN - 1, 2 * h + 1)))
    specs += [full(expand), full(rows)]
    shapes = [
        jax.ShapeDtypeStruct((count, columns), BF16),
        jax.ShapeDtypeStruct((count // CHUNK, heads, STATE, HEAD_DIM), F32),
        jax.ShapeDtypeStruct((heads, STATE, HEAD_DIM), BF16),
        jax.ShapeDtypeStruct((heads, SENT, HEAD_DIM), BF16),
    ]
    return pl.pallas_call(
        functools.partial(late_kernel, len(chips)),
        grid_spec=pltpu.PrefetchScalarGridSpec(
            num_scalar_prefetch=2,
            grid=(columns // size,),
            in_specs=specs,
            out_specs=[full(a) for a in shapes],
            scratch_shapes=[pltpu.VMEM((count, 2 * width * len(chips)), BF16)],
        ),
        out_shape=shapes,
        compiler_params=params(50 * 1024 * 1024),
    )(place, limits, *mine, *theirs, *[weight] * (len(chips) * (1 + heads)), before,
      *[window_before] * heads, expand, rows)


def expansions(heads):
    lanes = -(-heads * 2 * FEAT // LANES) * LANES
    maps = np.zeros((2, heads, lanes, 2 * WIDE), np.float32)
    rows = np.zeros((3, WIDE), np.float32)
    for h in range(heads):
        for side in (0, 1):
            base = h * 2 * FEAT + side * FEAT
            for n, (i, j) in enumerate(PAIRS):
                maps[side, h, base + i, n] = 1.0
                maps[side, h, base + j, WIDE + n] = 1.0
            for i in range(FEAT):
                maps[side, h, base + i, len(PAIRS) + i] = 1.0
    for n, (i, j) in enumerate(PAIRS):
        rows[2, n] = (2.0 * FEAT) ** -0.5 * (1.0 if i == j else 2.0**0.5)
    rows[1, len(PAIRS) : len(PAIRS) + FEAT + 1] = 1.0
    rows[0, len(PAIRS) + FEAT] = 1.0
    rows[2, len(PAIRS) : len(PAIRS) + FEAT] = FEAT**-0.25
    rows[2, len(PAIRS) + FEAT] = 1.0
    return maps.astype(jnp.bfloat16), rows


def picks(heads):
    lanes = -(-heads * 2 * FEAT // LANES) * LANES
    maps = np.zeros((heads, lanes, 256), np.float32)
    for h in range(heads):
        for i in range(FEAT):
            maps[h, h * 2 * FEAT + i, i] = 1.0
            maps[h, h * 2 * FEAT + FEAT + i, 128 + i] = 1.0
    return maps.astype(jnp.bfloat16)


def phi(features, expand, rows):
    factors = jnp.dot(features, expand, preferred_element_type=F32)
    left = factors[:, :WIDE] + rows[0:1]
    right = factors[:, WIDE:] + rows[1:2]
    return (left * right * rows[2:3]).astype(BF16)


def windows(tiles):
    wide = TILE + WIN
    logits = jnp.concatenate(
        [
            lax.dot_general(q, k, (((1,), (1,)), ((), ())), preferred_element_type=F32)
            for q, k, _, _, _ in tiles
        ],
        0,
    )
    at = lax.broadcasted_iota(jnp.int32, (TILE, wide), 1)
    row = lax.broadcasted_iota(jnp.int32, (TILE, wide), 0)
    near = (at <= row + WIN) & (at > row)
    good = jnp.concatenate([near & (at >= first - start) for _, _, _, first, start in tiles], 0)
    logits = jnp.where(good, logits * HEAD_DIM**-0.5, -1e30)
    top = jnp.max(logits, 1, keepdims=True)
    weight = jnp.where(good, jnp.exp(logits - top), 0.0)
    probs = (weight / jnp.sum(weight, 1, keepdims=True)).astype(BF16)
    return [
        jnp.dot(probs[n * TILE : (n + 1) * TILE], tile[2], preferred_element_type=F32)
        for n, tile in enumerate(tiles)
    ]


def mix_kernel(
    shifts, limits, values, features, window, bounds, pick, expand, rows, prefix, tail_docs, first_doc, *refs
):
    states, outs = refs[:shifts], refs[shifts:]
    count = values.shape[0]
    half = count // 2

    pair = jnp.dot(features[...], pick[0], preferred_element_type=F32).astype(BF16)
    phi_query = phi(features[...], expand[0], rows[...])
    chunks = count // CHUNK
    at = lax.broadcasted_iota(jnp.int32, (CHUNK, CHUNK), 1)
    row = lax.broadcasted_iota(jnp.int32, (CHUNK, CHUNK), 0)
    dots, good = [], []
    for n in range(chunks):
        here = slice(n * CHUNK, (n + 1) * CHUNK)
        dots.append(
            lax.dot_general(
                pair[here, :128], pair[here, 128:], (((1,), (1,)), ((), ())),
                preferred_element_type=F32,
            )
        )
        good.append((at <= row) & (at >= bounds[here] - n * CHUNK))
    dots, good = jnp.concatenate(dots, 0), jnp.concatenate(good, 0)
    score = dots * (dots * (0.5 / FEAT) + FEAT**-0.5) + 1.0
    score = jnp.where(good, score, 0.0).astype(BF16)

    same = jnp.where(tail_docs[...].astype(F32) == first_doc[0:1, 0:1] + 1.0, 1.0, 0.0)
    in_tail = jnp.sum(same, 0, keepdims=True)[:, 0:1].astype(jnp.int32)
    tiles = []
    for n in range(count // TILE):
        near = slice(n * TILE - WIN, (n + 1) * TILE)
        first = bounds[n * TILE : (n + 1) * TILE]
        if n:
            keys, vals = window[near, HEAD_DIM:], values[near]
        else:
            keys = jnp.concatenate([states[0][0, STATE + WIN :], window[:TILE, HEAD_DIM:]], 0)
            vals = jnp.concatenate([states[0][0, STATE : STATE + WIN], values[:TILE]], 0)
            first = jnp.where(first == 0, -in_tail, first)
        tiles.append(
            (window[n * TILE : (n + 1) * TILE, :HEAD_DIM], keys, vals, first, n * TILE - WIN)
        )
    windowed = jnp.concatenate(windows(tiles), 0)

    unmarked = lax.broadcasted_iota(jnp.int32, (STATE, HEAD_DIM), 0) < STATE - 1
    incoming = jnp.zeros((STATE, HEAD_DIM), F32)
    for k in range(shifts):
        sent = states[k][0, :STATE].astype(F32)
        wanted = (sent[STATE - 1 :] == first_doc[0:1, 0:1] + 1.0) & unmarked
        incoming += jnp.where(wanted, sent, 0.0)
    linear = []
    for n in range(chunks):
        here = slice(n * CHUNK, (n + 1) * CHUNK)
        state = incoming
        if n:
            state = jnp.where(limits[n - 1] <= 0, incoming, 0.0) + prefix[n, 0]
        state = jnp.concatenate([state, jnp.zeros((WIDE - STATE, HEAD_DIM), F32)], 0)
        carried = jnp.dot(phi_query[here], state.astype(BF16), preferred_element_type=F32)
        inner = jnp.dot(score[here], values[here], preferred_element_type=F32)
        linear.append(inner + jnp.where(bounds[here] <= n * CHUNK, carried, 0.0))
    linear = jnp.concatenate(linear, 0)
    mean = jnp.mean(linear * linear, 1, keepdims=True)
    mixed = (linear * lax.rsqrt(mean + 1e-5) + windowed).astype(BF16)
    outs[0][...] = mixed[:half]
    outs[1][...] = mixed[half:]


def mix(limits, both, window, bounds, pick, expand, rows, prefix, tail_docs, first_doc, states):
    count = both.shape[0]
    heads = states[0].shape[0]
    half = count // 2

    def full(a):
        return pl.BlockSpec(a.shape, lambda h, _: (0,) * a.ndim)

    def per_head(a):
        return pl.BlockSpec((1,) + a.shape[1:], lambda h, _: (h, 0, 0))

    return pl.pallas_call(
        functools.partial(mix_kernel, len(states)),
        grid_spec=pltpu.PrefetchScalarGridSpec(
            num_scalar_prefetch=1,
            grid=(heads,),
            in_specs=[
                pl.BlockSpec((count, HEAD_DIM), lambda h, _: (0, h)),
                pl.BlockSpec((count, LANES), lambda h, _: (0, heads)),
                pl.BlockSpec((count, 2 * HEAD_DIM), lambda h, _: (0, h)),
                full(bounds), per_head(pick), per_head(expand), full(rows),
                pl.BlockSpec((prefix.shape[0], 1, STATE, HEAD_DIM), lambda h, _: (0, h, 0, 0)),
                full(tail_docs), full(first_doc),
            ]
            + [per_head(a) for a in states],
            out_specs=[pl.BlockSpec((half, HEAD_DIM), lambda h, _: (0, h))] * 2,
        ),
        out_shape=[jax.ShapeDtypeStruct((half, heads * HEAD_DIM), BF16)] * 2,
        compiler_params=params(40 * 1024 * 1024),
    )(limits, both, both, window, bounds, pick, expand, rows, prefix, tail_docs, first_doc, *states)


def after(x, *others):
    return lax.optimization_barrier((x, *others))[0]


def shards(tokens, doc_ids, w_feat, w_value, w_window, w_out):
    rows = tokens.shape[0]
    chunks = rows // CHUNK
    value_columns = w_value.shape[1]
    heads = value_columns // HEAD_DIM
    count = lax.axis_size("head") // 2
    blocks = lax.axis_size("ctx")
    me = lax.axis_index("head")
    z, c = me // 2, me % 2
    place = jnp.stack([z, c]).astype(jnp.int32)

    pieces = {0: tokens, 1: ring(tokens, -1, count), count - 1: ring(tokens, 1, count)}
    tokens_there = swap(tokens, count)

    docs = doc_ids.astype(F32)
    ends = jnp.concatenate([docs[CHUNK::CHUNK], docs[rows - 1 :]])
    limits = jnp.sum((docs[None, :] < ends[:, None]).astype(F32), 1).astype(jnp.int32)
    limits = jnp.concatenate([limits, doc_ids[rows - 1 :]])
    first = jnp.sum((docs[None, :] < docs[:, None]).astype(F32), 1, keepdims=True)
    bounds = first.astype(jnp.int32)
    first_doc = docs.reshape(-1, LANES)
    tail_docs = jnp.broadcast_to((docs[rows - WIN :] + 1.0).astype(BF16)[:, None], (WIN, HEAD_DIM))
    onward = [(i, i + 1) for i in range(blocks - 1)]
    tail_docs = lax.ppermute(tail_docs, "ctx", onward)

    maps, scale_rows = expansions(heads)
    query_map, key_map = jnp.asarray(maps[0]), jnp.asarray(maps[1])
    scale_rows = jnp.asarray(scale_rows)
    pick = jnp.asarray(picks(heads))

    depth, columns = w_out.shape
    width = columns // (2 * count)

    rows_out = after(w_out, tokens_there)

    def cut(chip, core):
        return lax.dynamic_slice(rows_out, (0, (2 * chip + core) * width), (depth, width))

    other_rows = swap(jnp.stack([cut(chip, 1 - c) for chip in range(count)]), count)
    out_rows = []
    for n in range(count):
        chip = lax.rem(z + n, count)
        theirs = lax.dynamic_index_in_dim(other_rows, chip, 0, keepdims=False)
        out_rows += [cut(chip, c), theirs]

    used = value_columns + w_feat.shape[1]
    fv_columns = -(-used // 256) * 256
    weight = jnp.concatenate(
        [w_value, w_feat, jnp.zeros((w_value.shape[0], fv_columns - used), BF16), w_window], 1
    )
    all_columns = weight.shape[1]
    widths = (fv_columns, all_columns - fv_columns)
    part = project(place, (0,), [tokens], [tokens_there], weight, 0, widths)

    ready = lax.optimization_barrier(
        (pieces[1], pieces[count - 1], limits, bounds, first_doc, tail_docs, *part, *out_rows)
    )
    pieces[1], pieces[count - 1], limits, bounds, first_doc, tail_docs = ready[:6]
    part, out_rows = ready[6:8], ready[8:]

    for n in range(2, count // 2 + 1):
        pieces[n] = ring(pieces[n - 1], -1, count)
    for n in range(count - 2, count // 2, -1):
        pieces[n] = ring(pieces[n + 1], 1, count)
    near = (1, count - 1)
    mine = [pieces[n] for n in near]
    part = project(
        place, near, mine, [swap(p, count) for p in mine], weight, 0, widths, part
    )
    late = tuple(range(2, count - 1))
    *mine, fv_part, win_part = lax.optimization_barrier((*[pieces[n] for n in late], *part))
    theirs = [swap(p, count) for p in mine]
    both, prefix, state, state_and_tail = project_late(
        place, limits, late, mine, theirs, weight, heads, fv_part, win_part, key_map, scale_rows
    )
    states = [
        lax.ppermute(
            state_and_tail if k == 1 else state, "ctx", [(i, i + k) for i in range(blocks - k)]
        )
        for k in range(1, blocks)
    ]
    (window,) = project(
        place, late, [after(mine[0], state), *mine[1:]], theirs, weight, fv_columns, widths[1:],
        [win_part], BF16, 40 * 1024 * 1024,
    )
    low, high = mix(
        limits, both, window, bounds, pick, query_map, scale_rows, prefix, tail_docs, first_doc, states
    )

    def scattered(mixed, step):
        swapped = swap(mixed, count)
        sent = None
        for n in range(1, count + 1):
            at = 2 * (-step * n % count)
            total = jnp.dot(mixed, out_rows[at], preferred_element_type=F32)
            total += jnp.dot(swapped, out_rows[at + 1], preferred_element_type=F32)
            if sent is not None:
                total += ring(sent, step, count).astype(F32)
            sent = total.astype(BF16)
        return sent

    high_out = scattered(high, -1)
    low_out = scattered(low, 1)
    return jnp.concatenate([low_out, high_out], 0)


def solution(mesh):
    return jax.shard_map(
        shards,
        mesh=mesh,
        in_specs=(
            P("ctx", "head"),
            P("ctx"),
            P(None, "head"),
            P(None, "head"),
            P(None, "head"),
            P("head", None),
        ),
        out_specs=P("ctx", "head"),
        check_vma=False,
    )
```
